128 devices in a mesh: pipe: 2 (over core), tensor: 4 (over z), dp: 16 (over y, x).
Axes of the slice: x: 4, y: 4, z: 4, core: 2. Of those that a mesh axis runs over, the one named last changes fastest.
Arguments:
- tokens: bfloat16 [16384, 1024], P('dp'), may hold values from -6 to 6
- cotangent: bfloat16 [16384, 1024], P('dp'), may hold values from -6 to 6
- segment_ids: int32 [16, 1024], P('dp'), may hold values from 0 to 3, never falling along the last dimension, each value on 1 to 512 neighbouring positions
- mixer_gain: float32 [2, 1024], P('pipe', 'dp'), may hold values from 0.1 to 1.9
- ffn_gain: float32 [2, 1024], P('pipe', 'dp'), may hold values from 0.1 to 1.9
- gate_master: float32 [2, 1024, 4608], P('pipe', 'dp', 'tensor'), may hold values from -0.1875 to 0.1875
- up_master: float32 [2, 1024, 4608], P('pipe', 'dp', 'tensor'), may hold values from -0.1875 to 0.1875
- down_master: float32 [2, 4608, 1024], P('pipe', 'tensor', 'dp'), may hold values from -0.09375 to 0.09375
- conv_in: float32 [1024, 3, 1024], P(('pipe', 'dp'), None, 'tensor'), may hold values from -0.1875 to 0.1875
- conv_kernel: float32 [3, 1024], P(None, 'tensor'), may hold values from -3.5 to 3.5
- conv_out: float32 [1024, 1024], P('tensor', ('pipe', 'dp')), may hold values from -0.1875 to 0.1875
- query_master: float32 [1024, 1024], P(('pipe', 'dp'), 'tensor'), may hold values from -0.1875 to 0.1875
- key_master: float32 [1024, 512], P(('pipe', 'dp'), 'tensor'), may hold values from -0.1875 to 0.1875
- value_master: float32 [1024, 512], P(('pipe', 'dp'), 'tensor'), may hold values from -0.1875 to 0.1875
- query_gain: float32 [64], replicated, may hold values from 0.1 to 1.9
- key_gain: float32 [64], replicated, may hold values from 0.1 to 1.9
- output_master: float32 [1024, 1024], P('tensor', ('pipe', 'dp')), may hold values from -1.5 to 1.5
Outputs:
- section_outputs: bfloat16 [2, 16384, 1024], P('pipe', 'dp')
- input_grads: float32 [2, 16384, 1024], P('pipe', 'dp')
- grad_mixer_gain: float32 [2, 1024], P('pipe', 'dp')
- grad_ffn_gain: float32 [2, 1024], P('pipe', 'dp')
- grad_gate: float32 [2, 1024, 4608], P('pipe', 'dp', 'tensor')
- grad_up: float32 [2, 1024, 4608], P('pipe', 'dp', 'tensor')
- grad_down: float32 [2, 4608, 1024], P('pipe', 'tensor', 'dp')
- grad_conv_in: float32 [1024, 3, 1024], P(('pipe', 'dp'), None, 'tensor')
- grad_conv_kernel: float32 [3, 1024], replicated
- grad_conv_out: float32 [1024, 1024], P('tensor', ('pipe', 'dp'))
- grad_query: float32 [1024, 1024], P(('pipe', 'dp'), 'tensor')
- grad_key: float32 [1024, 512], P(('pipe', 'dp'), 'tensor')
- grad_value: float32 [1024, 512], P(('pipe', 'dp'), 'tensor')
- grad_query_gain: float32 [64], replicated
- grad_key_gain: float32 [64], replicated
- grad_output: float32 [1024, 1024], P('tensor', ('pipe', 'dp'))
The draws below stay inside these ranges and needn't reach their ends.
Inputs may be any that keep to these rules, and one draw needn't show every extreme that they name: `segment_ids`: along each sequence the document numbers never fall; equal numbers mark one document.
All inputs are finite; a program needn't handle non-finite values.
Results may differ from the reference program's by a relative error of at most 0.025.
The reference program's roundings to bfloat16 on the way count: a program that leaves them out, or rounds other values in their place, can miss the bound.
Values may be sent and summed in bfloat16 or wider, within the bound.
No kernel may reach another device: no remote copies, remote signals or barrier semaphores. Data moves between devices by JAX's collectives and lax.ppermute only.
A program may use at most 384 MiB of HBM per device.

```python
import math
import jax
import jax.numpy as jnp
import numpy as np
from jax import lax

D = 1024
FF = 4608
H = 16
KVH = 8
HD = 64
KSIZE = 3
SEQ = 1024
QBLK = 512
DOCS = 4
SEQS = 16
TOKENS = 16384
QW = 1024
KW = 512


def block_levels(own_key, extent, split, low, top_value):
    level = 1.0
    for axis_at, parts in split:
        heights = jax.random.uniform(jax.random.fold_in(jax.random.fold_in(own_key, 6), axis_at), (parts,), jnp.float32, low / len(split), top_value / len(split))
        level = level * jnp.repeat(jnp.exp(heights), extent[axis_at] // parts).reshape((-1,) + (1,) * (len(extent) - 1 - axis_at))
    return level


def split_up(number_of, total, bound, lean):
    portions = [(1 << 20) // math.isqrt(grade ** lean) + 1 for grade in range(2, number_of + 1)]
    rest, holding = total - bound - (number_of - 1), [1] * (number_of - 1)
    while rest > 0:
        candidates = [i for i in range(number_of - 1) if holding[i] < bound]
        whole, budget = sum([portions[i] for i in candidates]), rest
        for i in candidates:
            addition = min(bound - holding[i], max(1, budget * portions[i] // whole), rest)
            holding[i] = holding[i] + addition
            rest = rest - addition
    return np.array([bound] + holding)


def uneven(own_key, number_of, total, reach, slope):
    if number_of == 2:
        one = jax.random.randint(own_key, (), max(1, total - reach), min(reach, total - 1) + 1)
        return jnp.stack([one, total - one])
    lengths = jnp.asarray(split_up(number_of, total, reach, slope), jnp.int32)
    couples = (number_of - 1) // 2
    giver, taker = lengths[1:1 + 2 * couples:2], lengths[2:2 + 2 * couples:2]
    slack = jnp.minimum(giver - 1, reach - taker)
    moved = jax.random.randint(jax.random.fold_in(own_key, 1), (couples,), 0, 1 << 20) % (slack + 1)
    lengths = lengths.at[1:1 + 2 * couples:2].set(giver - moved).at[2:2 + 2 * couples:2].set(taker + moved)
    return lengths[jax.random.permutation(jax.random.fold_in(own_key, 2), number_of)]


def noise(own_key, extent, width, limit, split=(), held_as=jnp.bfloat16):
    result = width * jax.random.normal(own_key, extent, jnp.float32)
    if split:
        result = result * block_levels(own_key, extent, split, -0.22, 0.18)
    return jnp.clip(result, -limit, limit).astype(held_as)


def setup_inputs(seed: int = 0) -> dict:
    key_of = jax.random.split(jax.random.key(seed), 18)
    tokens = noise(key_of[0], (TOKENS, D), 1.0, 6.0, ((0, 16),))
    cotangent = noise(key_of[1], (TOKENS, D), 1.0, 6.0, ((0, 16),))
    segment_ids = jax.vmap(lambda own: jnp.searchsorted(jnp.cumsum(uneven(own, DOCS, SEQ, SEQ // 2, 2)), jnp.arange(SEQ), side="right"))(jax.random.split(key_of[2], SEQS)).reshape((SEQS, SEQ)).astype(jnp.int32)
    mixer_gain = jnp.clip(1.0 + 0.18 * jax.random.normal(key_of[3], (2, D), jnp.float32), 0.1, 1.9)
    ffn_gain = jnp.clip(1.0 + 0.18 * jax.random.normal(key_of[4], (2, D), jnp.float32), 0.1, 1.9)
    gate_master = noise(key_of[5], (2, D, FF), D ** -0.5, 0.1875, ((0, 2), (1, 16), (2, 4)), jnp.float32)
    up_master = noise(key_of[6], (2, D, FF), D ** -0.5, 0.1875, ((0, 2), (1, 16), (2, 4)), jnp.float32)
    down_master = noise(key_of[7], (2, FF, D), FF ** -0.5, 0.09375, ((0, 2), (1, 4), (2, 16)), jnp.float32)
    conv_in = noise(key_of[8], (D, 3, D), D ** -0.5, 0.1875, ((0, 32), (2, 4)), jnp.float32)
    conv_kernel = noise(key_of[9], (KSIZE, D), KSIZE ** -0.5, 3.5, ((1, 4),), jnp.float32)
    conv_out = noise(key_of[10], (D, D), D ** -0.5, 0.1875, ((0, 4), (1, 32)), jnp.float32)
    query_master = noise(key_of[11], (D, QW), D ** -0.5, 0.1875, ((0, 32), (1, 4)), jnp.float32)
    key_master = noise(key_of[12], (D, KW), D ** -0.5, 0.1875, ((0, 32), (1, 4)), jnp.float32)
    value_master = noise(key_of[13], (D, KW), D ** -0.5, 0.1875, ((0, 32), (1, 4)), jnp.float32)
    query_gain = jnp.clip(1.0 + 0.18 * jax.random.normal(key_of[14], (HD,), jnp.float32), 0.1, 1.9)
    key_gain = jnp.clip(1.0 + 0.18 * jax.random.normal(key_of[15], (HD,), jnp.float32), 0.1, 1.9)
    output_master = noise(key_of[16], (QW, D), (max(QW // 64, 1)) ** -0.5, 1.5, ((0, 4), (1, 32)), jnp.float32)
    return dict(tokens=tokens, cotangent=cotangent, segment_ids=segment_ids, mixer_gain=mixer_gain, ffn_gain=ffn_gain, gate_master=gate_master, up_master=up_master, down_master=down_master, conv_in=conv_in, conv_kernel=conv_kernel, conv_out=conv_out, query_master=query_master, key_master=key_master, value_master=value_master, query_gain=query_gain, key_gain=key_gain, output_master=output_master)


@jax.custom_vjp
def low(v):
    return lax.optimization_barrier(v.astype(jnp.bfloat16)).astype(jnp.float32)

@jax.custom_vjp
def low_back(v):
    return v

def low_keep(v):
    return (low(v), None)

def low_pass(kept, grad):
    return (grad,)

def back_keep(v):
    return (v, None)

def back_low(kept, grad):
    return (low(grad),)
low.defvjp(low_keep, low_pass)
low_back.defvjp(back_keep, back_low)
EPS = 1e-05
THETA = 1000000.0
NEGATIVE = -1e+30
HIGH = lax.Precision.HIGHEST

def matmul(left, right):
    return jnp.dot(left, right, precision=HIGH, preferred_element_type=jnp.float32)

def rms_scale(value, gain):
    return value * lax.rsqrt(lax.optimization_barrier(jnp.mean(value * value, axis=-1, keepdims=True)) + EPS) * gain

def positions_of(segments):
    count = segments.shape[0]
    index = jnp.arange(count, dtype=jnp.int32)
    change = jnp.concatenate([jnp.ones((1,), jnp.bool_), segments[1:] != segments[:-1]])
    return index - lax.cummax(jnp.where(change, index, 0), axis=0)

def rotation(positions, half):
    frequency = THETA ** (-2.0 * jnp.arange(half, dtype=jnp.float32) / (2.0 * half))
    angle = positions.astype(jnp.float32)[:, None] * frequency[None, :]
    return (jnp.cos(angle), jnp.sin(angle))

def rotate(value, cosine, sine):
    half = value.shape[-1] // 2
    first = value[..., :half]
    second = value[..., half:]
    cosine = cosine[:, None, :]
    sine = sine[:, None, :]
    return jnp.concatenate([first * cosine - second * sine, second * cosine + first * sine], axis=-1)

def conv_mixer(normed, segments, conv_in, conv_kernel, conv_out):
    count = normed.shape[0]
    projected = low_back(matmul(normed, low(conv_in).reshape(D, 3 * D)))
    input_gate = projected[:, :D]
    output_gate = projected[:, D:2 * D]
    signal = projected[:, 2 * D:]
    product = input_gate * signal
    lag = KSIZE - 1
    total = jnp.zeros((count, D), jnp.float32)
    for back in range(lag + 1):
        moved = jnp.concatenate([jnp.zeros((back, D), jnp.float32), product[:count - back]], axis=0)
        same = jnp.concatenate([jnp.zeros((back,), jnp.bool_), segments[back:] == segments[:count - back]])
        total = total + conv_kernel[lag - back] * jnp.where(same[:, None], moved, 0.0)
    convolved = low(output_gate * total)
    return low_back(matmul(convolved, low(conv_out)))

def attention_mixer(normed, segments, w_query, w_key, w_value, query_gain, key_gain, w_output):
    count = normed.shape[0]
    group = H // KVH
    queries = low_back(matmul(normed, low(w_query))).reshape(count, H, HD)
    keys = low_back(matmul(normed, low(w_key))).reshape(count, KVH, HD)
    values = low(low_back(matmul(normed, low(w_value)))).reshape(count, KVH, HD)
    cosine, sine = rotation(positions_of(segments), HD // 2)
    queries = low(rotate(rms_scale(queries, query_gain), cosine, sine))
    keys = low(rotate(rms_scale(keys, key_gain), cosine, sine))
    keys = jnp.repeat(keys, group, axis=1)
    values = jnp.repeat(values, group, axis=1)
    index = jnp.arange(count, dtype=jnp.int32)

    def block(start):
        own_rows = start + jnp.arange(QBLK, dtype=jnp.int32)
        piece = lax.dynamic_slice_in_dim(queries, start, QBLK, 0)
        own = lax.dynamic_slice_in_dim(segments, start, QBLK, 0)
        allowed = (index[None, :] <= own_rows[:, None]) & (segments[None, :] == own[:, None])
        scores = low_back(jnp.einsum('qhd,khd->hqk', piece, keys, precision=HIGH) * HD ** (-0.5))
        scores = jnp.where(allowed[None], scores, NEGATIVE)
        weights = jnp.exp(scores - lax.optimization_barrier(jnp.max(scores, axis=-1, keepdims=True)))
        probs = low(weights / lax.optimization_barrier(jnp.sum(weights, axis=-1, keepdims=True)))
        return jnp.einsum('hqk,khd->qhd', probs, values, precision=HIGH)
    starts = jnp.arange(count // QBLK, dtype=jnp.int32) * QBLK
    attended = lax.map(jax.checkpoint(block), starts).reshape(count, H * HD)
    attended = low(low_back(attended))
    return low_back(matmul(attended, low(w_output)))

def dense_block(hidden, gain, w_gate, w_up, w_down):
    normed = low(rms_scale(hidden, low(gain)))
    gate = low_back(matmul(normed, low(w_gate)))
    up = low_back(matmul(normed, low(w_up)))
    inner = low(jax.nn.silu(gate) * up)
    return hidden + low_back(matmul(inner, low(w_down)))

def forward(params, tokens, delta, segments):
    mixer_gain, ffn_gain, w_gate, w_up, w_down, conv_in, conv_kernel, conv_out, w_query, w_key, w_value, query_gain, key_gain, w_output = params
    normed = low(rms_scale(tokens, low(mixer_gain[0])))
    hidden = tokens + conv_mixer(normed, segments, conv_in, conv_kernel, conv_out)
    first = dense_block(hidden, ffn_gain[0], w_gate[0], w_up[0], w_down[0])
    passed = low_back(low(first)) + delta
    normed = low(rms_scale(passed, low(mixer_gain[1])))
    hidden = passed + attention_mixer(normed, segments, w_query, w_key, w_value, query_gain, key_gain, w_output)
    second = dense_block(hidden, ffn_gain[1], w_gate[1], w_up[1], w_down[1])
    return (second, low(first))

def reference(tokens, cotangent, segment_ids, mixer_gain, ffn_gain, gate_master, up_master, down_master, conv_in, conv_kernel, conv_out, query_master, key_master, value_master, query_gain, key_gain, output_master):
    params = (mixer_gain, ffn_gain, gate_master, up_master, down_master, conv_in, conv_kernel, conv_out, query_master, key_master, value_master, query_gain, key_gain, output_master)
    params = tuple((item.astype(jnp.float32) for item in params))
    inputs = tokens.astype(jnp.float32).reshape(SEQS, SEQ, D)
    incoming = cotangent.astype(jnp.float32).reshape(SEQS, SEQ, D)

    def sequence_step(carry, item):
        source, gradient, segments = item
        delta = jnp.zeros((SEQ, D), jnp.float32)

        def sectioned(weights, values, shift):
            return forward(weights, values, shift, segments)
        second, pullback, first = jax.vjp(sectioned, params, source, delta, has_aux=True)
        weight_grads, source_grad, delta_grad = pullback(gradient)
        carry = jax.tree.map(lambda left, right: left + right, carry, weight_grads)
        return (carry, (first, second, source_grad, delta_grad))
    zeros = jax.tree.map(jnp.zeros_like, params)
    sums, (firsts, seconds, source_grads, delta_grads) = lax.scan(sequence_step, zeros, (inputs, incoming, segment_ids))
    section_outputs = jnp.stack([firsts.reshape(TOKENS, D), seconds.reshape(TOKENS, D)]).astype(jnp.bfloat16)
    input_grads = jnp.stack([source_grads.reshape(TOKENS, D), delta_grads.reshape(TOKENS, D)])
    return (section_outputs, input_grads, sums[0], sums[1], sums[2], sums[3], sums[4], sums[5], sums[6], sums[7], sums[8], sums[9], sums[10], sums[11], sums[12], sums[13])
```

```python
import functools

import jax
import jax.numpy as jnp
from jax import lax
from jax.experimental import pallas as pl
from jax.experimental.pallas import tpu as pltpu
from jax.sharding import Mesh
from jax.sharding import PartitionSpec as P

DP = ("dp_0", "dp_1")
PIPE_DP = ("pipe", "dp_0", "dp_1")
EPS = 1e-05
THETA = 1000000.0
NEGATIVE = -1e30
HALO = 16
BF = jnp.bfloat16
F32 = jnp.float32


def dot(left, right, dims=((1,), (0,))):
    return lax.dot_general(left, right, (dims, ((), ())), preferred_element_type=F32)


def dot_cols(left, right):
    return dot(left, right, ((1,), (1,)))


def dot_rows(left, right):
    return dot(left, right, ((0,), (0,)))


def exchange(parts, axis):
    return lax.all_to_all(parts, axis, 0, 0)


def scatter_sum(value, axis):
    size = lax.axis_size(axis)
    parts = value.reshape(size, value.shape[0] // size, *value.shape[1:])
    return jnp.sum(exchange(parts, axis).astype(F32), axis=0)


def gather(value, axis):
    size = lax.axis_size(axis)
    parts = exchange(jnp.broadcast_to(value[None], (size, *value.shape)), axis)
    return parts.reshape(size * value.shape[0], *value.shape[1:])


def turned(value, axis, by):
    size = lax.axis_size(axis)
    return lax.ppermute(value, axis, [(i, (i + by) % size) for i in range(size)])


def direct_scatter_sum(value, axis):
    me = lax.axis_index(axis)
    rows = value.shape[0] // 4

    def block(by):
        return lax.dynamic_slice_in_dim(value, lax.rem(me + by, 4) * rows, rows, 0)

    total = block(0).astype(F32)
    for by in (1, 3, 2):
        total = total + turned(block(by), axis, by).astype(F32)
    return total


def direct_gather(value, axis):
    me = lax.axis_index(axis)
    whole = jnp.zeros((4, *value.shape), value.dtype)
    for by in (0, 1, 3, 2):
        part = turned(value, axis, by) if by else value
        whole = lax.dynamic_update_slice_in_dim(whole, part[None], lax.rem(me + 4 - by, 4), 0)
    return whole.reshape(4 * value.shape[0], *value.shape[1:])


def after(value, *others):
    return lax.optimization_barrier((value, *others))[0]


def other_core(value):
    return lax.ppermute(value, "pipe", [(0, 1), (1, 0)])


def in_core_order(core, own, other):
    return jnp.where(
        core == 0, jnp.concatenate([own, other], 0), jnp.concatenate([other, own], 0)
    )


def half_of(value, core):
    rows = value.shape[0] // 2
    return lax.dynamic_slice_in_dim(value, core * rows, rows, 0)


def rms_forward(value, gain):
    scale = lax.rsqrt(jnp.mean(value * value, axis=-1, keepdims=True) + EPS)
    return value * scale * gain, scale


def rms_backward(value, scale, gain, grad):
    weighted = grad * gain
    inner = jnp.mean(weighted * value, axis=-1, keepdims=True)
    return scale * weighted - value * (scale * scale * scale) * inner


def positions_of(segments):
    first = jnp.sum((segments[None, :] < segments[:, None]).astype(jnp.int32), axis=1)
    return jnp.arange(segments.shape[0], dtype=jnp.int32) - first


def rotation(positions, head_dim):
    half = head_dim // 2
    frequency = THETA ** (-2.0 * jnp.arange(half, dtype=F32) / head_dim)
    angle = positions.astype(F32)[:, None] * frequency[None, :]
    cosine, sine = jnp.cos(angle), jnp.sin(angle)
    return jnp.tile(cosine, (1, 4)), jnp.tile(jnp.concatenate([-sine, sine], 1), (1, 2))


def whole(kernel, out_shapes, *operands, scratch=(), flops=0, vmem=40):
    spec = pl.BlockSpec(memory_space=pltpu.VMEM)
    moved = sum(x.size * x.dtype.itemsize for x in (*operands, *out_shapes))
    return pl.pallas_call(
        kernel,
        out_shape=tuple(out_shapes),
        in_specs=[spec] * len(operands),
        out_specs=tuple(spec for _ in out_shapes),
        scratch_shapes=scratch,
        compiler_params=pltpu.CompilerParams(vmem_limit_bytes=vmem * 2**20),
        cost_estimate=pl.CostEstimate(flops=flops, bytes_accessed=moved, transcendentals=0),
    )(*operands)


def head_mean(value, low):
    first = jnp.sum(jnp.where(low, value, 0.0), axis=1, keepdims=True)
    second = jnp.sum(jnp.where(low, 0.0, value), axis=1, keepdims=True)
    return jnp.where(low, first, second) * (1.0 / 64.0)


def partner(value, first_half):
    return jnp.where(first_half, pltpu.roll(value, 96, 1), pltpu.roll(value, 32, 1))


def lanes_of(rows):
    lane = lax.broadcasted_iota(jnp.int32, (rows, 128), 1)
    return lane < 64, (lane & 63) < 32


CHUNK = 128


def rope_forward_kernel(raw_ref, cosine_ref, sine_ref, gain_ref, out_ref):
    rows = raw_ref.shape[0]
    low, first_half = lanes_of(CHUNK)

    @pl.loop(0, rows // CHUNK)
    def _(step):
        at = pl.ds(pl.multiple_of(step * CHUNK, CHUNK), CHUNK)
        cosine, sine = cosine_ref[at, :], sine_ref[at, :]
        for tile in range(3):
            cols = pl.ds(tile * 128, 128)
            value = raw_ref[at, cols]
            gain = gain_ref[pl.ds(tile // 2, 1), :]
            normed = value * lax.rsqrt(head_mean(value * value, low) + EPS) * gain
            turned = normed * cosine + partner(normed, first_half) * sine
            out_ref[at, cols] = turned.astype(BF)
        out_ref[at, pl.ds(384, 128)] = raw_ref[at, pl.ds(384, 128)].astype(BF)


def rope_backward_kernel(
    raw_ref, grad_query_ref, grad_kv_ref, more_kv_ref, cosine_ref, sine_ref, gain_ref, out_ref, sums_ref
):
    rows = raw_ref.shape[0]
    low, first_half = lanes_of(CHUNK)
    sums_ref[...] = jnp.zeros_like(sums_ref)

    @pl.loop(0, rows // CHUNK)
    def _(step):
        at = pl.ds(pl.multiple_of(step * CHUNK, CHUNK), CHUNK)
        cosine, sine = cosine_ref[at, :], sine_ref[at, :]
        for tile in range(3):
            cols = pl.ds(tile * 128, 128)
            if tile < 2:
                grad = grad_query_ref[at, cols]
            else:
                grad = grad_kv_ref[at, pl.ds(0, 128)] + more_kv_ref[at, pl.ds(0, 128)]
            grad = grad * cosine - partner(grad, first_half) * sine
            value = raw_ref[at, cols]
            gain = gain_ref[pl.ds(tile // 2, 1), :]
            scale = lax.rsqrt(head_mean(value * value, low) + EPS)
            weighted = grad * gain
            inner = head_mean(weighted * value, low)
            back = scale * weighted - value * (scale * scale * scale) * inner
            out_ref[at, cols] = back.astype(BF)
            sums_ref[pl.ds(tile // 2, 1), :] += jnp.sum(grad * value * scale, axis=0, keepdims=True)
        out_ref[at, pl.ds(384, 128)] = (
            grad_kv_ref[at, pl.ds(128, 128)] + more_kv_ref[at, pl.ds(128, 128)]
        ).astype(BF)


def fill_window(own_ref, before_ref, keys_ref):
    rows = own_ref.shape[0]
    keys_ref[pl.ds(0, rows), :] = before_ref[...]
    keys_ref[pl.ds(rows, rows), :] = own_ref[:, pl.ds(256, 256)]


def bias_of(column_ref, row_ref, start, block, span):
    keys = column_ref[pl.ds(start, span), pl.ds(0, 1)]
    queries = row_ref[pl.ds(0, 1), pl.ds(start, block)]
    key_at = lax.broadcasted_iota(jnp.int32, (span, block), 0)
    query_at = lax.broadcasted_iota(jnp.int32, (span, block), 1) + (span - block)
    return jnp.where((key_at <= query_at) & (keys == queries), 0.0, NEGATIVE)


BLOCK = 256
SPAN = 768


def attend_forward_kernel(own_ref, before_ref, column_ref, row_ref, out_ref, log_ref, keys_ref):
    rows = own_ref.shape[0]
    fill_window(own_ref, before_ref, keys_ref)
    log_ref[...] = jnp.zeros_like(log_ref)
    for sub in range(rows // BLOCK):
        start = sub * BLOCK
        bias = bias_of(column_ref, row_ref, start, BLOCK, SPAN)
        values = keys_ref[pl.ds(start, SPAN), pl.ds(128, 128)].astype(F32).T.astype(BF)
        parts = []
        for head in range(4):
            kv = head // 2
            key = keys_ref[pl.ds(start, SPAN), pl.ds(kv * 64, 64)]
            query = own_ref[pl.ds(start, BLOCK), pl.ds(head * 64, 64)] * jnp.asarray(0.125, BF)
            scores = dot_cols(key, query) + bias
            top = jnp.max(scores, axis=0, keepdims=True)
            weights = jnp.exp(scores - top)
            total = jnp.sum(weights, axis=0, keepdims=True)
            probs = (weights * (1.0 / total)).astype(BF)
            parts.append(dot(values[kv * 64 : kv * 64 + 64], probs))
            log_ref[pl.ds(head, 1), pl.ds(start, BLOCK)] = top + jnp.log(total)
        out_ref[pl.ds(start, BLOCK), :] = jnp.concatenate(parts, 0).T.astype(BF)


def attend_backward_kernel(
    own_ref, before_ref, column_ref, row_ref, log_ref, grad_ref, query_ref, kv_ref, keys_ref
):
    rows = own_ref.shape[0]
    fill_window(own_ref, before_ref, keys_ref)
    kv_ref[...] = jnp.zeros_like(kv_ref)
    for sub in range(rows // BLOCK):
        start = sub * BLOCK
        window = pl.ds(start, SPAN)
        bias = bias_of(column_ref, row_ref, start, BLOCK, SPAN)
        keys = keys_ref[window, pl.ds(0, 128)].astype(F32).T.astype(BF)
        parts = []
        for kv in range(2):
            key = keys_ref[window, pl.ds(kv * 64, 64)]
            value = keys_ref[window, pl.ds(128 + kv * 64, 64)]
            grad_key = jnp.zeros((SPAN, 64), F32)
            grad_value = jnp.zeros((SPAN, 64), F32)
            for head in (2 * kv, 2 * kv + 1):
                query = own_ref[pl.ds(start, BLOCK), pl.ds(head * 64, 64)] * jnp.asarray(0.125, BF)
                grad = grad_ref[pl.ds(start, BLOCK), pl.ds(head * 64, 64)]
                log = log_ref[pl.ds(head, 1), pl.ds(start, BLOCK)]
                probs = jnp.exp(dot_cols(key, query) + bias - log)
                grad_probs = dot_cols(value, grad)
                shared = jnp.sum(probs * grad_probs, axis=0, keepdims=True)
                grad_scores = (probs * (grad_probs - shared)).astype(BF)
                grad_key += dot(grad_scores, query)
                grad_value += dot(probs.astype(BF), grad)
                parts.append(dot(keys[kv * 64 : kv * 64 + 64], grad_scores) * 0.125)
            kv_ref[window, pl.ds(kv * 64, 64)] += grad_key
            kv_ref[window, pl.ds(128 + kv * 64, 64)] += grad_value
        query_ref[pl.ds(start, BLOCK), :] = jnp.concatenate(parts, 0).T


HALF = 32
GATE, UP, DOWN = range(3)


def fetch_weights(core_ref, own_ref, other_ref, weights_ref, sems, order):
    core = core_ref[0]

    def copies(k):
        return [
            pltpu.make_async_copy(
                ref.at[:, pl.ds(HALF * k, HALF), :], weights_ref.at[k, :, part], sems.at[k, side]
            )
            for side, (ref, part) in enumerate(((own_ref, core), (other_ref, 1 - core)))
        ]

    for k in order:
        for copy in copies(k):
            copy.start()

    def matrix(k):
        for copy in copies(k):
            copy.wait()
        return lambda: weights_ref[k].reshape(-1, weights_ref.shape[-1])

    return matrix


def gates_back(grad_inner, gate, up):
    sigma = 1.0 / (1.0 + jnp.exp(-gate))
    silu = gate * sigma
    grad_gate = grad_inner * up * (sigma * (1.0 + gate * (1.0 - sigma)))
    return grad_gate.astype(BF), (grad_inner * silu).astype(BF), (silu * up).astype(BF)


def silu(gate):
    return gate * (1.0 / (1.0 + jnp.exp(-gate)))


class Moved:
    def __init__(self, source, target, sem):
        self.copy = pltpu.make_async_copy(source, target, sem)

    def start(self):
        self.copy.start()
        return self

    def wait(self):
        self.copy.wait()


def feed_forward_kernel(
    core_ref, in_ref, own_ref, other_ref, acts_ref, out_ref, held_ref, weights_ref, sems, out_sems
):
    matrix = fetch_weights(core_ref, own_ref, other_ref, weights_ref, sems, (GATE, UP, DOWN))
    held_ref[0] = dot(in_ref[...], matrix(GATE)())
    first = Moved(held_ref.at[0], acts_ref.at[0], out_sems.at[0]).start()
    held_ref[1] = dot(in_ref[...], matrix(UP)())
    second = Moved(held_ref.at[1], acts_ref.at[1], out_sems.at[1]).start()
    inner = (silu(held_ref[0]) * held_ref[1]).astype(BF)
    out_ref[...] = dot_cols(inner, matrix(DOWN)()).astype(BF)
    first.wait()
    second.wait()


def send_parts(parts_ref, held_ref, sems):
    return [Moved(held_ref.at[k], parts_ref.at[k], sems.at[k]).start() for k in range(3)]


def feed_backward_kernel(
    core_ref, grad_ref, own_ref, other_ref, acts_ref, parts_ref, out_ref,
    acts_held_ref, held_ref, weights_ref, sems, in_sems, out_sems,
):
    matrix = fetch_weights(core_ref, own_ref, other_ref, weights_ref, sems, (DOWN,))
    acts = [Moved(acts_ref.at[k], acts_held_ref.at[k], in_sems.at[k]).start() for k in range(2)]
    more = fetch_weights(core_ref, own_ref, other_ref, weights_ref, sems, (GATE, UP))
    grad_inner = dot(grad_ref[...], matrix(DOWN)())
    acts[0].wait()
    acts[1].wait()
    grad_gate, grad_up, inner = gates_back(grad_inner, acts_held_ref[0], acts_held_ref[1])
    held_ref[0] = grad_gate
    held_ref[1] = grad_up
    held_ref[2] = inner
    sent = send_parts(parts_ref, held_ref, out_sems)
    out = dot_cols(held_ref[0], more(GATE)())
    out_ref[...] = (out + dot_cols(held_ref[1], more(UP)())).astype(BF)
    for copy in sent:
        copy.wait()


def feed_both_kernel(
    core_ref, in_ref, grad_ref, own_ref, other_ref, parts_ref, second_ref, out_ref,
    held_ref, weights_ref, sems, out_sems,
):
    matrix = fetch_weights(core_ref, own_ref, other_ref, weights_ref, sems, (DOWN, GATE, UP))
    down = matrix(DOWN)
    grad_inner = dot(grad_ref[...], down())
    gate_w = matrix(GATE)
    gate = dot(in_ref[...], gate_w())
    up_w = matrix(UP)
    up = dot(in_ref[...], up_w())
    grad_gate, grad_up, inner = gates_back(grad_inner, gate, up)
    held_ref[0] = grad_gate
    held_ref[1] = grad_up
    held_ref[2] = inner
    sent = send_parts(parts_ref, held_ref, out_sems)
    out = dot_cols(held_ref[0], gate_w())
    out_ref[...] = (out + dot_cols(held_ref[1], up_w())).astype(BF)
    second_ref[...] = dot_cols(held_ref[2], down()).astype(BF)
    for copy in sent:
        copy.wait()


def feed_weights_kernel(
    core_ref, in_ref, grad_ref, part_ref, keep_ref, send_ref, in_t_ref, grad_t_ref, both_ref
):
    core = core_ref[0]
    step = pl.program_id(0)

    @pl.when(step == 0)
    def _():
        in_t_ref[...] = in_ref[...].astype(F32).T.astype(BF)
        grad_t_ref[...] = grad_ref[...].astype(F32).T.astype(BF)

    @pl.when(step < 2)
    def _():
        both_ref[...] = dot(in_t_ref[...], part_ref[0]).astype(BF).reshape(both_ref.shape)

    @pl.when(step == 2)
    def _():
        both_ref[...] = dot(grad_t_ref[...], part_ref[0]).astype(BF).reshape(both_ref.shape)

    keep_ref[...] = both_ref[:, core]
    send_ref[...] = both_ref[:, 1 - core]


SMEM_SPEC = pl.BlockSpec(memory_space=pltpu.SMEM)
HBM_SPEC = pl.BlockSpec(memory_space=pltpu.HBM)
VMEM_SPEC = pl.BlockSpec(memory_space=pltpu.VMEM)


def feed(kernel, in_specs, outs, scratch, hidden, width, flops, vmem, *operands):
    moved = sum(x.size * x.dtype.itemsize for x in (*operands, *outs))
    return pl.pallas_call(
        kernel,
        in_specs=in_specs,
        out_specs=(HBM_SPEC, *[VMEM_SPEC] * (len(outs) - 1)),
        out_shape=tuple(outs),
        scratch_shapes=[
            *scratch,
            pltpu.VMEM((3, width // (2 * HALF), 2, HALF, hidden), BF),
            pltpu.SemaphoreType.DMA((3, 2)),
            *[pltpu.SemaphoreType.DMA((3,))] * len(scratch),
        ],
        compiler_params=pltpu.CompilerParams(vmem_limit_bytes=vmem * 2**20),
        cost_estimate=pl.CostEstimate(flops=flops, bytes_accessed=moved, transcendentals=0),
    )(*operands)


def feed_forward(core, ffn_in, own, other):
    rows, width = ffn_in.shape
    hidden = own.shape[-1]
    return feed(
        feed_forward_kernel,
        [SMEM_SPEC, VMEM_SPEC, HBM_SPEC, HBM_SPEC],
        [jax.ShapeDtypeStruct((2, rows, hidden), F32), jax.ShapeDtypeStruct(ffn_in.shape, BF)],
        [pltpu.VMEM((2, rows, hidden), F32)],
        hidden, width, 6 * rows * width * hidden, FEED_VMEM,
        core, ffn_in, own, other,
    )


def feed_backward(core, grad_low, own, other, acts):
    rows, width = grad_low.shape
    hidden = own.shape[-1]
    return feed(
        feed_backward_kernel,
        [SMEM_SPEC, VMEM_SPEC, HBM_SPEC, HBM_SPEC, HBM_SPEC],
        [jax.ShapeDtypeStruct((3, rows, hidden), BF), jax.ShapeDtypeStruct(grad_low.shape, BF)],
        [pltpu.VMEM((2, rows, hidden), F32), pltpu.VMEM((3, rows, hidden), BF)],
        hidden, width, 6 * rows * width * hidden, FEED_VMEM,
        core, grad_low, own, other, acts,
    )


def feed_both(core, ffn_in, grad_low, own, other):
    rows, width = grad_low.shape
    hidden = own.shape[-1]
    out = jax.ShapeDtypeStruct(grad_low.shape, BF)
    return feed(
        feed_both_kernel,
        [SMEM_SPEC, VMEM_SPEC, VMEM_SPEC, HBM_SPEC, HBM_SPEC],
        [jax.ShapeDtypeStruct((3, rows, hidden), BF), out, out],
        [pltpu.VMEM((3, rows, hidden), BF)],
        hidden, width, 12 * rows * width * hidden, FEED_VMEM,
        core, ffn_in, grad_low, own, other,
    )


FEED_VMEM = 58


def feed_weights(core, ffn_in, grad_low, parts):
    rows, width = ffn_in.shape
    hidden = parts.shape[-1]
    blocks = width // (2 * HALF)
    out = jax.ShapeDtypeStruct((blocks, 3 * HALF, hidden), BF)
    out_spec = pl.BlockSpec((blocks, HALF, hidden), lambda k: (0, k, 0))
    return pl.pallas_call(
        feed_weights_kernel,
        grid=(3,),
        in_specs=[
            SMEM_SPEC,
            VMEM_SPEC,
            VMEM_SPEC,
            pl.BlockSpec((1, rows, hidden), lambda k: (k, 0, 0)),
        ],
        out_specs=(out_spec, out_spec),
        out_shape=(out, out),
        scratch_shapes=[
            pltpu.VMEM((width, rows), BF),
            pltpu.VMEM((width, rows), BF),
            pltpu.VMEM((blocks, 2, HALF, hidden), BF),
        ],
        compiler_params=pltpu.CompilerParams(
            dimension_semantics=("arbitrary",), vmem_limit_bytes=FEED_VMEM * 2**20
        ),
        cost_estimate=pl.CostEstimate(flops=2**20, bytes_accessed=2**20, transcendentals=0),
    )(core, ffn_in, grad_low, parts)


def per_device(
    tokens,
    cotangent,
    segment_ids,
    mixer_gain,
    ffn_gain,
    gate_master,
    up_master,
    down_master,
    conv_in,
    conv_kernel,
    conv_out,
    query_master,
    key_master,
    value_master,
    query_gain,
    key_gain,
    output_master,
):
    core = lax.axis_index("pipe")
    lane = lax.axis_index("tensor")
    at_dp = lax.axis_index("dp_0") * 4 + lax.axis_index("dp_1")
    seq_len, width = tokens.shape
    rows = seq_len // 2
    shard = rows // 4
    channels = conv_kernel.shape[1]
    head_dim = query_gain.shape[0]
    hidden_width = gate_master.shape[2]
    dp_rows = gate_master.shape[1]
    mix_rows = conv_in.shape[0]
    attn_cols = 3 * channels
    segments = segment_ids[0]

    core_at = core.astype(jnp.int32).reshape(1)
    dense_shard = jnp.stack([gate_master[0], up_master[0], down_master[0].T]).astype(BF)
    dense_shard = dense_shard.reshape(3, 2, HALF, hidden_width)
    keep = lax.dynamic_index_in_dim(dense_shard, core, 1, False).reshape(3 * HALF, hidden_width)
    send = lax.dynamic_index_in_dim(dense_shard, 1 - core, 1, False).reshape(3 * HALF, hidden_width)
    got = other_core(send)
    attn_shard = jnp.concatenate([query_master, key_master, value_master, output_master.T], axis=1)
    attn_shard = jnp.pad(attn_shard.astype(BF), ((0, 0), (0, hidden_width - attn_cols)))
    own0 = jnp.concatenate([jnp.where(core == 0, keep, got), attn_shard], axis=0)
    own0 = lax.all_gather(own0, DP, axis=0, tiled=False)
    own1 = lax.all_gather(jnp.where(core == 0, got, keep), DP, axis=0, tiled=False)

    conv_shard = jnp.concatenate(
        [conv_in.reshape(mix_rows, 3 * channels), conv_out.T], axis=1
    ).astype(BF)
    gains = jnp.concatenate([mixer_gain, ffn_gain], 1).astype(BF)
    conv_shard = jnp.concatenate(
        [conv_shard, jnp.pad(gains, ((0, 7), (0, width - 2 * dp_rows)))], axis=0
    )
    conv_half = exchange(jnp.broadcast_to(conv_shard[None], (16, *conv_shard.shape)), DP)
    conv_other = other_core(conv_half)

    def rows_of(half):
        return half[:, :mix_rows].reshape(width // 2, width)

    def gains_of(half):
        return half[:, mix_rows, : 2 * dp_rows].reshape(16, 2, dp_rows).swapaxes(0, 1).reshape(2, width)

    conv_whole = in_core_order(core, rows_of(conv_half), rows_of(conv_other))
    conv_in_w, conv_out_t = conv_whole[:, : 3 * channels], conv_whole[:, 3 * channels :]
    gains = in_core_order(core, gains_of(conv_half), gains_of(conv_other)).astype(F32)
    gain_mix, gain_ffn = (gains[0], gains[2]), (gains[1], gains[3])

    start = core * rows
    shard_start = start + lane * shard

    def shard_of(value):
        return lax.dynamic_slice_in_dim(value, shard_start, shard, 0).astype(F32)

    own_segments = lax.dynamic_slice_in_dim(segments, start, rows, 0)
    near = jnp.concatenate(
        [jnp.full((HALO,), -1, jnp.int32), segments, jnp.full((HALO,), -2, jnp.int32)]
    )
    near = lax.dynamic_slice_in_dim(near, start, rows + 2 * HALO, 0)

    padded = jnp.pad(tokens, ((HALO, HALO), (0, 0)))
    window = lax.dynamic_slice_in_dim(padded, start, rows + 2 * HALO, 0)
    normed0, scale_mix0 = rms_forward(window.astype(F32), gain_mix[0])
    normed0 = normed0.astype(BF)
    projected = dot(normed0, conv_in_w)
    in_gate = projected[:, :channels]
    out_gate = projected[:, channels : 2 * channels]
    signal = projected[:, 2 * channels :]
    product = in_gate * signal

    def same(back, count):
        return (near[HALO : HALO + count] == near[HALO - back : HALO - back + count])[:, None]

    total = jnp.zeros((rows, channels), F32)
    for back in range(3):
        moved = product[HALO - back : HALO - back + rows]
        total = total + conv_kernel[2 - back] * jnp.where(same(back, rows), moved, 0.0)
    convolved = (out_gate[HALO : HALO + rows] * total).astype(BF)
    partial = dot_cols(convolved, conv_out_t).astype(BF)
    hidden0 = shard_of(tokens) + scatter_sum(partial, "tensor")
    ffn_in0, scale_ffn0 = rms_forward(hidden0, gain_ffn[0])
    ffn_in0 = ffn_in0.astype(BF)
    own0 = after(own0, hidden0)
    other0 = other_core(own0)
    ffn_in0 = gather(ffn_in0, "tensor")
    acts0, partial = feed_forward(core_at, ffn_in0, own0, other0)
    attn_whole = in_core_order(
        core,
        own0[:, 3 * HALF :, :attn_cols].reshape(width // 2, attn_cols),
        other0[:, 3 * HALF :, :attn_cols].reshape(width // 2, attn_cols),
    )
    qkv_w, output_t = attn_whole[:, : 2 * channels], attn_whole[:, 2 * channels :]
    passed_shard = (hidden0 + scatter_sum(partial, "tensor")).astype(BF)
    passed = gather(passed_shard, "tensor")

    cosine, sine = rotation(positions_of(segments), head_dim)
    cosine = lax.dynamic_slice_in_dim(cosine, start, rows, 0)
    sine = lax.dynamic_slice_in_dim(sine, start, rows, 0)
    head_gains = jnp.stack([jnp.tile(query_gain, 2), jnp.tile(key_gain, 2)])
    head_gains = jnp.pad(head_gains, ((0, 6), (0, 0)))
    before = jnp.where(core == 0, -1, segments[:rows])
    key_column = jnp.broadcast_to(
        jnp.concatenate([before, own_segments])[:, None], (2 * rows, 128)
    )
    query_row = jnp.broadcast_to(own_segments[None, :], (8, rows))

    normed1, scale_mix1 = rms_forward(passed.astype(F32), gain_mix[1])
    normed1 = normed1.astype(BF)
    raw = dot(normed1, qkv_w)
    (low,) = whole(
        rope_forward_kernel,
        [jax.ShapeDtypeStruct((rows, 512), BF)],
        raw,
        cosine,
        sine,
        head_gains,
        vmem=16,
    )
    before_kv = lax.ppermute(low[:, 256:], "pipe", [(0, 1)])
    attended, logs = whole(
        attend_forward_kernel,
        [jax.ShapeDtypeStruct((rows, 256), BF), jax.ShapeDtypeStruct((8, rows), F32)],
        low,
        before_kv,
        key_column,
        query_row,
        scratch=[pltpu.VMEM((2 * rows, 256), BF)],
        flops=4 * 4 * rows * SPAN * 64,
        vmem=32,
    )
    partial = dot_cols(attended, output_t).astype(BF)
    hidden1 = passed_shard.astype(F32) + scatter_sum(partial, "tensor")
    ffn_in1, scale_ffn1 = rms_forward(hidden1, gain_ffn[1])
    ffn_in1 = ffn_in1.astype(BF)
    own1 = after(own1, hidden1)
    other1 = other_core(own1)
    ffn_in1 = gather(ffn_in1, "tensor")
    grad_low = lax.dynamic_slice_in_dim(cotangent, start, rows, 0)
    parts1, second, partial = feed_both(core_at, ffn_in1, grad_low, own1, other1)
    second = lax.psum_scatter(second, "tensor", scatter_dimension=0, tiled=True)
    second = lax.all_gather(
        (hidden1 + second.astype(F32)).astype(BF), "tensor", axis=0, tiled=True
    )
    swapped = other_core(jnp.where(core == 0, second, passed))
    section_output = in_core_order(core, jnp.where(core == 0, passed, second), swapped)

    def gain_sum(value, scale, grad):
        return jnp.sum(grad * value * scale, axis=0)

    grad_ffn_in = scatter_sum(partial, "tensor")
    keep1, send1 = feed_weights(core_at, ffn_in1, grad_low, parts1)
    sum1 = (keep1.astype(F32) + other_core(send1)).astype(BF)
    sum1 = sum1.reshape(-1, hidden_width)
    sum1 = lax.psum_scatter(sum1, DP, scatter_dimension=0, tiled=True)
    ffn_gain1 = gain_sum(hidden1, scale_ffn1, grad_ffn_in)
    grad_hidden = shard_of(cotangent) + rms_backward(hidden1, scale_ffn1, gain_ffn[1], grad_ffn_in)
    hidden_low = gather(grad_hidden.astype(BF), "tensor")
    grad_output_t = dot_rows(hidden_low, attended).astype(BF)
    grad_attended = dot(hidden_low, output_t).astype(BF)
    grad_query, grad_kv = whole(
        attend_backward_kernel,
        [jax.ShapeDtypeStruct((rows, 256), F32), jax.ShapeDtypeStruct((2 * rows, 256), F32)],
        low,
        before_kv,
        key_column,
        query_row,
        logs,
        grad_attended,
        scratch=[pltpu.VMEM((2 * rows, 256), BF)],
        flops=10 * 4 * rows * SPAN * 64,
        vmem=40,
    )
    more_kv = lax.ppermute(grad_kv[:rows], "pipe", [(1, 0)])
    grad_qkv, head_sums = whole(
        rope_backward_kernel,
        [jax.ShapeDtypeStruct((rows, 512), BF), jax.ShapeDtypeStruct((8, 128), F32)],
        raw,
        grad_query,
        grad_kv[rows:],
        more_kv,
        cosine,
        sine,
        head_gains,
        vmem=20,
    )
    partial = dot_cols(grad_qkv, qkv_w)
    mix_gain1 = jnp.sum(partial * passed.astype(F32) * scale_mix1, axis=0)
    grad_normed = scatter_sum(partial.astype(BF), "tensor")
    passed_f32 = passed_shard.astype(F32)
    scale_shard = lax.dynamic_slice_in_dim(scale_mix1, lane * shard, shard, 0)
    grad_passed = grad_hidden + rms_backward(passed_f32, scale_shard, gain_mix[1], grad_normed)
    grad_shard = grad_passed.astype(BF)
    grad_low = gather(grad_shard, "tensor")
    grad_passed = grad_low

    parts0, partial = feed_backward(core_at, grad_low, own0, other0, acts0)
    grad_ffn_in = scatter_sum(partial, "tensor")
    keep0, send0 = feed_weights(core_at, ffn_in0, grad_low, parts0)
    ffn_gain0 = gain_sum(hidden0, scale_ffn0, grad_ffn_in)
    grad_hidden = grad_shard.astype(F32) + rms_backward(
        hidden0, scale_ffn0, gain_ffn[0], grad_ffn_in
    )

    grad_attn = jnp.concatenate(
        [dot_rows(normed1, grad_qkv).astype(BF), grad_output_t], axis=1
    )

    attn_sum = half_of(grad_attn, core).astype(F32) + other_core(half_of(grad_attn, 1 - core))
    attn_sum = attn_sum.astype(BF).reshape(16, mix_rows, attn_cols)
    attn_sum = jnp.pad(attn_sum, ((0, 0), (0, 0), (0, hidden_width - attn_cols)))
    sum0 = (keep0.astype(F32) + other_core(send0)).astype(BF)
    sum0 = jnp.concatenate([sum0, attn_sum], axis=1)
    hidden_low = gather(grad_hidden.astype(BF), "tensor")
    sum0 = after(sum0.reshape(-1, hidden_width), hidden_low)
    sum0 = lax.psum_scatter(sum0, DP, scatter_dimension=0, tiled=True)
    grad_attn = sum0[3 * HALF :, :attn_cols].astype(F32)
    sum0 = sum0[: 3 * HALF]
    mine = jnp.where(core == 0, sum0, sum1).reshape(3, HALF, hidden_width)
    theirs = other_core(jnp.where(core == 0, sum1, sum0)).reshape(3, HALF, hidden_width)
    grad_gate, grad_up, grad_down = (
        in_core_order(core, mine[k], theirs[k]).astype(F32) for k in range(3)
    )

    following = lax.ppermute(hidden_low[:HALO], "pipe", [(1, 0)])
    hidden_more = jnp.concatenate([hidden_low, following], 0)
    grad_out_t = dot_rows(hidden_low, convolved).astype(BF)
    grad_convolved = dot(hidden_more, conv_out_t)
    grad_out_gate = grad_convolved[:rows] * total
    grad_total = grad_convolved * out_gate[HALO:]
    grad_product = jnp.zeros((rows, channels), F32)
    taps = []
    for back in range(3):
        mask = (near[HALO + back : HALO + back + rows] == near[HALO : HALO + rows])[:, None]
        grad_product = grad_product + conv_kernel[2 - back] * jnp.where(
            mask, grad_total[back : back + rows], 0.0
        )
        moved = product[HALO - back : HALO - back + rows]
        taps.append(jnp.sum(jnp.where(same(back, rows), grad_total[:rows] * moved, 0.0), axis=0))
    taps = jnp.stack(taps[::-1])
    own = slice(HALO, HALO + rows)
    grad_projected = jnp.concatenate(
        [grad_product * signal[own], grad_out_gate, grad_product * in_gate[own]], axis=1
    ).astype(BF)
    grad_conv = jnp.concatenate(
        [dot_rows(normed0[own], grad_projected).astype(BF), grad_out_t], axis=1
    )
    partial = dot_cols(grad_projected, conv_in_w)
    mix_gain0 = jnp.sum(partial * window[own].astype(F32) * scale_mix0[own], axis=0)

    taps_wide = lax.dynamic_update_slice_in_dim(
        jnp.zeros((3, width), F32), taps, lane * channels, 1
    )
    heads = (head_sums[:2, :64] + head_sums[:2, 64:]).reshape(1, 128)
    small = jnp.concatenate(
        [
            jnp.stack([mix_gain0, ffn_gain0, mix_gain1, ffn_gain1]),
            taps_wide,
            jnp.pad(heads, ((0, 0), (0, width - 128))),
        ],
        0,
    )

    def two_terms(value):
        high = value.astype(BF)
        return jnp.concatenate([high, (value - high.astype(F32)).astype(BF)], 0)

    def one_term(value):
        return value[:8] + value[8:]

    def sum_beside(blocks, small, axis):
        terms = jnp.broadcast_to(two_terms(small)[None], (blocks.shape[0], 16, width))
        parts = exchange(jnp.concatenate([blocks.astype(BF), terms], 1), axis)
        summed = jnp.sum(parts.astype(F32), axis=0)
        return summed[:-16], one_term(summed[-16:])

    terms = exchange(jnp.broadcast_to(two_terms(small)[None], (4, 16, width)), "tensor")
    small = one_term(jnp.sum(terms.astype(F32), axis=0))
    small = small + one_term(other_core(two_terms(small)).astype(F32))

    grad_normed = direct_scatter_sum(partial.astype(BF), "tensor")
    tokens_shard = shard_of(tokens)
    scale_shard = lax.dynamic_slice_in_dim(scale_mix0, HALO + lane * shard, shard, 0)
    grad_tokens = grad_hidden + rms_backward(tokens_shard, scale_shard, gain_mix[0], grad_normed)
    grad_tokens = direct_gather(grad_tokens.astype(BF), "tensor")
    swapped = other_core(jnp.where(core == 0, grad_passed, grad_tokens))
    input_grad = in_core_order(
        core, jnp.where(core == 0, grad_tokens, grad_passed), swapped
    ).astype(F32)

    blocks = half_of(grad_conv, core).astype(F32) + other_core(half_of(grad_conv, 1 - core))
    blocks, small = sum_beside(blocks.reshape(16, mix_rows, width), small, DP)

    def own_gain(pair):
        return lax.dynamic_slice(pair, (core, at_dp * dp_rows), (1, dp_rows))

    return (
        section_output[None],
        input_grad[None],
        own_gain(small[0:4:2]),
        own_gain(small[1:4:2]),
        grad_gate[None],
        grad_up[None],
        grad_down.T[None],
        blocks[:, : 3 * channels].reshape(mix_rows, 3, channels),
        small[4:7],
        blocks[:, 3 * channels :].T,
        grad_attn[:, :channels],
        grad_attn[:, channels : channels + 128],
        grad_attn[:, channels + 128 : 2 * channels],
        small[7, :64],
        small[7, 64:128],
        grad_attn[:, 2 * channels :].T,
    )


def solution(mesh):
    finer = Mesh(
        mesh.devices.reshape(mesh.shape["pipe"], mesh.shape["tensor"], 4, 4),
        ("pipe", "tensor", "dp_0", "dp_1"),
    )
    return jax.shard_map(
        per_device,
        mesh=finer,
        in_specs=(
            P(DP, None),
            P(DP, None),
            P(DP, None),
            P("pipe", DP),
            P("pipe", DP),
            P("pipe", DP, "tensor"),
            P("pipe", DP, "tensor"),
            P("pipe", "tensor", DP),
            P(PIPE_DP, None, "tensor"),
            P(None, "tensor"),
            P("tensor", PIPE_DP),
            P(PIPE_DP, "tensor"),
            P(PIPE_DP, "tensor"),
            P(PIPE_DP, "tensor"),
            P(),
            P(),
            P("tensor", PIPE_DP),
        ),
        out_specs=(
            P("pipe", DP, None),
            P("pipe", DP, None),
            P("pipe", DP),
            P("pipe", DP),
            P("pipe", DP, "tensor"),
            P("pipe", DP, "tensor"),
            P("pipe", "tensor", DP),
            P(PIPE_DP, None, "tensor"),
            P(),
            P("tensor", PIPE_DP),
            P(PIPE_DP, "tensor"),
            P(PIPE_DP, "tensor"),
            P(PIPE_DP, "tensor"),
            P(),
            P(),
            P("tensor", PIPE_DP),
        ),
        check_vma=False,
    )
```

```python
import functools

import jax
import jax.numpy as jnp
from jax import lax
from jax.experimental import pallas as pl
from jax.experimental.pallas import tpu as pltpu
from jax.sharding import Mesh
from jax.sharding import PartitionSpec as P

DP = ("dp_0", "dp_1")
PIPE_DP = ("pipe", "dp_0", "dp_1")
EPS = 1e-05
THETA = 1000000.0
NEGATIVE = -1e30
HALO = 16
BF = jnp.bfloat16
F32 = jnp.float32


def dot(left, right, dims=((1,), (0,))):
    return lax.dot_general(left, right, (dims, ((), ())), preferred_element_type=F32)


def dot_cols(left, right):
    return dot(left, right, ((1,), (1,)))


def dot_rows(left, right):
    return dot(left, right, ((0,), (0,)))


def exchange(parts, axis):
    return lax.all_to_all(parts, axis, 0, 0)


def blocks_of(value):
    return exchange(value.reshape(4, value.shape[0] // 4, value.shape[1]), "tensor")


def gathered(copies):
    return exchange(copies, "tensor").reshape(-1, copies.shape[-1])


def scatter_sum(value, axis):
    size = lax.axis_size(axis)
    parts = value.reshape(size, value.shape[0] // size, *value.shape[1:])
    return jnp.sum(exchange(parts, axis).astype(F32), axis=0)


def gather(value, axis):
    size = lax.axis_size(axis)
    parts = exchange(jnp.broadcast_to(value[None], (size, *value.shape)), axis)
    return parts.reshape(size * value.shape[0], *value.shape[1:])


def turned(value, axis, by):
    size = lax.axis_size(axis)
    return lax.ppermute(value, axis, [(i, (i + by) % size) for i in range(size)])


def direct_scatter_sum(value, axis):
    me = lax.axis_index(axis)
    rows = value.shape[0] // 4

    def block(by):
        return lax.dynamic_slice_in_dim(value, lax.rem(me + by, 4) * rows, rows, 0)

    total = block(0).astype(F32)
    for by in (1, 3, 2):
        total = total + turned(block(by), axis, by).astype(F32)
    return total


def direct_gather(value, axis):
    me = lax.axis_index(axis)
    whole = jnp.zeros((4, *value.shape), value.dtype)
    for by in (0, 1, 3, 2):
        part = turned(value, axis, by) if by else value
        whole = lax.dynamic_update_slice_in_dim(whole, part[None], lax.rem(me + 4 - by, 4), 0)
    return whole.reshape(4 * value.shape[0], *value.shape[1:])


def after(value, *others):
    return lax.optimization_barrier((value, *others))[0]


def other_core(value):
    return lax.ppermute(value, "pipe", [(0, 1), (1, 0)])


def in_core_order(core, own, other):
    return jnp.where(
        core == 0, jnp.concatenate([own, other], 0), jnp.concatenate([other, own], 0)
    )


def half_of(value, core):
    rows = value.shape[0] // 2
    return lax.dynamic_slice_in_dim(value, core * rows, rows, 0)


def rms_forward(value, gain):
    scale = lax.rsqrt(jnp.mean(value * value, axis=-1, keepdims=True) + EPS)
    return value * scale * gain, scale


def rms_backward(value, scale, gain, grad):
    weighted = grad * gain
    inner = jnp.mean(weighted * value, axis=-1, keepdims=True)
    return scale * weighted - value * (scale * scale * scale) * inner


def positions_of(segments):
    first = jnp.sum((segments[None, :] < segments[:, None]).astype(jnp.int32), axis=1)
    return jnp.arange(segments.shape[0], dtype=jnp.int32) - first


def rotation(positions, head_dim):
    half = head_dim // 2
    frequency = THETA ** (-2.0 * jnp.arange(half, dtype=F32) / head_dim)
    angle = positions.astype(F32)[:, None] * frequency[None, :]
    cosine, sine = jnp.cos(angle), jnp.sin(angle)
    return jnp.tile(cosine, (1, 4)), jnp.tile(jnp.concatenate([-sine, sine], 1), (1, 2))


def not_before(kernel, operands, needed):
    skipped = range(operands, operands + needed)

    def body(*refs):
        kernel(*(ref for k, ref in enumerate(refs) if k not in skipped))

    return body


def whole(kernel, out_shapes, *operands, scratch=(), flops=0, vmem=40, needs=()):
    kernel = not_before(kernel, len(operands), len(needs))
    spec = pl.BlockSpec(memory_space=pltpu.VMEM)
    moved = sum(x.size * x.dtype.itemsize for x in (*operands, *out_shapes))
    return pl.pallas_call(
        kernel,
        out_shape=tuple(out_shapes),
        in_specs=[spec] * len(operands) + [pl.BlockSpec(memory_space=pl.ANY)] * len(needs),
        out_specs=tuple(spec for _ in out_shapes),
        scratch_shapes=scratch,
        compiler_params=pltpu.CompilerParams(vmem_limit_bytes=vmem * 2**20),
        cost_estimate=pl.CostEstimate(flops=flops, bytes_accessed=moved, transcendentals=0),
    )(*operands, *needs)


def head_mean(value, low):
    first = jnp.sum(jnp.where(low, value, 0.0), axis=1, keepdims=True)
    second = jnp.sum(jnp.where(low, 0.0, value), axis=1, keepdims=True)
    return jnp.where(low, first, second) * (1.0 / 64.0)


def partner(value, first_half):
    return jnp.where(first_half, pltpu.roll(value, 96, 1), pltpu.roll(value, 32, 1))


def lanes_of(rows):
    lane = lax.broadcasted_iota(jnp.int32, (rows, 128), 1)
    return lane < 64, (lane & 63) < 32


CHUNK = 128


def rope_forward_kernel(raw_ref, cosine_ref, sine_ref, gain_ref, out_ref):
    rows = raw_ref.shape[0]
    low, first_half = lanes_of(CHUNK)

    @pl.loop(0, rows // CHUNK)
    def _(step):
        at = pl.ds(pl.multiple_of(step * CHUNK, CHUNK), CHUNK)
        cosine, sine = cosine_ref[at, :], sine_ref[at, :]
        for tile in range(3):
            cols = pl.ds(tile * 128, 128)
            value = raw_ref[at, cols]
            gain = gain_ref[pl.ds(tile // 2, 1), :]
            normed = value * lax.rsqrt(head_mean(value * value, low) + EPS) * gain
            turned = normed * cosine + partner(normed, first_half) * sine
            out_ref[at, cols] = turned.astype(BF)
        out_ref[at, pl.ds(384, 128)] = raw_ref[at, pl.ds(384, 128)].astype(BF)


def rope_backward_kernel(
    raw_ref, grad_query_ref, grad_kv_ref, more_kv_ref, cosine_ref, sine_ref, gain_ref, out_ref, sums_ref
):
    rows = raw_ref.shape[0]
    low, first_half = lanes_of(CHUNK)
    sums_ref[...] = jnp.zeros_like(sums_ref)

    @pl.loop(0, rows // CHUNK)
    def _(step):
        at = pl.ds(pl.multiple_of(step * CHUNK, CHUNK), CHUNK)
        cosine, sine = cosine_ref[at, :], sine_ref[at, :]
        for tile in range(3):
            cols = pl.ds(tile * 128, 128)
            if tile < 2:
                grad = grad_query_ref[at, cols]
            else:
                grad = grad_kv_ref[at, pl.ds(0, 128)] + more_kv_ref[at, pl.ds(0, 128)]
            grad = grad * cosine - partner(grad, first_half) * sine
            value = raw_ref[at, cols]
            gain = gain_ref[pl.ds(tile // 2, 1), :]
            scale = lax.rsqrt(head_mean(value * value, low) + EPS)
            weighted = grad * gain
            inner = head_mean(weighted * value, low)
            back = scale * weighted - value * (scale * scale * scale) * inner
            out_ref[at, cols] = back.astype(BF)
            sums_ref[pl.ds(tile // 2, 1), :] += jnp.sum(grad * value * scale, axis=0, keepdims=True)
        out_ref[at, pl.ds(384, 128)] = (
            grad_kv_ref[at, pl.ds(128, 128)] + more_kv_ref[at, pl.ds(128, 128)]
        ).astype(BF)


def fill_window(own_ref, before_ref, keys_ref):
    rows = own_ref.shape[0]
    keys_ref[pl.ds(0, rows), :] = before_ref[...]
    keys_ref[pl.ds(rows, rows), :] = own_ref[:, pl.ds(256, 256)]


def bias_of(column_ref, row_ref, start, block, span):
    keys = column_ref[pl.ds(start, span), pl.ds(0, 1)]
    queries = row_ref[pl.ds(0, 1), pl.ds(start, block)]
    key_at = lax.broadcasted_iota(jnp.int32, (span, block), 0)
    query_at = lax.broadcasted_iota(jnp.int32, (span, block), 1) + (span - block)
    return jnp.where((key_at <= query_at) & (keys == queries), 0.0, NEGATIVE)


BLOCK = 256
SPAN = 768


def attend_forward_kernel(own_ref, before_ref, column_ref, row_ref, out_ref, log_ref, keys_ref):
    rows = own_ref.shape[0]
    fill_window(own_ref, before_ref, keys_ref)
    log_ref[...] = jnp.zeros_like(log_ref)
    for sub in range(rows // BLOCK):
        start = sub * BLOCK
        bias = bias_of(column_ref, row_ref, start, BLOCK, SPAN)
        values = keys_ref[pl.ds(start, SPAN), pl.ds(128, 128)].astype(F32).T.astype(BF)
        parts = []
        for head in range(4):
            kv = head // 2
            key = keys_ref[pl.ds(start, SPAN), pl.ds(kv * 64, 64)]
            query = own_ref[pl.ds(start, BLOCK), pl.ds(head * 64, 64)] * jnp.asarray(0.125, BF)
            scores = dot_cols(key, query) + bias
            top = jnp.max(scores, axis=0, keepdims=True)
            weights = jnp.exp(scores - top)
            total = jnp.sum(weights, axis=0, keepdims=True)
            probs = (weights * (1.0 / total)).astype(BF)
            parts.append(dot(values[kv * 64 : kv * 64 + 64], probs))
            log_ref[pl.ds(head, 1), pl.ds(start, BLOCK)] = top + jnp.log(total)
        out_ref[pl.ds(start, BLOCK), :] = jnp.concatenate(parts, 0).T.astype(BF)


def attend_backward_kernel(
    own_ref, before_ref, column_ref, row_ref, log_ref, grad_ref, query_ref, kv_ref, keys_ref
):
    rows = own_ref.shape[0]
    fill_window(own_ref, before_ref, keys_ref)
    kv_ref[...] = jnp.zeros_like(kv_ref)
    for sub in range(rows // BLOCK):
        start = sub * BLOCK
        window = pl.ds(start, SPAN)
        bias = bias_of(column_ref, row_ref, start, BLOCK, SPAN)
        keys = keys_ref[window, pl.ds(0, 128)].astype(F32).T.astype(BF)
        parts = []
        for kv in range(2):
            key = keys_ref[window, pl.ds(kv * 64, 64)]
            value = keys_ref[window, pl.ds(128 + kv * 64, 64)]
            grad_key = jnp.zeros((SPAN, 64), F32)
            grad_value = jnp.zeros((SPAN, 64), F32)
            for head in (2 * kv, 2 * kv + 1):
                query = own_ref[pl.ds(start, BLOCK), pl.ds(head * 64, 64)] * jnp.asarray(0.125, BF)
                grad = grad_ref[pl.ds(start, BLOCK), pl.ds(head * 64, 64)]
                log = log_ref[pl.ds(head, 1), pl.ds(start, BLOCK)]
                probs = jnp.exp(dot_cols(key, query) + bias - log)
                grad_probs = dot_cols(value, grad)
                shared = jnp.sum(probs * grad_probs, axis=0, keepdims=True)
                grad_scores = (probs * (grad_probs - shared)).astype(BF)
                grad_key += dot(grad_scores, query)
                grad_value += dot(probs.astype(BF), grad)
                parts.append(dot(keys[kv * 64 : kv * 64 + 64], grad_scores) * 0.125)
            kv_ref[window, pl.ds(kv * 64, 64)] += grad_key
            kv_ref[window, pl.ds(128 + kv * 64, 64)] += grad_value
        query_ref[pl.ds(start, BLOCK), :] = jnp.concatenate(parts, 0).T


HALF = 32
GATE, UP, DOWN = range(3)


def fetch_weights(core_ref, own_ref, other_ref, weights_ref, sems, order):
    core = core_ref[0]

    def copies(k):
        return [
            pltpu.make_async_copy(
                ref.at[:, pl.ds(HALF * k, HALF), :], weights_ref.at[k, :, part], sems.at[k, side]
            )
            for side, (ref, part) in enumerate(((own_ref, core), (other_ref, 1 - core)))
        ]

    for k in order:
        for copy in copies(k):
            copy.start()

    def matrix(k):
        for copy in copies(k):
            copy.wait()
        return lambda: weights_ref[k].reshape(-1, weights_ref.shape[-1])

    return matrix


def gates_back(grad_inner, gate, up):
    sigma = 1.0 / (1.0 + jnp.exp(-gate))
    silu = gate * sigma
    grad_gate = grad_inner * up * (sigma * (1.0 + gate * (1.0 - sigma)))
    return grad_gate.astype(BF), (grad_inner * silu).astype(BF), (silu * up).astype(BF)


def silu(gate):
    return gate * (1.0 / (1.0 + jnp.exp(-gate)))


class Moved:
    def __init__(self, source, target, sem):
        self.copy = pltpu.make_async_copy(source, target, sem)

    def start(self):
        self.copy.start()
        return self

    def wait(self):
        self.copy.wait()


def feed_forward_kernel(
    core_ref, in_ref, own_ref, other_ref, acts_ref, out_ref, held_ref, weights_ref, sems, out_sems
):
    matrix = fetch_weights(core_ref, own_ref, other_ref, weights_ref, sems, (GATE, UP, DOWN))
    held_ref[0] = dot(in_ref[...], matrix(GATE)())
    first = Moved(held_ref.at[0], acts_ref.at[0], out_sems.at[0]).start()
    held_ref[1] = dot(in_ref[...], matrix(UP)())
    second = Moved(held_ref.at[1], acts_ref.at[1], out_sems.at[1]).start()
    inner = (silu(held_ref[0]) * held_ref[1]).astype(BF)
    out_ref[...] = dot_cols(inner, matrix(DOWN)()).astype(BF)
    first.wait()
    second.wait()


def send_parts(parts_ref, held_ref, sems):
    return [Moved(held_ref.at[k], parts_ref.at[k], sems.at[k]).start() for k in range(3)]


def feed_backward_kernel(
    core_ref, grad_ref, own_ref, other_ref, acts_ref, parts_ref, out_ref,
    acts_held_ref, held_ref, weights_ref, sems, in_sems, out_sems,
):
    matrix = fetch_weights(core_ref, own_ref, other_ref, weights_ref, sems, (DOWN,))
    acts = [Moved(acts_ref.at[k], acts_held_ref.at[k], in_sems.at[k]).start() for k in range(2)]
    more = fetch_weights(core_ref, own_ref, other_ref, weights_ref, sems, (GATE, UP))
    grad_inner = dot(grad_ref[...], matrix(DOWN)())
    acts[0].wait()
    acts[1].wait()
    grad_gate, grad_up, inner = gates_back(grad_inner, acts_held_ref[0], acts_held_ref[1])
    held_ref[0] = grad_gate
    held_ref[1] = grad_up
    held_ref[2] = inner
    sent = send_parts(parts_ref, held_ref, out_sems)
    out = dot_cols(held_ref[0], more(GATE)())
    out_ref[...] = (out + dot_cols(held_ref[1], more(UP)())).astype(BF)
    for copy in sent:
        copy.wait()


def feed_both_kernel(
    core_ref, in_ref, grad_ref, own_ref, other_ref, parts_ref, second_ref, out_ref,
    held_ref, weights_ref, sems, out_sems,
):
    matrix = fetch_weights(core_ref, own_ref, other_ref, weights_ref, sems, (DOWN, GATE, UP))
    down = matrix(DOWN)
    grad_inner = dot(grad_ref[...], down())
    gate_w = matrix(GATE)
    gate = dot(in_ref[...], gate_w())
    up_w = matrix(UP)
    up = dot(in_ref[...], up_w())
    grad_gate, grad_up, inner = gates_back(grad_inner, gate, up)
    held_ref[0] = grad_gate
    held_ref[1] = grad_up
    held_ref[2] = inner
    sent = send_parts(parts_ref, held_ref, out_sems)
    out = dot_cols(held_ref[0], gate_w())
    out_ref[...] = (out + dot_cols(held_ref[1], up_w())).astype(BF)
    second_ref[...] = dot_cols(held_ref[2], down()).astype(BF)
    for copy in sent:
        copy.wait()


def feed_weights_kernel(in_ref, grad_ref, part_ref, *refs):
    more_ref = refs[0] if len(refs) == 5 else None
    out_ref, done_ref, in_t_ref, grad_t_ref = refs[-4:]
    step = pl.program_id(0)
    done_ref[...] = jnp.zeros_like(done_ref)

    @pl.when(step == 0)
    def _():
        in_t_ref[...] = in_ref[...].astype(F32).T.astype(BF)
        grad_t_ref[...] = grad_ref[...].astype(F32).T.astype(BF)

    @pl.when(step < 2)
    def _():
        out_ref[...] = dot(in_t_ref[...], part_ref[0]).astype(BF).reshape(out_ref.shape)

    @pl.when(step == 2)
    def _():
        out_ref[...] = dot(grad_t_ref[...], part_ref[0]).astype(BF).reshape(out_ref.shape)

    if more_ref is not None:

        @pl.when(step == 3)
        def _():
            out_ref[...] = jnp.zeros_like(out_ref)
            wide = more_ref.shape[1]
            blocks = out_ref.shape[0]
            for part in range(2):
                rows = more_ref[pl.ds(part * blocks * HALF, blocks * HALF), :]
                out_ref[:, pl.ds(part * HALF, HALF), pl.ds(0, wide)] = rows.reshape(blocks, HALF, wide)


SMEM_SPEC = pl.BlockSpec(memory_space=pltpu.SMEM)
HBM_SPEC = pl.BlockSpec(memory_space=pltpu.HBM)
ANY_SPEC = pl.BlockSpec(memory_space=pl.ANY)
VMEM_SPEC = pl.BlockSpec(memory_space=pltpu.VMEM)


def feed(kernel, in_specs, outs, scratch, hidden, width, flops, vmem, *operands, needs=()):
    kernel = not_before(kernel, len(operands), len(needs))
    moved = sum(x.size * x.dtype.itemsize for x in (*operands, *outs))
    return pl.pallas_call(
        kernel,
        in_specs=in_specs + [ANY_SPEC] * len(needs),
        out_specs=(HBM_SPEC, *[VMEM_SPEC] * (len(outs) - 1)),
        out_shape=tuple(outs),
        scratch_shapes=[
            *scratch,
            pltpu.VMEM((3, width // (2 * HALF), 2, HALF, hidden), BF),
            pltpu.SemaphoreType.DMA((3, 2)),
            *[pltpu.SemaphoreType.DMA((3,))] * len(scratch),
        ],
        compiler_params=pltpu.CompilerParams(vmem_limit_bytes=vmem * 2**20),
        cost_estimate=pl.CostEstimate(flops=flops, bytes_accessed=moved, transcendentals=0),
    )(*operands, *needs)


def feed_forward(core, ffn_in, own, other):
    rows, width = ffn_in.shape
    hidden = own.shape[-1]
    return feed(
        feed_forward_kernel,
        [SMEM_SPEC, VMEM_SPEC, HBM_SPEC, HBM_SPEC],
        [jax.ShapeDtypeStruct((2, rows, hidden), F32), jax.ShapeDtypeStruct(ffn_in.shape, BF)],
        [pltpu.VMEM((2, rows, hidden), F32)],
        hidden, width, 6 * rows * width * hidden, FEED_VMEM,
        core, ffn_in, own, other,
    )


def feed_backward(core, grad_low, own, other, acts, needs=()):
    rows, width = grad_low.shape
    hidden = own.shape[-1]
    return feed(
        feed_backward_kernel,
        [SMEM_SPEC, VMEM_SPEC, HBM_SPEC, HBM_SPEC, HBM_SPEC],
        [jax.ShapeDtypeStruct((3, rows, hidden), BF), jax.ShapeDtypeStruct(grad_low.shape, BF)],
        [pltpu.VMEM((2, rows, hidden), F32), pltpu.VMEM((3, rows, hidden), BF)],
        hidden, width, 6 * rows * width * hidden, FEED_VMEM,
        core, grad_low, own, other, acts, needs=needs,
    )


def feed_both(core, ffn_in, grad_low, own, other):
    rows, width = grad_low.shape
    hidden = own.shape[-1]
    out = jax.ShapeDtypeStruct(grad_low.shape, BF)
    return feed(
        feed_both_kernel,
        [SMEM_SPEC, VMEM_SPEC, VMEM_SPEC, HBM_SPEC, HBM_SPEC],
        [jax.ShapeDtypeStruct((3, rows, hidden), BF), out, out],
        [pltpu.VMEM((3, rows, hidden), BF)],
        hidden, width, 12 * rows * width * hidden, FEED_VMEM,
        core, ffn_in, grad_low, own, other,
    )


FEED_VMEM = 58


def feed_weights(ffn_in, grad_low, parts, more=(), needs=()):
    rows, width = ffn_in.shape
    hidden = parts.shape[-1]
    blocks, steps = width // (2 * HALF), 3 + len(more)
    return pl.pallas_call(
        not_before(feed_weights_kernel, steps, len(needs)),
        grid=(steps,),
        in_specs=[
            VMEM_SPEC,
            VMEM_SPEC,
            pl.BlockSpec((1, rows, hidden), lambda k: (jnp.minimum(k, 2), 0, 0)),
            *[VMEM_SPEC] * len(more),
            *[ANY_SPEC] * len(needs),
        ],
        out_specs=(
            pl.BlockSpec((blocks, 2 * HALF, hidden), lambda k: (0, k, 0)),
            pl.BlockSpec((8, 128), lambda k: (0, 0)),
        ),
        out_shape=(
            shape_of(blocks, 2 * HALF * steps, hidden),
            shape_of(8, 128, kind=F32),
        ),
        scratch_shapes=[pltpu.VMEM((width, rows), BF), pltpu.VMEM((width, rows), BF)],
        compiler_params=pltpu.CompilerParams(
            dimension_semantics=("arbitrary",), vmem_limit_bytes=FEED_VMEM * 2**20
        ),
        cost_estimate=pl.CostEstimate(flops=2**20, bytes_accessed=2**20, transcendentals=0),
    )(ffn_in, grad_low, parts, *more, *needs)


def fetch_conv(core_ref, own_ref, other_ref, weights_ref, sems):
    core = core_ref[0]
    rows = pl.ds(0, HALF)
    return [
        Moved(ref.at[:, rows, :], weights_ref.at[part], sems.at[side]).start()
        for side, (ref, part) in enumerate(((own_ref, core), (other_ref, 1 - core)))
    ]


def conv_total(product_ref, near_ref, taps_ref, rows):
    total = jnp.zeros((rows, product_ref.shape[1]), F32)
    here = near_ref[pl.ds(HALO, rows), :]
    for back in range(3):
        same = here == near_ref[pl.ds(HALO - back, rows), :]
        moved = jnp.where(same, product_ref[pl.ds(HALO - back, rows), :], 0.0)
        total = total + taps_ref[pl.ds(2 - back, 1), :] * moved
    return total


def conv_forward_kernel(
    core_ref, own_ref, other_ref, window_ref, gain_ref, near_ref, taps_ref,
    projected_ref, normed_ref, convolved_ref, out_ref, weights_ref, product_ref, sems,
):
    rows, channels = convolved_ref.shape
    copies = fetch_conv(core_ref, own_ref, other_ref, weights_ref, sems)
    value = window_ref[...].astype(F32)
    scale = lax.rsqrt(jnp.mean(value * value, axis=1, keepdims=True) + EPS)
    normed = (value * scale * gain_ref[pl.ds(0, 1), :]).astype(BF)
    normed_ref[...] = normed[HALO : HALO + rows]
    for copy in copies:
        copy.wait()
    weights = weights_ref[...].reshape(-1, weights_ref.shape[-1])
    projected_ref[...] = dot(normed, weights[:, : 3 * channels])
    product_ref[...] = (
        projected_ref[:, pl.ds(0, channels)] * projected_ref[:, pl.ds(2 * channels, channels)]
    )
    out_gate = projected_ref[pl.ds(HALO, rows), pl.ds(channels, channels)]
    convolved_ref[...] = (out_gate * conv_total(product_ref, near_ref, taps_ref, rows)).astype(BF)
    out_ref[...] = dot_cols(convolved_ref[...], weights[:, 3 * channels :]).astype(BF)


def conv_backward_kernel(
    core_ref, own_ref, other_ref, window_ref, near_ref, taps_ref, projected_ref, hidden_ref, next_ref,
    grad_ref, out_ref, sums_ref, gain_ref, weights_ref, product_ref, total_ref, sems,
):
    rows, channels = hidden_ref.shape[0], taps_ref.shape[1]
    copies = fetch_conv(core_ref, own_ref, other_ref, weights_ref, sems)
    product_ref[...] = (
        projected_ref[:, pl.ds(0, channels)] * projected_ref[:, pl.ds(2 * channels, channels)]
    )
    for copy in copies:
        copy.wait()
    weights = weights_ref[...].reshape(-1, weights_ref.shape[-1])
    conv_out_t = weights[:, 3 * channels :]
    gates = pl.ds(channels, channels)
    grad_convolved = dot(hidden_ref[...], conv_out_t)
    total_ref[pl.ds(0, rows), :] = grad_convolved * projected_ref[pl.ds(HALO, rows), gates]
    total_ref[pl.ds(rows, HALO), :] = (
        dot(next_ref[...], conv_out_t) * projected_ref[pl.ds(HALO + rows, HALO), gates]
    )
    grad_gate = grad_convolved * conv_total(product_ref, near_ref, taps_ref, rows)
    grad_ref[:, gates] = grad_gate.astype(BF)
    here = near_ref[pl.ds(HALO, rows), :]
    own_total = total_ref[pl.ds(0, rows), :]
    grad_product = jnp.zeros((rows, channels), F32)
    sums_ref[...] = jnp.zeros_like(sums_ref)
    for back in range(3):
        same = here == near_ref[pl.ds(HALO + back, rows), :]
        moved = jnp.where(same, total_ref[pl.ds(back, rows), :], 0.0)
        grad_product = grad_product + taps_ref[pl.ds(2 - back, 1), :] * moved
        same = here == near_ref[pl.ds(HALO - back, rows), :]
        moved = jnp.where(same, own_total * product_ref[pl.ds(HALO - back, rows), :], 0.0)
        sums_ref[pl.ds(2 - back, 1), :] = jnp.sum(moved, axis=0, keepdims=True)
    signal = projected_ref[pl.ds(HALO, rows), pl.ds(2 * channels, channels)]
    in_gate = projected_ref[pl.ds(HALO, rows), pl.ds(0, channels)]
    grad_ref[:, pl.ds(0, channels)] = (grad_product * signal).astype(BF)
    grad_ref[:, pl.ds(2 * channels, channels)] = (grad_product * in_gate).astype(BF)
    out = dot_cols(grad_ref[...], weights[:, : 3 * channels])
    out_ref[...] = out.astype(BF)
    value = window_ref[pl.ds(HALO, rows), :].astype(F32)
    scale = lax.rsqrt(jnp.mean(value * value, axis=1, keepdims=True) + EPS)
    gain_ref[...] = jnp.zeros_like(gain_ref)
    gain_ref[pl.ds(0, 1), :] = jnp.sum(out * value * scale, axis=0, keepdims=True)


def conv_weights_kernel(
    core_ref, normed_ref, hidden_ref, grad_ref, convolved_ref, keep_ref, send_ref, in_t_ref, out_t_ref
):
    core = core_ref[0]
    half, wide = keep_ref.shape[0], grad_ref.shape[1]
    in_t_ref[...] = normed_ref[...].astype(F32).T.astype(BF)
    out_t_ref[...] = hidden_ref[...].astype(F32).T.astype(BF)
    for part, ref in ((1 - core, send_ref), (core, keep_ref)):
        at = pl.ds(pl.multiple_of(part * half, half), half)
        ref[:, pl.ds(0, wide)] = dot(in_t_ref[at, :], grad_ref[...]).astype(BF)
        ref[:, pl.ds(wide, convolved_ref.shape[1])] = dot(
            out_t_ref[at, :], convolved_ref[...]
        ).astype(BF)


def local(kernel, in_specs, outs, scratch, flops, vmem, *operands, needs=()):
    kernel = not_before(kernel, len(operands), len(needs))
    moved = sum(x.size * x.dtype.itemsize for x in (*operands, *outs))
    return pl.pallas_call(
        kernel,
        in_specs=in_specs + [ANY_SPEC] * len(needs),
        out_specs=tuple(VMEM_SPEC for _ in outs),
        out_shape=tuple(outs),
        scratch_shapes=scratch,
        compiler_params=pltpu.CompilerParams(vmem_limit_bytes=vmem * 2**20),
        cost_estimate=pl.CostEstimate(flops=flops, bytes_accessed=moved, transcendentals=0),
    )(*operands, *needs)


def conv_scratch(width, channels, rows, sums):
    return [
        pltpu.VMEM((2, width // (2 * HALF), HALF, width), BF),
        pltpu.VMEM((rows + 2 * HALO, channels), F32),
        *[pltpu.VMEM((rows + HALO, channels), F32)] * sums,
        pltpu.SemaphoreType.DMA((2,)),
    ]


def shape_of(*shape, kind=BF):
    return jax.ShapeDtypeStruct(shape, kind)


def conv_forward(core, own, other, window, gain, near, taps):
    rows, width, channels = window.shape[0] - 2 * HALO, window.shape[1], taps.shape[1]
    return local(
        conv_forward_kernel,
        [SMEM_SPEC, HBM_SPEC, HBM_SPEC] + [VMEM_SPEC] * 4,
        [
            shape_of(rows + 2 * HALO, 3 * channels, kind=F32),
            shape_of(rows, width),
            shape_of(rows, channels),
            shape_of(rows, width),
        ],
        conv_scratch(width, channels, rows, 0),
        8 * rows * width * channels, 28,
        core, own, other, window, gain, near, taps,
    )


def conv_backward(core, own, other, window, near, taps, projected, hidden, following, needs):
    rows, width, channels = hidden.shape[0], hidden.shape[1], taps.shape[1]
    return local(
        conv_backward_kernel,
        [SMEM_SPEC, HBM_SPEC, HBM_SPEC] + [VMEM_SPEC] * 6,
        [
            shape_of(rows, 3 * channels),
            shape_of(rows, width),
            shape_of(8, channels, kind=F32),
            shape_of(8, width, kind=F32),
        ],
        conv_scratch(width, channels, rows, 1),
        8 * rows * width * channels, 32,
        core, own, other, window, near, taps, projected, hidden, following, needs=needs,
    )


def conv_weights(core, normed, hidden, grad, convolved):
    rows, width = hidden.shape
    out = shape_of(width // 2, width)
    return local(
        conv_weights_kernel,
        [SMEM_SPEC] + [VMEM_SPEC] * 4,
        [out, out],
        [pltpu.VMEM((width, rows), BF)] * 2,
        2**20, 24,
        core, normed, hidden, grad, convolved,
    )


def sum_of(parts_ref, rows):
    total = parts_ref[0, pl.ds(0, rows), :].astype(F32)
    for k in range(1, 4):
        total = total + parts_ref[k, pl.ds(0, rows), :].astype(F32)
    return total


def spread(out_ref, value):
    for k in range(4):
        out_ref[k] = value


def back_kernel(parts_ref, base_ref, value_ref, gain_ref, grad_ref, out_ref, sums_ref):
    rows = base_ref.shape[0]
    grad = sum_of(parts_ref, rows)
    value = value_ref[...].astype(F32)
    scale = lax.rsqrt(jnp.mean(value * value, axis=1, keepdims=True) + EPS)
    weighted = grad * gain_ref[pl.ds(0, 1), :]
    inner = jnp.mean(weighted * value, axis=1, keepdims=True)
    back = scale * weighted - value * (scale * scale * scale) * inner
    grad_ref[...] = base_ref[...].astype(F32) + back
    spread(out_ref, grad_ref[...].astype(BF))
    sums_ref[...] = jnp.zeros_like(sums_ref)
    if parts_ref.shape[1] == rows:
        sums_ref[pl.ds(0, 1), :] = jnp.sum(grad * value * scale, axis=0, keepdims=True)
    else:
        for k in range(4):
            sums_ref[...] += (
                parts_ref[k, pl.ds(rows, 8), :].astype(F32)
                + parts_ref[k, pl.ds(rows + 8, 8), :].astype(F32)
            )


def back(parts, base, value, gain, needs=()):
    rows, width = base.shape
    return local(
        back_kernel, [VMEM_SPEC] * 4,
        [
            shape_of(rows, width, kind=F32),
            shape_of(4, rows, width),
            shape_of(8, width, kind=F32),
        ],
        [], 2**20, 16, parts, base, value, gain, needs=needs,
    )


def arrange_kernel(place_ref, own_ref, first_ref, third_ref, second_ref, mine_ref, send_ref):
    lane, core = place_ref[0], place_ref[1]
    rows, width = own_ref.shape[0], mine_ref.shape[1]
    mine = pl.ds(pl.multiple_of(core * width, width), width)
    send = pl.ds(pl.multiple_of((1 - core) * width, width), width)
    for by, ref in ((0, own_ref), (1, first_ref), (3, third_ref), (2, second_ref)):
        at = lax.rem(lane + 4 - by, 4) * rows
        at = pl.ds(pl.multiple_of(at, rows), rows)
        mine_ref[at, :] = ref[:, mine]
        send_ref[at, :] = ref[:, send]


def arrange(place, parts, needs):
    rows, width = parts[0].shape[0], parts[0].shape[1] // 2
    out = shape_of(4 * rows, width)
    return local(
        arrange_kernel, [SMEM_SPEC] + [VMEM_SPEC] * 4, [out, out],
        [], 2**20, 24, place, *parts, needs=needs,
    )


def last_sums_kernel(parts_ref, in_ref, out_ref, small_ref):
    rows, wide = in_ref.shape
    total = parts_ref[0].astype(F32)
    for k in range(1, parts_ref.shape[0]):
        total = total + parts_ref[k].astype(F32)
    in_ref[...] = total[:rows, :wide]
    out_ref[...] = total[:rows, wide:]
    small_ref[...] = total[rows : rows + 8] + total[rows + 8 :]


def last_sums(parts, wide, needs):
    rows, width = parts.shape[1] - 16, parts.shape[2]
    return local(
        last_sums_kernel, [VMEM_SPEC],
        [
            shape_of(rows, wide, kind=F32),
            shape_of(rows, width - wide, kind=F32),
            shape_of(8, width, kind=F32),
        ],
        [], 2**20, 16, parts, needs=needs,
    )


def per_device(
    tokens,
    cotangent,
    segment_ids,
    mixer_gain,
    ffn_gain,
    gate_master,
    up_master,
    down_master,
    conv_in,
    conv_kernel,
    conv_out,
    query_master,
    key_master,
    value_master,
    query_gain,
    key_gain,
    output_master,
):
    core = lax.axis_index("pipe")
    lane = lax.axis_index("tensor")
    at_dp = lax.axis_index("dp_0") * 4 + lax.axis_index("dp_1")
    seq_len, width = tokens.shape
    rows = seq_len // 2
    shard = rows // 4
    channels = conv_kernel.shape[1]
    head_dim = query_gain.shape[0]
    hidden_width = gate_master.shape[2]
    dp_rows = gate_master.shape[1]
    mix_rows = conv_in.shape[0]
    attn_cols = 3 * channels
    segments = segment_ids[0]

    core_at = core.astype(jnp.int32).reshape(1)
    dense_shard = jnp.stack([gate_master[0], up_master[0], down_master[0].T]).astype(BF)
    dense_shard = dense_shard.reshape(3, 2, HALF, hidden_width)
    keep = lax.dynamic_index_in_dim(dense_shard, core, 1, False).reshape(3 * HALF, hidden_width)
    send = lax.dynamic_index_in_dim(dense_shard, 1 - core, 1, False).reshape(3 * HALF, hidden_width)
    got = other_core(send)
    attn_shard = jnp.concatenate([query_master, key_master, value_master, output_master.T], axis=1)
    attn_shard = jnp.pad(attn_shard.astype(BF), ((0, 0), (0, hidden_width - attn_cols)))
    own0 = jnp.concatenate([jnp.where(core == 0, keep, got), attn_shard], axis=0)
    own0 = lax.all_gather(own0, DP, axis=0, tiled=False)
    own1 = lax.all_gather(jnp.where(core == 0, got, keep), DP, axis=0, tiled=False)

    conv_shard = jnp.concatenate(
        [conv_in.reshape(mix_rows, 3 * channels), conv_out.T], axis=1
    ).astype(BF)
    gains = jnp.concatenate([mixer_gain, ffn_gain], 1).astype(BF)
    conv_shard = jnp.concatenate(
        [conv_shard, jnp.pad(gains, ((0, 7), (0, width - 2 * dp_rows)))], axis=0
    )
    conv_half = exchange(jnp.broadcast_to(conv_shard[None], (16, *conv_shard.shape)), DP)
    conv_other = other_core(conv_half)

    def gains_of(half):
        return half[:, mix_rows, : 2 * dp_rows].reshape(16, 2, dp_rows).swapaxes(0, 1).reshape(2, width)

    gains = in_core_order(core, gains_of(conv_half), gains_of(conv_other)).astype(F32)
    gain_mix, gain_ffn = (gains[0], gains[2]), (gains[1], gains[3])

    start = core * rows
    shard_start = start + lane * shard

    def shard_of(value):
        return lax.dynamic_slice_in_dim(value, shard_start, shard, 0).astype(F32)

    own_segments = lax.dynamic_slice_in_dim(segments, start, rows, 0)
    near = jnp.concatenate(
        [jnp.full((HALO,), -1, jnp.int32), segments, jnp.full((HALO,), -2, jnp.int32)]
    )
    near = lax.dynamic_slice_in_dim(near, start, rows + 2 * HALO, 0)

    near = jnp.broadcast_to(near[:, None], (rows + 2 * HALO, channels))
    taps_in = jnp.pad(conv_kernel, ((0, 5), (0, 0)))

    padded = jnp.pad(tokens, ((HALO, HALO), (0, 0)))
    window = lax.dynamic_slice_in_dim(padded, start, rows + 2 * HALO, 0)
    gain_rows = jnp.broadcast_to(gain_mix[0][None], (8, width))
    projected, normed0, convolved, partial = conv_forward(
        core_at, conv_half, conv_other, window, gain_rows, near, taps_in
    )
    hidden0 = shard_of(tokens) + scatter_sum(partial, "tensor")
    ffn_in0, scale_ffn0 = rms_forward(hidden0, gain_ffn[0])
    ffn_in0 = ffn_in0.astype(BF)
    own0 = after(own0, hidden0)
    other0 = other_core(own0)
    ffn_in0 = gather(ffn_in0, "tensor")
    acts0, partial = feed_forward(core_at, ffn_in0, own0, other0)
    attn_whole = in_core_order(
        core,
        own0[:, 3 * HALF :, :attn_cols].reshape(width // 2, attn_cols),
        other0[:, 3 * HALF :, :attn_cols].reshape(width // 2, attn_cols),
    )
    qkv_w, output_t = attn_whole[:, : 2 * channels], attn_whole[:, 2 * channels :]
    passed_shard = (hidden0 + scatter_sum(partial, "tensor")).astype(BF)
    passed = gather(passed_shard, "tensor")

    cosine, sine = rotation(positions_of(segments), head_dim)
    cosine = lax.dynamic_slice_in_dim(cosine, start, rows, 0)
    sine = lax.dynamic_slice_in_dim(sine, start, rows, 0)
    head_gains = jnp.stack([jnp.tile(query_gain, 2), jnp.tile(key_gain, 2)])
    head_gains = jnp.pad(head_gains, ((0, 6), (0, 0)))
    before = jnp.where(core == 0, -1, segments[:rows])
    key_column = jnp.broadcast_to(
        jnp.concatenate([before, own_segments])[:, None], (2 * rows, 128)
    )
    query_row = jnp.broadcast_to(own_segments[None, :], (8, rows))

    normed1, scale_mix1 = rms_forward(passed.astype(F32), gain_mix[1])
    normed1 = normed1.astype(BF)
    raw = dot(normed1, qkv_w)
    (low,) = whole(
        rope_forward_kernel,
        [jax.ShapeDtypeStruct((rows, 512), BF)],
        raw,
        cosine,
        sine,
        head_gains,
        vmem=16,
    )
    before_kv = lax.ppermute(low[:, 256:], "pipe", [(0, 1)])
    attended, logs = whole(
        attend_forward_kernel,
        [jax.ShapeDtypeStruct((rows, 256), BF), jax.ShapeDtypeStruct((8, rows), F32)],
        low,
        before_kv,
        key_column,
        query_row,
        scratch=[pltpu.VMEM((2 * rows, 256), BF)],
        flops=4 * 4 * rows * SPAN * 64,
        vmem=32,
    )
    partial = dot_cols(attended, output_t).astype(BF)
    hidden1 = passed_shard.astype(F32) + scatter_sum(partial, "tensor")
    ffn_in1, scale_ffn1 = rms_forward(hidden1, gain_ffn[1])
    ffn_in1 = ffn_in1.astype(BF)
    own1 = after(own1, hidden1)
    other1 = other_core(own1)
    ffn_in1 = gather(ffn_in1, "tensor")
    grad_low = lax.dynamic_slice_in_dim(cotangent, start, rows, 0)
    parts1, second, partial = feed_both(core_at, ffn_in1, grad_low, own1, other1)
    def gain_sum(value, scale, grad):
        return jnp.sum(grad * value * scale, axis=0)

    sum1, done = feed_weights(ffn_in1, grad_low, parts1)
    gain_rows = jnp.broadcast_to(gain_ffn[1][None], (8, width))
    grad_hidden, copies, ffn_gain1 = back(
        blocks_of(partial), shard_of(cotangent), hidden1, gain_rows, (done,)
    )
    ffn_gain1 = ffn_gain1[0]
    sum1 = after(sum1.reshape(-1, hidden_width), grad_hidden)
    sum1 = lax.psum_scatter(sum1, DP, scatter_dimension=0, tiled=True)
    hidden_low = gathered(copies)
    grad_output_t = dot_rows(hidden_low, attended).astype(BF)
    grad_attended = dot(hidden_low, output_t).astype(BF)
    second = after(second, grad_attended)
    second = (hidden1 + direct_scatter_sum(second, "tensor")).astype(BF)
    grad_query, grad_kv = whole(
        attend_backward_kernel,
        [jax.ShapeDtypeStruct((rows, 256), F32), jax.ShapeDtypeStruct((2 * rows, 256), F32)],
        low,
        before_kv,
        key_column,
        query_row,
        logs,
        grad_attended,
        scratch=[pltpu.VMEM((2 * rows, 256), BF)],
        flops=10 * 4 * rows * SPAN * 64,
        vmem=40,
    )
    more_kv = lax.ppermute(grad_kv[:rows], "pipe", [(1, 0)])
    grad_qkv, head_sums = whole(
        rope_backward_kernel,
        [jax.ShapeDtypeStruct((rows, 512), BF), jax.ShapeDtypeStruct((8, 128), F32)],
        raw,
        grad_query,
        grad_kv[rows:],
        more_kv,
        cosine,
        sine,
        head_gains,
        vmem=20,
    )
    partial = dot_cols(grad_qkv, qkv_w)
    grad_attn = jnp.concatenate([dot_rows(normed1, grad_qkv).astype(BF), grad_output_t], axis=1)
    gain_rows = jnp.broadcast_to(gain_mix[1][None], (8, width))
    grad_hidden, copies, mix_gain1 = back(
        blocks_of(partial.astype(BF)), grad_hidden, passed_shard, gain_rows, (grad_attn,)
    )
    mix_gain1 = mix_gain1[0]
    grad_shard = copies[0]
    grad_low = gathered(copies)
    grad_passed = grad_low

    parts0, partial = feed_backward(
        core_at, grad_low, own0, other0, acts0, needs=(second,)
    )
    early = other_core(jnp.where(core == 0, grad_passed, passed))

    sum0, done = feed_weights(ffn_in0, grad_low, parts0, (grad_attn,), (sum1,))
    gain_rows = jnp.broadcast_to(gain_ffn[0][None], (8, width))
    grad_hidden, copies, ffn_gain0 = back(
        blocks_of(partial), grad_shard, hidden0, gain_rows, (done,)
    )
    ffn_gain0 = ffn_gain0[0]
    hidden_low = gathered(copies)

    sum0 = after(sum0.reshape(-1, hidden_width), grad_hidden)
    sum0 = lax.psum_scatter(sum0, DP, scatter_dimension=0, tiled=True)
    dense0 = sum0[: 3 * dp_rows]
    theirs = other_core(jnp.where(core == 0, sum1, dense0)).astype(F32)
    dense = jnp.where(core == 0, dense0, sum1).astype(F32) + theirs
    grad_gate, grad_up, grad_down = (dense[k * dp_rows : (k + 1) * dp_rows] for k in range(3))
    attn_both = sum0[3 * dp_rows :, :attn_cols]
    grad_attn = half_of(attn_both, core).astype(F32) + other_core(half_of(attn_both, 1 - core))

    following = lax.ppermute(hidden_low[:HALO], "pipe", [(1, 0)])
    grad_projected, partial, taps, mix_gain0 = conv_backward(
        core_at, conv_half, conv_other, window, near, taps_in, projected, hidden_low, following,
        needs=(early,),
    )
    taps, mix_gain0 = taps[:3], mix_gain0[0]

    taps_wide = lax.dynamic_update_slice_in_dim(
        jnp.zeros((3, width), F32), taps, lane * channels, 1
    )
    heads = (head_sums[:2, :64] + head_sums[:2, 64:]).reshape(1, 128)
    small = jnp.concatenate(
        [
            jnp.stack([mix_gain0, ffn_gain0, mix_gain1, ffn_gain1]),
            taps_wide,
            jnp.pad(heads, ((0, 0), (0, width - 128))),
        ],
        0,
    )

    def two_terms(value):
        high = value.astype(BF)
        return jnp.concatenate([high, (value - high.astype(F32)).astype(BF)], 0)

    def one_term(value):
        return value[:8] + value[8:]

    def sum_beside(blocks, small, axis):
        terms = jnp.broadcast_to(two_terms(small)[None], (blocks.shape[0], 16, width))
        parts = exchange(jnp.concatenate([blocks.astype(BF), terms], 1), axis)
        summed = jnp.sum(parts.astype(F32), axis=0)
        return summed[:-16], one_term(summed[-16:])

    grad_normed, small = sum_beside(partial.reshape(4, shard, width), small, "tensor")
    small = small + one_term(other_core(two_terms(small)).astype(F32))
    tokens_shard = shard_of(tokens)
    scale_shard = rms_forward(tokens_shard, gain_mix[0])[1]
    grad_tokens = grad_hidden + rms_backward(tokens_shard, scale_shard, gain_mix[0], grad_normed)
    late = jnp.concatenate([grad_tokens.astype(BF), second], axis=1)
    keep, send = conv_weights(core_at, normed0, hidden_low, grad_projected, convolved)
    blocks = keep.astype(F32) + other_core(send)
    terms = jnp.broadcast_to(two_terms(small)[None], (16, 16, width))
    blocks = jnp.concatenate([blocks.astype(BF).reshape(16, mix_rows, width), terms], 1)
    grad_in, grad_out, small = last_sums(
        exchange(blocks, DP), 3 * channels, ()
    )

    parts = [late, *(turned(late, "tensor", by) for by in (1, 3, 2))]
    place = jnp.stack([lane, core]).astype(jnp.int32)
    mine, send = arrange(place, parts, (small,))
    swapped = other_core(send)
    section_output = jnp.where(
        core == 0, jnp.concatenate([passed, early], 0), jnp.concatenate([swapped, mine], 0)
    )
    input_grad = jnp.where(
        core == 0, jnp.concatenate([mine, swapped], 0), jnp.concatenate([early, grad_passed], 0)
    ).astype(F32)

    def own_gain(pair):
        return lax.dynamic_slice(pair, (core, at_dp * dp_rows), (1, dp_rows))

    return (
        section_output[None],
        input_grad[None],
        own_gain(small[0:4:2]),
        own_gain(small[1:4:2]),
        grad_gate[None],
        grad_up[None],
        grad_down.T[None],
        grad_in.reshape(mix_rows, 3, channels),
        small[4:7],
        grad_out.T,
        grad_attn[:, :channels],
        grad_attn[:, channels : channels + 128],
        grad_attn[:, channels + 128 : 2 * channels],
        small[7, :64],
        small[7, 64:128],
        grad_attn[:, 2 * channels :].T,
    )


def solution(mesh):
    finer = Mesh(
        mesh.devices.reshape(mesh.shape["pipe"], mesh.shape["tensor"], 4, 4),
        ("pipe", "tensor", "dp_0", "dp_1"),
    )
    return jax.shard_map(
        per_device,
        mesh=finer,
        in_specs=(
            P(DP, None),
            P(DP, None),
            P(DP, None),
            P("pipe", DP),
            P("pipe", DP),
            P("pipe", DP, "tensor"),
            P("pipe", DP, "tensor"),
            P("pipe", "tensor", DP),
            P(PIPE_DP, None, "tensor"),
            P(None, "tensor"),
            P("tensor", PIPE_DP),
            P(PIPE_DP, "tensor"),
            P(PIPE_DP, "tensor"),
            P(PIPE_DP, "tensor"),
            P(),
            P(),
            P("tensor", PIPE_DP),
        ),
        out_specs=(
            P("pipe", DP, None),
            P("pipe", DP, None),
            P("pipe", DP),
            P("pipe", DP),
            P("pipe", DP, "tensor"),
            P("pipe", DP, "tensor"),
            P("pipe", "tensor", DP),
            P(PIPE_DP, None, "tensor"),
            P(),
            P("tensor", PIPE_DP),
            P(PIPE_DP, "tensor"),
            P(PIPE_DP, "tensor"),
            P(PIPE_DP, "tensor"),
            P(),
            P(),
            P("tensor", PIPE_DP),
        ),
        check_vma=False,
    )
```

```python
import functools

import jax
import jax.numpy as jnp
from jax import lax
from jax.experimental import pallas as pl
from jax.experimental.pallas import tpu as pltpu
from jax.sharding import Mesh
from jax.sharding import PartitionSpec as P

DP = ("dp_0", "dp_1")
PIPE_DP = ("pipe", "dp_0", "dp_1")
EPS = 1e-05
THETA = 1000000.0
NEGATIVE = -1e30
HALO = 16
BF = jnp.bfloat16
F32 = jnp.float32


def dot(left, right, dims=((1,), (0,))):
    return lax.dot_general(left, right, (dims, ((), ())), preferred_element_type=F32)


def dot_cols(left, right):
    return dot(left, right, ((1,), (1,)))


def dot_rows(left, right):
    return dot(left, right, ((0,), (0,)))


def exchange(parts, axis):
    return lax.all_to_all(parts, axis, 0, 0)


def blocks_of(value):
    return exchange(value.reshape(4, value.shape[0] // 4, value.shape[1]), "tensor")


def gathered(copies):
    return exchange(copies, "tensor").reshape(-1, copies.shape[-1])


def scatter_sum(value, axis):
    size = lax.axis_size(axis)
    parts = value.reshape(size, value.shape[0] // size, *value.shape[1:])
    return jnp.sum(exchange(parts, axis).astype(F32), axis=0)


def gather(value, axis):
    size = lax.axis_size(axis)
    parts = exchange(jnp.broadcast_to(value[None], (size, *value.shape)), axis)
    return parts.reshape(size * value.shape[0], *value.shape[1:])


def turned(value, axis, by):
    size = lax.axis_size(axis)
    return lax.ppermute(value, axis, [(i, (i + by) % size) for i in range(size)])


def direct_scatter_sum(value, axis):
    me = lax.axis_index(axis)
    rows = value.shape[0] // 4

    def block(by):
        return lax.dynamic_slice_in_dim(value, lax.rem(me + by, 4) * rows, rows, 0)

    total = block(0).astype(F32)
    for by in (1, 3, 2):
        total = total + turned(block(by), axis, by).astype(F32)
    return total


def direct_gather(value, axis):
    me = lax.axis_index(axis)
    whole = jnp.zeros((4, *value.shape), value.dtype)
    for by in (0, 1, 3, 2):
        part = turned(value, axis, by) if by else value
        whole = lax.dynamic_update_slice_in_dim(whole, part[None], lax.rem(me + 4 - by, 4), 0)
    return whole.reshape(4 * value.shape[0], *value.shape[1:])


def after(value, *others):
    return lax.optimization_barrier((value, *others))[0]


def other_core(value):
    return lax.ppermute(value, "pipe", [(0, 1), (1, 0)])


def in_core_order(core, own, other):
    return jnp.where(
        core == 0, jnp.concatenate([own, other], 0), jnp.concatenate([other, own], 0)
    )


def half_of(value, core):
    rows = value.shape[0] // 2
    return lax.dynamic_slice_in_dim(value, core * rows, rows, 0)


def rms_forward(value, gain):
    scale = lax.rsqrt(jnp.mean(value * value, axis=-1, keepdims=True) + EPS)
    return value * scale * gain, scale


def rms_backward(value, scale, gain, grad):
    weighted = grad * gain
    inner = jnp.mean(weighted * value, axis=-1, keepdims=True)
    return scale * weighted - value * (scale * scale * scale) * inner


def positions_of(segments):
    first = jnp.sum((segments[None, :] < segments[:, None]).astype(jnp.int32), axis=1)
    return jnp.arange(segments.shape[0], dtype=jnp.int32) - first


def rotation(positions, head_dim):
    half = head_dim // 2
    frequency = THETA ** (-2.0 * jnp.arange(half, dtype=F32) / head_dim)
    angle = positions.astype(F32)[:, None] * frequency[None, :]
    cosine, sine = jnp.cos(angle), jnp.sin(angle)
    return jnp.tile(cosine, (1, 4)), jnp.tile(jnp.concatenate([-sine, sine], 1), (1, 2))


def not_before(kernel, operands, needed):
    skipped = range(operands, operands + needed)

    def body(*refs):
        kernel(*(ref for k, ref in enumerate(refs) if k not in skipped))

    return body


def whole(kernel, out_shapes, *operands, scratch=(), flops=0, vmem=40, needs=()):
    kernel = not_before(kernel, len(operands), len(needs))
    spec = pl.BlockSpec(memory_space=pltpu.VMEM)
    moved = sum(x.size * x.dtype.itemsize for x in (*operands, *out_shapes))
    return pl.pallas_call(
        kernel,
        out_shape=tuple(out_shapes),
        in_specs=[spec] * len(operands) + [pl.BlockSpec(memory_space=pl.ANY)] * len(needs),
        out_specs=tuple(spec for _ in out_shapes),
        scratch_shapes=scratch,
        compiler_params=pltpu.CompilerParams(vmem_limit_bytes=vmem * 2**20),
        cost_estimate=pl.CostEstimate(flops=flops, bytes_accessed=moved, transcendentals=0),
    )(*operands, *needs)


def head_mean(value, low):
    first = jnp.sum(jnp.where(low, value, 0.0), axis=1, keepdims=True)
    second = jnp.sum(jnp.where(low, 0.0, value), axis=1, keepdims=True)
    return jnp.where(low, first, second) * (1.0 / 64.0)


def partner(value, first_half):
    return jnp.where(first_half, pltpu.roll(value, 96, 1), pltpu.roll(value, 32, 1))


def lanes_of(rows):
    lane = lax.broadcasted_iota(jnp.int32, (rows, 128), 1)
    return lane < 64, (lane & 63) < 32


CHUNK = 128


def rope_forward_kernel(raw_ref, cosine_ref, sine_ref, gain_ref, out_ref):
    rows = raw_ref.shape[0]
    low, first_half = lanes_of(CHUNK)

    @pl.loop(0, rows // CHUNK)
    def _(step):
        at = pl.ds(pl.multiple_of(step * CHUNK, CHUNK), CHUNK)
        cosine, sine = cosine_ref[at, :], sine_ref[at, :]
        for tile in range(3):
            cols = pl.ds(tile * 128, 128)
            value = raw_ref[at, cols]
            gain = gain_ref[pl.ds(tile // 2, 1), :]
            normed = value * lax.rsqrt(head_mean(value * value, low) + EPS) * gain
            turned = normed * cosine + partner(normed, first_half) * sine
            out_ref[at, cols] = turned.astype(BF)
        out_ref[at, pl.ds(384, 128)] = raw_ref[at, pl.ds(384, 128)].astype(BF)


def rope_backward_kernel(
    raw_ref, grad_query_ref, grad_kv_ref, more_kv_ref, cosine_ref, sine_ref, gain_ref, out_ref, sums_ref
):
    rows = raw_ref.shape[0]
    low, first_half = lanes_of(CHUNK)
    sums_ref[...] = jnp.zeros_like(sums_ref)

    @pl.loop(0, rows // CHUNK)
    def _(step):
        at = pl.ds(pl.multiple_of(step * CHUNK, CHUNK), CHUNK)
        cosine, sine = cosine_ref[at, :], sine_ref[at, :]
        for tile in range(3):
            cols = pl.ds(tile * 128, 128)
            if tile < 2:
                grad = grad_query_ref[at, cols]
            else:
                grad = grad_kv_ref[at, pl.ds(0, 128)] + more_kv_ref[at, pl.ds(0, 128)]
            grad = grad * cosine - partner(grad, first_half) * sine
            value = raw_ref[at, cols]
            gain = gain_ref[pl.ds(tile // 2, 1), :]
            scale = lax.rsqrt(head_mean(value * value, low) + EPS)
            weighted = grad * gain
            inner = head_mean(weighted * value, low)
            back = scale * weighted - value * (scale * scale * scale) * inner
            out_ref[at, cols] = back.astype(BF)
            sums_ref[pl.ds(tile // 2, 1), :] += jnp.sum(grad * value * scale, axis=0, keepdims=True)
        out_ref[at, pl.ds(384, 128)] = (
            grad_kv_ref[at, pl.ds(128, 128)] + more_kv_ref[at, pl.ds(128, 128)]
        ).astype(BF)


def fill_window(own_ref, before_ref, keys_ref):
    rows = own_ref.shape[0]
    keys_ref[pl.ds(0, rows), :] = before_ref[...]
    keys_ref[pl.ds(rows, rows), :] = own_ref[:, pl.ds(256, 256)]


def bias_of(column_ref, row_ref, start, block, span):
    keys = column_ref[pl.ds(start, span), pl.ds(0, 1)]
    queries = row_ref[pl.ds(0, 1), pl.ds(start, block)]
    key_at = lax.broadcasted_iota(jnp.int32, (span, block), 0)
    query_at = lax.broadcasted_iota(jnp.int32, (span, block), 1) + (span - block)
    return jnp.where((key_at <= query_at) & (keys == queries), 0.0, NEGATIVE)


BLOCK = 256
SPAN = 768


def attend_forward_kernel(own_ref, before_ref, column_ref, row_ref, out_ref, log_ref, keys_ref):
    rows = own_ref.shape[0]
    fill_window(own_ref, before_ref, keys_ref)
    log_ref[...] = jnp.zeros_like(log_ref)
    for sub in range(rows // BLOCK):
        start = sub * BLOCK
        bias = bias_of(column_ref, row_ref, start, BLOCK, SPAN)
        values = keys_ref[pl.ds(start, SPAN), pl.ds(128, 128)].astype(F32).T.astype(BF)
        parts = []
        for head in range(4):
            kv = head // 2
            key = keys_ref[pl.ds(start, SPAN), pl.ds(kv * 64, 64)]
            query = own_ref[pl.ds(start, BLOCK), pl.ds(head * 64, 64)] * jnp.asarray(0.125, BF)
            scores = dot_cols(key, query) + bias
            top = jnp.max(scores, axis=0, keepdims=True)
            weights = jnp.exp(scores - top)
            total = jnp.sum(weights, axis=0, keepdims=True)
            probs = (weights * (1.0 / total)).astype(BF)
            parts.append(dot(values[kv * 64 : kv * 64 + 64], probs))
            log_ref[pl.ds(head, 1), pl.ds(start, BLOCK)] = top + jnp.log(total)
        out_ref[pl.ds(start, BLOCK), :] = jnp.concatenate(parts, 0).T.astype(BF)


def attend_backward_kernel(
    own_ref, before_ref, column_ref, row_ref, log_ref, grad_ref, query_ref, kv_ref, keys_ref
):
    rows = own_ref.shape[0]
    fill_window(own_ref, before_ref, keys_ref)
    kv_ref[...] = jnp.zeros_like(kv_ref)
    for sub in range(rows // BLOCK):
        start = sub * BLOCK
        window = pl.ds(start, SPAN)
        bias = bias_of(column_ref, row_ref, start, BLOCK, SPAN)
        keys = keys_ref[window, pl.ds(0, 128)].astype(F32).T.astype(BF)
        parts = []
        for kv in range(2):
            key = keys_ref[window, pl.ds(kv * 64, 64)]
            value = keys_ref[window, pl.ds(128 + kv * 64, 64)]
            grad_key = jnp.zeros((SPAN, 64), F32)
            grad_value = jnp.zeros((SPAN, 64), F32)
            for head in (2 * kv, 2 * kv + 1):
                query = own_ref[pl.ds(start, BLOCK), pl.ds(head * 64, 64)] * jnp.asarray(0.125, BF)
                grad = grad_ref[pl.ds(start, BLOCK), pl.ds(head * 64, 64)]
                log = log_ref[pl.ds(head, 1), pl.ds(start, BLOCK)]
                probs = jnp.exp(dot_cols(key, query) + bias - log)
                grad_probs = dot_cols(value, grad)
                shared = jnp.sum(probs * grad_probs, axis=0, keepdims=True)
                grad_scores = (probs * (grad_probs - shared)).astype(BF)
                grad_key += dot(grad_scores, query)
                grad_value += dot(probs.astype(BF), grad)
                parts.append(dot(keys[kv * 64 : kv * 64 + 64], grad_scores) * 0.125)
            kv_ref[window, pl.ds(kv * 64, 64)] += grad_key
            kv_ref[window, pl.ds(128 + kv * 64, 64)] += grad_value
        query_ref[pl.ds(start, BLOCK), :] = jnp.concatenate(parts, 0).T


HALF = 32
GATE, UP, DOWN = range(3)


def fetch_weights(core_ref, own_ref, other_ref, weights_ref, sems, order):
    core = core_ref[0]

    def copies(k):
        return [
            pltpu.make_async_copy(
                ref.at[:, pl.ds(HALF * k, HALF), :], weights_ref.at[k, :, part], sems.at[k, side]
            )
            for side, (ref, part) in enumerate(((own_ref, core), (other_ref, 1 - core)))
        ]

    for k in order:
        for copy in copies(k):
            copy.start()

    def matrix(k):
        for copy in copies(k):
            copy.wait()
        return lambda: weights_ref[k].reshape(-1, weights_ref.shape[-1])

    return matrix


def gates_back(grad_inner, gate, up):
    sigma = 1.0 / (1.0 + jnp.exp(-gate))
    silu = gate * sigma
    grad_gate = grad_inner * up * (sigma * (1.0 + gate * (1.0 - sigma)))
    return grad_gate.astype(BF), (grad_inner * silu).astype(BF), (silu * up).astype(BF)


def silu(gate):
    return gate * (1.0 / (1.0 + jnp.exp(-gate)))


class Moved:
    def __init__(self, source, target, sem):
        self.copy = pltpu.make_async_copy(source, target, sem)

    def start(self):
        self.copy.start()
        return self

    def wait(self):
        self.copy.wait()


def feed_forward_kernel(
    core_ref, in_ref, own_ref, other_ref, acts_ref, out_ref, held_ref, weights_ref, sems, out_sems
):
    matrix = fetch_weights(core_ref, own_ref, other_ref, weights_ref, sems, (GATE, UP, DOWN))
    held_ref[0] = dot(in_ref[...], matrix(GATE)())
    first = Moved(held_ref.at[0], acts_ref.at[0], out_sems.at[0]).start()
    held_ref[1] = dot(in_ref[...], matrix(UP)())
    second = Moved(held_ref.at[1], acts_ref.at[1], out_sems.at[1]).start()
    inner = (silu(held_ref[0]) * held_ref[1]).astype(BF)
    out_ref[...] = dot_cols(inner, matrix(DOWN)()).astype(BF)
    first.wait()
    second.wait()


def send_parts(parts_ref, held_ref, sems):
    return [Moved(held_ref.at[k], parts_ref.at[k], sems.at[k]).start() for k in range(3)]


def feed_backward_kernel(
    core_ref, grad_ref, own_ref, other_ref, acts_ref, parts_ref, out_ref,
    acts_held_ref, held_ref, weights_ref, sems, in_sems, out_sems,
):
    matrix = fetch_weights(core_ref, own_ref, other_ref, weights_ref, sems, (DOWN,))
    acts = [Moved(acts_ref.at[k], acts_held_ref.at[k], in_sems.at[k]).start() for k in range(2)]
    more = fetch_weights(core_ref, own_ref, other_ref, weights_ref, sems, (GATE, UP))
    grad_inner = dot(grad_ref[...], matrix(DOWN)())
    acts[0].wait()
    acts[1].wait()
    grad_gate, grad_up, inner = gates_back(grad_inner, acts_held_ref[0], acts_held_ref[1])
    held_ref[0] = grad_gate
    held_ref[1] = grad_up
    held_ref[2] = inner
    sent = send_parts(parts_ref, held_ref, out_sems)
    out = dot_cols(held_ref[0], more(GATE)())
    out_ref[...] = (out + dot_cols(held_ref[1], more(UP)())).astype(BF)
    for copy in sent:
        copy.wait()


def feed_both_kernel(
    core_ref, in_ref, grad_ref, own_ref, other_ref, parts_ref, second_ref, out_ref,
    held_ref, weights_ref, sems, out_sems,
):
    matrix = fetch_weights(core_ref, own_ref, other_ref, weights_ref, sems, (DOWN, GATE, UP))
    down = matrix(DOWN)
    grad_inner = dot(grad_ref[...], down())
    gate_w = matrix(GATE)
    gate = dot(in_ref[...], gate_w())
    up_w = matrix(UP)
    up = dot(in_ref[...], up_w())
    grad_gate, grad_up, inner = gates_back(grad_inner, gate, up)
    held_ref[0] = grad_gate
    held_ref[1] = grad_up
    held_ref[2] = inner
    sent = send_parts(parts_ref, held_ref, out_sems)
    out = dot_cols(held_ref[0], gate_w())
    out_ref[...] = (out + dot_cols(held_ref[1], up_w())).astype(BF)
    second_ref[...] = dot_cols(held_ref[2], down()).astype(BF)
    for copy in sent:
        copy.wait()


def feed_weights_kernel(in_ref, grad_ref, part_ref, *refs):
    more_ref = refs[0] if len(refs) == 5 else None
    out_ref, done_ref, in_t_ref, grad_t_ref = refs[-4:]
    step = pl.program_id(0)
    done_ref[...] = jnp.zeros_like(done_ref)

    @pl.when(step == 0)
    def _():
        in_t_ref[...] = in_ref[...].astype(F32).T.astype(BF)
        grad_t_ref[...] = grad_ref[...].astype(F32).T.astype(BF)

    @pl.when(step < 2)
    def _():
        out_ref[...] = dot(in_t_ref[...], part_ref[0]).astype(BF).reshape(out_ref.shape)

    @pl.when(step == 2)
    def _():
        out_ref[...] = dot(grad_t_ref[...], part_ref[0]).astype(BF).reshape(out_ref.shape)

    if more_ref is not None:

        @pl.when(step == 3)
        def _():
            out_ref[...] = jnp.zeros_like(out_ref)
            wide = more_ref.shape[1]
            blocks = out_ref.shape[0]
            for part in range(2):
                rows = more_ref[pl.ds(part * blocks * HALF, blocks * HALF), :]
                out_ref[:, pl.ds(part * HALF, HALF), pl.ds(0, wide)] = rows.reshape(blocks, HALF, wide)


SMEM_SPEC = pl.BlockSpec(memory_space=pltpu.SMEM)
HBM_SPEC = pl.BlockSpec(memory_space=pltpu.HBM)
ANY_SPEC = pl.BlockSpec(memory_space=pl.ANY)
VMEM_SPEC = pl.BlockSpec(memory_space=pltpu.VMEM)


def feed(kernel, in_specs, outs, scratch, hidden, width, flops, vmem, *operands, needs=()):
    kernel = not_before(kernel, len(operands), len(needs))
    moved = sum(x.size * x.dtype.itemsize for x in (*operands, *outs))
    return pl.pallas_call(
        kernel,
        in_specs=in_specs + [ANY_SPEC] * len(needs),
        out_specs=(HBM_SPEC, *[VMEM_SPEC] * (len(outs) - 1)),
        out_shape=tuple(outs),
        scratch_shapes=[
            *scratch,
            pltpu.VMEM((3, width // (2 * HALF), 2, HALF, hidden), BF),
            pltpu.SemaphoreType.DMA((3, 2)),
            *[pltpu.SemaphoreType.DMA((3,))] * len(scratch),
        ],
        compiler_params=pltpu.CompilerParams(vmem_limit_bytes=vmem * 2**20),
        cost_estimate=pl.CostEstimate(flops=flops, bytes_accessed=moved, transcendentals=0),
    )(*operands, *needs)


def feed_forward(core, ffn_in, own, other):
    rows, width = ffn_in.shape
    hidden = own.shape[-1]
    return feed(
        feed_forward_kernel,
        [SMEM_SPEC, VMEM_SPEC, HBM_SPEC, HBM_SPEC],
        [jax.ShapeDtypeStruct((2, rows, hidden), F32), jax.ShapeDtypeStruct(ffn_in.shape, BF)],
        [pltpu.VMEM((2, rows, hidden), F32)],
        hidden, width, 6 * rows * width * hidden, FEED_VMEM,
        core, ffn_in, own, other,
    )


def feed_backward(core, grad_low, own, other, acts, needs=()):
    rows, width = grad_low.shape
    hidden = own.shape[-1]
    return feed(
        feed_backward_kernel,
        [SMEM_SPEC, VMEM_SPEC, HBM_SPEC, HBM_SPEC, HBM_SPEC],
        [jax.ShapeDtypeStruct((3, rows, hidden), BF), jax.ShapeDtypeStruct(grad_low.shape, BF)],
        [pltpu.VMEM((2, rows, hidden), F32), pltpu.VMEM((3, rows, hidden), BF)],
        hidden, width, 6 * rows * width * hidden, FEED_VMEM,
        core, grad_low, own, other, acts, needs=needs,
    )


def feed_both(core, ffn_in, grad_low, own, other):
    rows, width = grad_low.shape
    hidden = own.shape[-1]
    out = jax.ShapeDtypeStruct(grad_low.shape, BF)
    return feed(
        feed_both_kernel,
        [SMEM_SPEC, VMEM_SPEC, VMEM_SPEC, HBM_SPEC, HBM_SPEC],
        [jax.ShapeDtypeStruct((3, rows, hidden), BF), out, out],
        [pltpu.VMEM((3, rows, hidden), BF)],
        hidden, width, 12 * rows * width * hidden, FEED_VMEM,
        core, ffn_in, grad_low, own, other,
    )


FEED_VMEM = 58


def feed_weights(ffn_in, grad_low, parts, more=(), needs=()):
    rows, width = ffn_in.shape
    hidden = parts.shape[-1]
    blocks, steps = width // (2 * HALF), 3 + len(more)
    return pl.pallas_call(
        not_before(feed_weights_kernel, steps, len(needs)),
        grid=(steps,),
        in_specs=[
            VMEM_SPEC,
            VMEM_SPEC,
            pl.BlockSpec((1, rows, hidden), lambda k: (jnp.minimum(k, 2), 0, 0)),
            *[VMEM_SPEC] * len(more),
            *[ANY_SPEC] * len(needs),
        ],
        out_specs=(
            pl.BlockSpec((blocks, 2 * HALF, hidden), lambda k: (0, k, 0)),
            pl.BlockSpec((8, 128), lambda k: (0, 0)),
        ),
        out_shape=(
            shape_of(blocks, 2 * HALF * steps, hidden),
            shape_of(8, 128, kind=F32),
        ),
        scratch_shapes=[pltpu.VMEM((width, rows), BF), pltpu.VMEM((width, rows), BF)],
        compiler_params=pltpu.CompilerParams(
            dimension_semantics=("arbitrary",), vmem_limit_bytes=FEED_VMEM * 2**20
        ),
        cost_estimate=pl.CostEstimate(flops=2**20, bytes_accessed=2**20, transcendentals=0),
    )(ffn_in, grad_low, parts, *more, *needs)


def fetch_conv(core_ref, own_ref, other_ref, weights_ref, sems):
    core = core_ref[0]
    rows = pl.ds(0, HALF)
    return [
        Moved(ref.at[:, rows, :], weights_ref.at[part], sems.at[side]).start()
        for side, (ref, part) in enumerate(((own_ref, core), (other_ref, 1 - core)))
    ]


def conv_total(product_ref, near_ref, taps_ref, rows):
    total = jnp.zeros((rows, product_ref.shape[1]), F32)
    here = near_ref[pl.ds(HALO, rows), :]
    for back in range(3):
        same = here == near_ref[pl.ds(HALO - back, rows), :]
        moved = jnp.where(same, product_ref[pl.ds(HALO - back, rows), :], 0.0)
        total = total + taps_ref[pl.ds(2 - back, 1), :] * moved
    return total


def conv_forward_kernel(
    core_ref, own_ref, other_ref, window_ref, gain_ref, near_ref, taps_ref,
    projected_ref, normed_ref, convolved_ref, out_ref, weights_ref, product_ref, sems,
):
    rows, channels = convolved_ref.shape
    copies = fetch_conv(core_ref, own_ref, other_ref, weights_ref, sems)
    value = window_ref[...].astype(F32)
    scale = lax.rsqrt(jnp.mean(value * value, axis=1, keepdims=True) + EPS)
    normed = (value * scale * gain_ref[pl.ds(0, 1), :]).astype(BF)
    normed_ref[...] = normed[HALO : HALO + rows]
    for copy in copies:
        copy.wait()
    weights = weights_ref[...].reshape(-1, weights_ref.shape[-1])
    projected_ref[...] = dot(normed, weights[:, : 3 * channels])
    product_ref[...] = (
        projected_ref[:, pl.ds(0, channels)] * projected_ref[:, pl.ds(2 * channels, channels)]
    )
    out_gate = projected_ref[pl.ds(HALO, rows), pl.ds(channels, channels)]
    convolved_ref[...] = (out_gate * conv_total(product_ref, near_ref, taps_ref, rows)).astype(BF)
    out_ref[...] = dot_cols(convolved_ref[...], weights[:, 3 * channels :]).astype(BF)


def conv_backward_kernel(
    core_ref, own_ref, other_ref, window_ref, near_ref, taps_ref, projected_ref, hidden_ref, next_ref,
    grad_ref, out_ref, sums_ref, gain_ref, weights_ref, product_ref, total_ref, sems,
):
    rows, channels = hidden_ref.shape[0], taps_ref.shape[1]
    copies = fetch_conv(core_ref, own_ref, other_ref, weights_ref, sems)
    product_ref[...] = (
        projected_ref[:, pl.ds(0, channels)] * projected_ref[:, pl.ds(2 * channels, channels)]
    )
    for copy in copies:
        copy.wait()
    weights = weights_ref[...].reshape(-1, weights_ref.shape[-1])
    conv_out_t = weights[:, 3 * channels :]
    gates = pl.ds(channels, channels)
    grad_convolved = dot(hidden_ref[...], conv_out_t)
    total_ref[pl.ds(0, rows), :] = grad_convolved * projected_ref[pl.ds(HALO, rows), gates]
    total_ref[pl.ds(rows, HALO), :] = (
        dot(next_ref[...], conv_out_t) * projected_ref[pl.ds(HALO + rows, HALO), gates]
    )
    grad_gate = grad_convolved * conv_total(product_ref, near_ref, taps_ref, rows)
    grad_ref[:, gates] = grad_gate.astype(BF)
    here = near_ref[pl.ds(HALO, rows), :]
    own_total = total_ref[pl.ds(0, rows), :]
    grad_product = jnp.zeros((rows, channels), F32)
    sums_ref[...] = jnp.zeros_like(sums_ref)
    for back in range(3):
        same = here == near_ref[pl.ds(HALO + back, rows), :]
        moved = jnp.where(same, total_ref[pl.ds(back, rows), :], 0.0)
        grad_product = grad_product + taps_ref[pl.ds(2 - back, 1), :] * moved
        same = here == near_ref[pl.ds(HALO - back, rows), :]
        moved = jnp.where(same, own_total * product_ref[pl.ds(HALO - back, rows), :], 0.0)
        sums_ref[pl.ds(2 - back, 1), :] = jnp.sum(moved, axis=0, keepdims=True)
    signal = projected_ref[pl.ds(HALO, rows), pl.ds(2 * channels, channels)]
    in_gate = projected_ref[pl.ds(HALO, rows), pl.ds(0, channels)]
    grad_ref[:, pl.ds(0, channels)] = (grad_product * signal).astype(BF)
    grad_ref[:, pl.ds(2 * channels, channels)] = (grad_product * in_gate).astype(BF)
    out = dot_cols(grad_ref[...], weights[:, : 3 * channels])
    out_ref[...] = out.astype(BF)
    value = window_ref[pl.ds(HALO, rows), :].astype(F32)
    scale = lax.rsqrt(jnp.mean(value * value, axis=1, keepdims=True) + EPS)
    gain_ref[...] = jnp.zeros_like(gain_ref)
    gain_ref[pl.ds(0, 1), :] = jnp.sum(out * value * scale, axis=0, keepdims=True)


def conv_weights_kernel(
    core_ref, normed_ref, hidden_ref, grad_ref, convolved_ref, keep_ref, send_ref, in_t_ref, out_t_ref
):
    core = core_ref[0]
    half, wide = keep_ref.shape[0], grad_ref.shape[1]
    in_t_ref[...] = normed_ref[...].astype(F32).T.astype(BF)
    out_t_ref[...] = hidden_ref[...].astype(F32).T.astype(BF)
    for part, ref in ((1 - core, send_ref), (core, keep_ref)):
        at = pl.ds(pl.multiple_of(part * half, half), half)
        ref[:, pl.ds(0, wide)] = dot(in_t_ref[at, :], grad_ref[...]).astype(BF)
        ref[:, pl.ds(wide, convolved_ref.shape[1])] = dot(
            out_t_ref[at, :], convolved_ref[...]
        ).astype(BF)


def local(kernel, in_specs, outs, scratch, flops, vmem, *operands, needs=()):
    kernel = not_before(kernel, len(operands), len(needs))
    moved = sum(x.size * x.dtype.itemsize for x in (*operands, *outs))
    return pl.pallas_call(
        kernel,
        in_specs=in_specs + [ANY_SPEC] * len(needs),
        out_specs=tuple(VMEM_SPEC for _ in outs),
        out_shape=tuple(outs),
        scratch_shapes=scratch,
        compiler_params=pltpu.CompilerParams(vmem_limit_bytes=vmem * 2**20),
        cost_estimate=pl.CostEstimate(flops=flops, bytes_accessed=moved, transcendentals=0),
    )(*operands, *needs)


def conv_scratch(width, channels, rows, sums):
    return [
        pltpu.VMEM((2, width // (2 * HALF), HALF, width), BF),
        pltpu.VMEM((rows + 2 * HALO, channels), F32),
        *[pltpu.VMEM((rows + HALO, channels), F32)] * sums,
        pltpu.SemaphoreType.DMA((2,)),
    ]


def shape_of(*shape, kind=BF):
    return jax.ShapeDtypeStruct(shape, kind)


def conv_forward(core, own, other, window, gain, near, taps):
    rows, width, channels = window.shape[0] - 2 * HALO, window.shape[1], taps.shape[1]
    return local(
        conv_forward_kernel,
        [SMEM_SPEC, HBM_SPEC, HBM_SPEC] + [VMEM_SPEC] * 4,
        [
            shape_of(rows + 2 * HALO, 3 * channels, kind=F32),
            shape_of(rows, width),
            shape_of(rows, channels),
            shape_of(rows, width),
        ],
        conv_scratch(width, channels, rows, 0),
        8 * rows * width * channels, 28,
        core, own, other, window, gain, near, taps,
    )


def conv_backward(core, own, other, window, near, taps, projected, hidden, following, needs):
    rows, width, channels = hidden.shape[0], hidden.shape[1], taps.shape[1]
    return local(
        conv_backward_kernel,
        [SMEM_SPEC, HBM_SPEC, HBM_SPEC] + [VMEM_SPEC] * 6,
        [
            shape_of(rows, 3 * channels),
            shape_of(rows, width),
            shape_of(8, channels, kind=F32),
            shape_of(8, width, kind=F32),
        ],
        conv_scratch(width, channels, rows, 1),
        8 * rows * width * channels, 32,
        core, own, other, window, near, taps, projected, hidden, following, needs=needs,
    )


def conv_weights(core, normed, hidden, grad, convolved, needs):
    rows, width = hidden.shape
    out = shape_of(width // 2, width)
    return local(
        conv_weights_kernel,
        [SMEM_SPEC] + [VMEM_SPEC] * 4,
        [out, out],
        [pltpu.VMEM((width, rows), BF)] * 2,
        2**20, 24,
        core, normed, hidden, grad, convolved, needs=needs,
    )


def sum_of(parts_ref, rows):
    total = parts_ref[0, pl.ds(0, rows), :].astype(F32)
    for k in range(1, 4):
        total = total + parts_ref[k, pl.ds(0, rows), :].astype(F32)
    return total


def spread(out_ref, value):
    for k in range(4):
        out_ref[k] = value


def back_kernel(parts_ref, base_ref, value_ref, gain_ref, grad_ref, out_ref, sums_ref):
    rows = base_ref.shape[0]
    grad = sum_of(parts_ref, rows)
    value = value_ref[...].astype(F32)
    scale = lax.rsqrt(jnp.mean(value * value, axis=1, keepdims=True) + EPS)
    weighted = grad * gain_ref[pl.ds(0, 1), :]
    inner = jnp.mean(weighted * value, axis=1, keepdims=True)
    back = scale * weighted - value * (scale * scale * scale) * inner
    grad_ref[...] = base_ref[...].astype(F32) + back
    spread(out_ref, grad_ref[...].astype(BF))
    sums_ref[...] = jnp.zeros_like(sums_ref)
    if parts_ref.shape[1] == rows:
        sums_ref[pl.ds(0, 1), :] = jnp.sum(grad * value * scale, axis=0, keepdims=True)
    else:
        for k in range(4):
            sums_ref[...] += (
                parts_ref[k, pl.ds(rows, 8), :].astype(F32)
                + parts_ref[k, pl.ds(rows + 8, 8), :].astype(F32)
            )


def back(parts, base, value, gain, needs=()):
    rows, width = base.shape
    return local(
        back_kernel, [VMEM_SPEC] * 4,
        [
            shape_of(rows, width, kind=F32),
            shape_of(4, rows, width),
            shape_of(8, width, kind=F32),
        ],
        [], 2**20, 16, parts, base, value, gain, needs=needs,
    )


def arrange_kernel(place_ref, own_ref, first_ref, third_ref, second_ref, mine_ref, theirs_ref):
    lane = place_ref[0]
    rows, width = own_ref.shape[0], mine_ref.shape[1]
    for by, ref in ((0, own_ref), (1, first_ref), (3, third_ref), (2, second_ref)):
        at = lax.rem(lane + 4 - by, 4) * rows
        at = pl.ds(pl.multiple_of(at, rows), rows)
        mine_ref[at, :] = ref[:, pl.ds(0, width)]
        theirs_ref[at, :] = ref[:, pl.ds(width, width)]


def arrange(place, parts, needs):
    rows, width = parts[0].shape[0], parts[0].shape[1] // 2
    out = shape_of(4 * rows, width)
    return local(
        arrange_kernel, [SMEM_SPEC] + [VMEM_SPEC] * 4, [out, out],
        [], 2**20, 24, place, *parts, needs=needs,
    )


def last_sums_kernel(parts_ref, in_ref, out_ref, small_ref):
    rows, wide = in_ref.shape
    total = parts_ref[0].astype(F32)
    for k in range(1, parts_ref.shape[0]):
        total = total + parts_ref[k].astype(F32)
    in_ref[...] = total[:rows, :wide]
    out_ref[...] = total[:rows, wide:]
    small_ref[...] = total[rows : rows + 8] + total[rows + 8 :]


def last_sums(parts, wide, needs):
    rows, width = parts.shape[1] - 16, parts.shape[2]
    return local(
        last_sums_kernel, [VMEM_SPEC],
        [
            shape_of(rows, wide, kind=F32),
            shape_of(rows, width - wide, kind=F32),
            shape_of(8, width, kind=F32),
        ],
        [], 2**20, 16, parts, needs=needs,
    )


def per_device(
    tokens,
    cotangent,
    segment_ids,
    mixer_gain,
    ffn_gain,
    gate_master,
    up_master,
    down_master,
    conv_in,
    conv_kernel,
    conv_out,
    query_master,
    key_master,
    value_master,
    query_gain,
    key_gain,
    output_master,
):
    core = lax.axis_index("pipe")
    lane = lax.axis_index("tensor")
    at_dp = lax.axis_index("dp_0") * 4 + lax.axis_index("dp_1")
    seq_len, width = tokens.shape
    rows = seq_len // 2
    shard = rows // 4
    channels = conv_kernel.shape[1]
    head_dim = query_gain.shape[0]
    hidden_width = gate_master.shape[2]
    dp_rows = gate_master.shape[1]
    mix_rows = conv_in.shape[0]
    attn_cols = 3 * channels
    segments = segment_ids[0]

    core_at = core.astype(jnp.int32).reshape(1)
    dense_shard = jnp.stack([gate_master[0], up_master[0], down_master[0].T]).astype(BF)
    dense_shard = dense_shard.reshape(3, 2, HALF, hidden_width)
    keep = lax.dynamic_index_in_dim(dense_shard, core, 1, False).reshape(3 * HALF, hidden_width)
    send = lax.dynamic_index_in_dim(dense_shard, 1 - core, 1, False).reshape(3 * HALF, hidden_width)
    got = other_core(send)
    attn_shard = jnp.concatenate([query_master, key_master, value_master, output_master.T], axis=1)
    attn_shard = jnp.pad(attn_shard.astype(BF), ((0, 0), (0, hidden_width - attn_cols)))
    own0 = jnp.concatenate([jnp.where(core == 0, keep, got), attn_shard], axis=0)
    own0 = lax.all_gather(own0, DP, axis=0, tiled=False)
    own1 = lax.all_gather(jnp.where(core == 0, got, keep), DP, axis=0, tiled=False)

    conv_shard = jnp.concatenate(
        [conv_in.reshape(mix_rows, 3 * channels), conv_out.T], axis=1
    ).astype(BF)
    gains = jnp.concatenate([mixer_gain, ffn_gain], 1).astype(BF)
    conv_shard = jnp.concatenate(
        [conv_shard, jnp.pad(gains, ((0, 7), (0, width - 2 * dp_rows)))], axis=0
    )
    conv_half = exchange(jnp.broadcast_to(conv_shard[None], (16, *conv_shard.shape)), DP)
    conv_other = other_core(conv_half)

    def gains_of(half):
        return half[:, mix_rows, : 2 * dp_rows].reshape(16, 2, dp_rows).swapaxes(0, 1).reshape(2, width)

    gains = in_core_order(core, gains_of(conv_half), gains_of(conv_other)).astype(F32)
    gain_mix, gain_ffn = (gains[0], gains[2]), (gains[1], gains[3])

    start = core * rows
    shard_start = start + lane * shard

    def shard_of(value):
        return lax.dynamic_slice_in_dim(value, shard_start, shard, 0).astype(F32)

    own_segments = lax.dynamic_slice_in_dim(segments, start, rows, 0)
    near = jnp.concatenate(
        [jnp.full((HALO,), -1, jnp.int32), segments, jnp.full((HALO,), -2, jnp.int32)]
    )
    near = lax.dynamic_slice_in_dim(near, start, rows + 2 * HALO, 0)

    near = jnp.broadcast_to(near[:, None], (rows + 2 * HALO, channels))
    taps_in = jnp.pad(conv_kernel, ((0, 5), (0, 0)))

    padded = jnp.pad(tokens, ((HALO, HALO), (0, 0)))
    window = lax.dynamic_slice_in_dim(padded, start, rows + 2 * HALO, 0)
    gain_rows = jnp.broadcast_to(gain_mix[0][None], (8, width))
    projected, normed0, convolved, partial = conv_forward(
        core_at, conv_half, conv_other, window, gain_rows, near, taps_in
    )
    hidden0 = shard_of(tokens) + scatter_sum(partial, "tensor")
    ffn_in0, scale_ffn0 = rms_forward(hidden0, gain_ffn[0])
    ffn_in0 = ffn_in0.astype(BF)
    own0 = after(own0, hidden0)
    other0 = other_core(own0)
    ffn_in0 = gather(ffn_in0, "tensor")
    acts0, partial = feed_forward(core_at, ffn_in0, own0, other0)
    attn_whole = in_core_order(
        core,
        own0[:, 3 * HALF :, :attn_cols].reshape(width // 2, attn_cols),
        other0[:, 3 * HALF :, :attn_cols].reshape(width // 2, attn_cols),
    )
    qkv_w, output_t = attn_whole[:, : 2 * channels], attn_whole[:, 2 * channels :]
    passed_shard = (hidden0 + scatter_sum(partial, "tensor")).astype(BF)
    passed = gather(passed_shard, "tensor")

    cosine, sine = rotation(positions_of(segments), head_dim)
    cosine = lax.dynamic_slice_in_dim(cosine, start, rows, 0)
    sine = lax.dynamic_slice_in_dim(sine, start, rows, 0)
    head_gains = jnp.stack([jnp.tile(query_gain, 2), jnp.tile(key_gain, 2)])
    head_gains = jnp.pad(head_gains, ((0, 6), (0, 0)))
    before = jnp.where(core == 0, -1, segments[:rows])
    key_column = jnp.broadcast_to(
        jnp.concatenate([before, own_segments])[:, None], (2 * rows, 128)
    )
    query_row = jnp.broadcast_to(own_segments[None, :], (8, rows))

    normed1, scale_mix1 = rms_forward(passed.astype(F32), gain_mix[1])
    normed1 = normed1.astype(BF)
    raw = dot(normed1, qkv_w)
    (low,) = whole(
        rope_forward_kernel,
        [jax.ShapeDtypeStruct((rows, 512), BF)],
        raw,
        cosine,
        sine,
        head_gains,
        vmem=16,
    )
    before_kv = lax.ppermute(low[:, 256:], "pipe", [(0, 1)])
    attended, logs = whole(
        attend_forward_kernel,
        [jax.ShapeDtypeStruct((rows, 256), BF), jax.ShapeDtypeStruct((8, rows), F32)],
        low,
        before_kv,
        key_column,
        query_row,
        scratch=[pltpu.VMEM((2 * rows, 256), BF)],
        flops=4 * 4 * rows * SPAN * 64,
        vmem=32,
    )
    partial = dot_cols(attended, output_t).astype(BF)
    hidden1 = passed_shard.astype(F32) + scatter_sum(partial, "tensor")
    ffn_in1, scale_ffn1 = rms_forward(hidden1, gain_ffn[1])
    ffn_in1 = ffn_in1.astype(BF)
    own1 = after(own1, hidden1)
    other1 = other_core(own1)
    ffn_in1 = gather(ffn_in1, "tensor")
    grad_low = lax.dynamic_slice_in_dim(cotangent, start, rows, 0)
    parts1, second, partial = feed_both(core_at, ffn_in1, grad_low, own1, other1)
    def gain_sum(value, scale, grad):
        return jnp.sum(grad * value * scale, axis=0)

    sum1, done = feed_weights(ffn_in1, grad_low, parts1)
    gain_rows = jnp.broadcast_to(gain_ffn[1][None], (8, width))
    grad_hidden, copies, ffn_gain1 = back(
        blocks_of(partial), shard_of(cotangent), hidden1, gain_rows, (done,)
    )
    ffn_gain1 = ffn_gain1[0]
    sum1 = after(sum1.reshape(-1, hidden_width), grad_hidden)
    sum1 = lax.psum_scatter(sum1, DP, scatter_dimension=0, tiled=True)
    hidden_low = gathered(copies)
    grad_output_t = dot_rows(hidden_low, attended).astype(BF)
    grad_attended = dot(hidden_low, output_t).astype(BF)
    grad_query, grad_kv = whole(
        attend_backward_kernel,
        [jax.ShapeDtypeStruct((rows, 256), F32), jax.ShapeDtypeStruct((2 * rows, 256), F32)],
        low,
        before_kv,
        key_column,
        query_row,
        logs,
        grad_attended,
        scratch=[pltpu.VMEM((2 * rows, 256), BF)],
        flops=10 * 4 * rows * SPAN * 64,
        vmem=40,
    )
    more_kv = lax.ppermute(grad_kv[:rows], "pipe", [(1, 0)])
    grad_qkv, head_sums = whole(
        rope_backward_kernel,
        [jax.ShapeDtypeStruct((rows, 512), BF), jax.ShapeDtypeStruct((8, 128), F32)],
        raw,
        grad_query,
        grad_kv[rows:],
        more_kv,
        cosine,
        sine,
        head_gains,
        vmem=20,
    )
    partial = dot_cols(grad_qkv, qkv_w)
    grad_attn = jnp.concatenate([dot_rows(normed1, grad_qkv).astype(BF), grad_output_t], axis=1)
    gain_rows = jnp.broadcast_to(gain_mix[1][None], (8, width))
    grad_hidden, copies, mix_gain1 = back(
        blocks_of(partial.astype(BF)), grad_hidden, passed_shard, gain_rows, (grad_attn,)
    )
    mix_gain1 = mix_gain1[0]
    grad_shard = copies[0]
    grad_low = gathered(copies)
    grad_passed = grad_low

    parts0, partial = feed_backward(
        core_at, grad_low, own0, other0, acts0
    )
    early = other_core(jnp.where(core == 0, grad_passed, passed))

    sum0, done = feed_weights(ffn_in0, grad_low, parts0, (grad_attn,), (sum1,))
    gain_rows = jnp.broadcast_to(gain_ffn[0][None], (8, width))
    grad_hidden, copies, ffn_gain0 = back(
        blocks_of(partial), grad_shard, hidden0, gain_rows, (done,)
    )
    ffn_gain0 = ffn_gain0[0]
    hidden_low = gathered(copies)

    sum0 = after(sum0.reshape(-1, hidden_width), grad_hidden)
    sum0 = lax.psum_scatter(sum0, DP, scatter_dimension=0, tiled=True)
    dense0 = sum0[: 3 * dp_rows]
    theirs = other_core(jnp.where(core == 0, sum1, dense0)).astype(F32)
    dense = jnp.where(core == 0, dense0, sum1).astype(F32) + theirs
    grad_gate, grad_up, grad_down = (dense[k * dp_rows : (k + 1) * dp_rows] for k in range(3))
    attn_both = sum0[3 * dp_rows :, :attn_cols]
    grad_attn = half_of(attn_both, core).astype(F32) + other_core(half_of(attn_both, 1 - core))

    following = lax.ppermute(hidden_low[:HALO], "pipe", [(1, 0)])
    grad_projected, partial, taps, mix_gain0 = conv_backward(
        core_at, conv_half, conv_other, window, near, taps_in, projected, hidden_low, following,
        needs=(),
    )
    taps, mix_gain0 = taps[:3], mix_gain0[0]

    taps_wide = lax.dynamic_update_slice_in_dim(
        jnp.zeros((3, width), F32), taps, lane * channels, 1
    )
    heads = (head_sums[:2, :64] + head_sums[:2, 64:]).reshape(1, 128)
    small = jnp.concatenate(
        [
            jnp.stack([mix_gain0, ffn_gain0, mix_gain1, ffn_gain1]),
            taps_wide,
            jnp.pad(heads, ((0, 0), (0, width - 128))),
        ],
        0,
    )

    def two_terms(value):
        high = value.astype(BF)
        return jnp.concatenate([high, (value - high.astype(F32)).astype(BF)], 0)

    def one_term(value):
        return value[:8] + value[8:]

    def sum_beside(blocks, small, axis):
        terms = jnp.broadcast_to(two_terms(small)[None], (blocks.shape[0], 16, width))
        parts = exchange(jnp.concatenate([blocks.astype(BF), terms], 1), axis)
        summed = jnp.sum(parts.astype(F32), axis=0)
        return summed[:-16], one_term(summed[-16:])

    terms = jnp.broadcast_to(two_terms(small)[None], (4, 16, width))
    parts = [x.reshape(4, shard, width) for x in (partial, second)]
    parts = exchange(jnp.concatenate([*parts, terms], 1), "tensor")
    parts = jnp.sum(parts.astype(F32), axis=0)
    grad_normed = parts[:shard]
    second = (hidden1 + parts[shard : 2 * shard]).astype(BF)
    small = one_term(parts[2 * shard :])
    tokens_shard = shard_of(tokens)
    scale_shard = rms_forward(tokens_shard, gain_mix[0])[1]
    grad_tokens = grad_hidden + rms_backward(tokens_shard, scale_shard, gain_mix[0], grad_normed)
    grad_tokens = grad_tokens.astype(BF)
    late = [
        jnp.where(core == 0, grad_tokens, second),
        other_core(jnp.where(core == 0, second, grad_tokens)),
    ]
    late = jnp.concatenate(late, axis=1)
    small = small + one_term(other_core(two_terms(small)).astype(F32))

    keep, send = conv_weights(
        core_at, normed0, hidden_low, grad_projected, convolved, ()
    )
    blocks = keep.astype(F32) + other_core(send)
    terms = jnp.broadcast_to(two_terms(small)[None], (16, 16, width))
    blocks = jnp.concatenate([blocks.astype(BF).reshape(16, mix_rows, width), terms], 1)
    grad_in, grad_out, small = last_sums(
        exchange(blocks, DP), 3 * channels, ()
    )

    parts = [late, *(turned(late, "tensor", by) for by in (1, 3, 2))]
    mine, theirs = arrange(lane.astype(jnp.int32).reshape(1), parts, (small,))
    section_output = jnp.where(
        core == 0, jnp.concatenate([passed, early], 0), jnp.concatenate([theirs, mine], 0)
    )
    input_grad = jnp.where(
        core == 0, jnp.concatenate([mine, theirs], 0), jnp.concatenate([early, grad_passed], 0)
    ).astype(F32)

    def own_gain(pair):
        return lax.dynamic_slice(pair, (core, at_dp * dp_rows), (1, dp_rows))

    return (
        section_output[None],
        input_grad[None],
        own_gain(small[0:4:2]),
        own_gain(small[1:4:2]),
        grad_gate[None],
        grad_up[None],
        grad_down.T[None],
        grad_in.reshape(mix_rows, 3, channels),
        small[4:7],
        grad_out.T,
        grad_attn[:, :channels],
        grad_attn[:, channels : channels + 128],
        grad_attn[:, channels + 128 : 2 * channels],
        small[7, :64],
        small[7, 64:128],
        grad_attn[:, 2 * channels :].T,
    )


def solution(mesh):
    finer = Mesh(
        mesh.devices.reshape(mesh.shape["pipe"], mesh.shape["tensor"], 4, 4),
        ("pipe", "tensor", "dp_0", "dp_1"),
    )
    return jax.shard_map(
        per_device,
        mesh=finer,
        in_specs=(
            P(DP, None),
            P(DP, None),
            P(DP, None),
            P("pipe", DP),
            P("pipe", DP),
            P("pipe", DP, "tensor"),
            P("pipe", DP, "tensor"),
            P("pipe", "tensor", DP),
            P(PIPE_DP, None, "tensor"),
            P(None, "tensor"),
            P("tensor", PIPE_DP),
            P(PIPE_DP, "tensor"),
            P(PIPE_DP, "tensor"),
            P(PIPE_DP, "tensor"),
            P(),
            P(),
            P("tensor", PIPE_DP),
        ),
        out_specs=(
            P("pipe", DP, None),
            P("pipe", DP, None),
            P("pipe", DP),
            P("pipe", DP),
            P("pipe", DP, "tensor"),
            P("pipe", DP, "tensor"),
            P("pipe", "tensor", DP),
            P(PIPE_DP, None, "tensor"),
            P(),
            P("tensor", PIPE_DP),
            P(PIPE_DP, "tensor"),
            P(PIPE_DP, "tensor"),
            P(PIPE_DP, "tensor"),
            P(),
            P(),
            P("tensor", PIPE_DP),
        ),
        check_vma=False,
    )
```

```python
import functools

import jax
import jax.numpy as jnp
from jax import lax
from jax.experimental import pallas as pl
from jax.experimental.pallas import tpu as pltpu
from jax.sharding import Mesh
from jax.sharding import PartitionSpec as P

DP = ("dp_0", "dp_1")
PIPE_DP = ("pipe", "dp_0", "dp_1")
EPS = 1e-05
THETA = 1000000.0
NEGATIVE = -1e30
HALO = 16
BF = jnp.bfloat16
F32 = jnp.float32


def dot(left, right, dims=((1,), (0,))):
    return lax.dot_general(left, right, (dims, ((), ())), preferred_element_type=F32)


def dot_cols(left, right):
    return dot(left, right, ((1,), (1,)))


def dot_rows(left, right):
    return dot(left, right, ((0,), (0,)))


def exchange(parts, axis):
    return lax.all_to_all(parts, axis, 0, 0)


def blocks_of(value):
    return exchange(value.reshape(4, value.shape[0] // 4, value.shape[1]), "tensor")


def gathered(copies):
    return exchange(copies, "tensor").reshape(-1, copies.shape[-1])


def scatter_sum(value, axis):
    size = lax.axis_size(axis)
    parts = value.reshape(size, value.shape[0] // size, *value.shape[1:])
    return jnp.sum(exchange(parts, axis).astype(F32), axis=0)


def gather(value, axis):
    size = lax.axis_size(axis)
    parts = exchange(jnp.broadcast_to(value[None], (size, *value.shape)), axis)
    return parts.reshape(size * value.shape[0], *value.shape[1:])


def turned(value, axis, by):
    size = lax.axis_size(axis)
    return lax.ppermute(value, axis, [(i, (i + by) % size) for i in range(size)])


def direct_scatter_sum(value, axis):
    me = lax.axis_index(axis)
    rows = value.shape[0] // 4

    def block(by):
        return lax.dynamic_slice_in_dim(value, lax.rem(me + by, 4) * rows, rows, 0)

    total = block(0).astype(F32)
    for by in (1, 3, 2):
        total = total + turned(block(by), axis, by).astype(F32)
    return total


def direct_gather(value, axis):
    me = lax.axis_index(axis)
    whole = jnp.zeros((4, *value.shape), value.dtype)
    for by in (0, 1, 3, 2):
        part = turned(value, axis, by) if by else value
        whole = lax.dynamic_update_slice_in_dim(whole, part[None], lax.rem(me + 4 - by, 4), 0)
    return whole.reshape(4 * value.shape[0], *value.shape[1:])


def after(value, *others):
    return lax.optimization_barrier((value, *others))[0]


def other_core(value):
    return lax.ppermute(value, "pipe", [(0, 1), (1, 0)])


def in_core_order(core, own, other):
    return jnp.where(
        core == 0, jnp.concatenate([own, other], 0), jnp.concatenate([other, own], 0)
    )


def half_of(value, core):
    rows = value.shape[0] // 2
    return lax.dynamic_slice_in_dim(value, core * rows, rows, 0)


def rms_forward(value, gain):
    scale = lax.rsqrt(jnp.mean(value * value, axis=-1, keepdims=True) + EPS)
    return value * scale * gain, scale


def rms_backward(value, scale, gain, grad):
    weighted = grad * gain
    inner = jnp.mean(weighted * value, axis=-1, keepdims=True)
    return scale * weighted - value * (scale * scale * scale) * inner


def positions_of(segments):
    first = jnp.sum((segments[None, :] < segments[:, None]).astype(jnp.int32), axis=1)
    return jnp.arange(segments.shape[0], dtype=jnp.int32) - first


def rotation(positions, head_dim):
    half = head_dim // 2
    frequency = THETA ** (-2.0 * jnp.arange(half, dtype=F32) / head_dim)
    angle = positions.astype(F32)[:, None] * frequency[None, :]
    cosine, sine = jnp.cos(angle), jnp.sin(angle)
    return jnp.tile(cosine, (1, 4)), jnp.tile(jnp.concatenate([-sine, sine], 1), (1, 2))


def not_before(kernel, operands, needed):
    skipped = range(operands, operands + needed)

    def body(*refs):
        kernel(*(ref for k, ref in enumerate(refs) if k not in skipped))

    return body


def whole(kernel, out_shapes, *operands, scratch=(), flops=0, vmem=40, needs=()):
    kernel = not_before(kernel, len(operands), len(needs))
    spec = pl.BlockSpec(memory_space=pltpu.VMEM)
    moved = sum(x.size * x.dtype.itemsize for x in (*operands, *out_shapes))
    return pl.pallas_call(
        kernel,
        out_shape=tuple(out_shapes),
        in_specs=[spec] * len(operands) + [pl.BlockSpec(memory_space=pl.ANY)] * len(needs),
        out_specs=tuple(spec for _ in out_shapes),
        scratch_shapes=scratch,
        compiler_params=pltpu.CompilerParams(vmem_limit_bytes=vmem * 2**20),
        cost_estimate=pl.CostEstimate(flops=flops, bytes_accessed=moved, transcendentals=0),
    )(*operands, *needs)


def head_mean(value, low):
    first = jnp.sum(jnp.where(low, value, 0.0), axis=1, keepdims=True)
    second = jnp.sum(jnp.where(low, 0.0, value), axis=1, keepdims=True)
    return jnp.where(low, first, second) * (1.0 / 64.0)


def partner(value, first_half):
    return jnp.where(first_half, pltpu.roll(value, 96, 1), pltpu.roll(value, 32, 1))


def lanes_of(rows):
    lane = lax.broadcasted_iota(jnp.int32, (rows, 128), 1)
    return lane < 64, (lane & 63) < 32


CHUNK = 128


def rope_forward_kernel(raw_ref, cosine_ref, sine_ref, gain_ref, out_ref):
    rows = raw_ref.shape[0]
    low, first_half = lanes_of(CHUNK)

    @pl.loop(0, rows // CHUNK)
    def _(step):
        at = pl.ds(pl.multiple_of(step * CHUNK, CHUNK), CHUNK)
        cosine, sine = cosine_ref[at, :], sine_ref[at, :]
        for tile in range(3):
            cols = pl.ds(tile * 128, 128)
            value = raw_ref[at, cols]
            gain = gain_ref[pl.ds(tile // 2, 1), :]
            normed = value * lax.rsqrt(head_mean(value * value, low) + EPS) * gain
            turned = normed * cosine + partner(normed, first_half) * sine
            out_ref[at, cols] = turned.astype(BF)
        out_ref[at, pl.ds(384, 128)] = raw_ref[at, pl.ds(384, 128)].astype(BF)


def rope_backward_kernel(
    raw_ref, grad_query_ref, grad_kv_ref, more_kv_ref, cosine_ref, sine_ref, gain_ref, out_ref, sums_ref
):
    rows = raw_ref.shape[0]
    low, first_half = lanes_of(CHUNK)
    sums_ref[...] = jnp.zeros_like(sums_ref)

    @pl.loop(0, rows // CHUNK)
    def _(step):
        at = pl.ds(pl.multiple_of(step * CHUNK, CHUNK), CHUNK)
        cosine, sine = cosine_ref[at, :], sine_ref[at, :]
        for tile in range(3):
            cols = pl.ds(tile * 128, 128)
            if tile < 2:
                grad = grad_query_ref[at, cols]
            else:
                grad = grad_kv_ref[at, pl.ds(0, 128)] + more_kv_ref[at, pl.ds(0, 128)]
            grad = grad * cosine - partner(grad, first_half) * sine
            value = raw_ref[at, cols]
            gain = gain_ref[pl.ds(tile // 2, 1), :]
            scale = lax.rsqrt(head_mean(value * value, low) + EPS)
            weighted = grad * gain
            inner = head_mean(weighted * value, low)
            back = scale * weighted - value * (scale * scale * scale) * inner
            out_ref[at, cols] = back.astype(BF)
            sums_ref[pl.ds(tile // 2, 1), :] += jnp.sum(grad * value * scale, axis=0, keepdims=True)
        out_ref[at, pl.ds(384, 128)] = (
            grad_kv_ref[at, pl.ds(128, 128)] + more_kv_ref[at, pl.ds(128, 128)]
        ).astype(BF)


def fill_window(own_ref, before_ref, keys_ref):
    rows = own_ref.shape[0]
    keys_ref[pl.ds(0, rows), :] = before_ref[...]
    keys_ref[pl.ds(rows, rows), :] = own_ref[:, pl.ds(256, 256)]


def bias_of(column_ref, row_ref, start, block, span):
    keys = column_ref[pl.ds(start, span), pl.ds(0, 1)]
    queries = row_ref[pl.ds(0, 1), pl.ds(start, block)]
    key_at = lax.broadcasted_iota(jnp.int32, (span, block), 0)
    query_at = lax.broadcasted_iota(jnp.int32, (span, block), 1) + (span - block)
    return jnp.where((key_at <= query_at) & (keys == queries), 0.0, NEGATIVE)


BLOCK = 256
SPAN = 768


def attend_forward_kernel(own_ref, before_ref, column_ref, row_ref, out_ref, log_ref, keys_ref):
    rows = own_ref.shape[0]
    fill_window(own_ref, before_ref, keys_ref)
    log_ref[...] = jnp.zeros_like(log_ref)
    for sub in range(rows // BLOCK):
        start = sub * BLOCK
        bias = bias_of(column_ref, row_ref, start, BLOCK, SPAN)
        values = keys_ref[pl.ds(start, SPAN), pl.ds(128, 128)].astype(F32).T.astype(BF)
        parts = []
        for head in range(4):
            kv = head // 2
            key = keys_ref[pl.ds(start, SPAN), pl.ds(kv * 64, 64)]
            query = own_ref[pl.ds(start, BLOCK), pl.ds(head * 64, 64)] * jnp.asarray(0.125, BF)
            scores = dot_cols(key, query) + bias
            top = jnp.max(scores, axis=0, keepdims=True)
            weights = jnp.exp(scores - top)
            total = jnp.sum(weights, axis=0, keepdims=True)
            probs = (weights * (1.0 / total)).astype(BF)
            parts.append(dot(values[kv * 64 : kv * 64 + 64], probs))
            log_ref[pl.ds(head, 1), pl.ds(start, BLOCK)] = top + jnp.log(total)
        out_ref[pl.ds(start, BLOCK), :] = jnp.concatenate(parts, 0).T.astype(BF)


def attend_backward_kernel(
    own_ref, before_ref, column_ref, row_ref, log_ref, grad_ref, query_ref, kv_ref, keys_ref
):
    rows = own_ref.shape[0]
    fill_window(own_ref, before_ref, keys_ref)
    kv_ref[...] = jnp.zeros_like(kv_ref)
    for sub in range(rows // BLOCK):
        start = sub * BLOCK
        window = pl.ds(start, SPAN)
        bias = bias_of(column_ref, row_ref, start, BLOCK, SPAN)
        keys = keys_ref[window, pl.ds(0, 128)].astype(F32).T.astype(BF)
        parts = []
        for kv in range(2):
            key = keys_ref[window, pl.ds(kv * 64, 64)]
            value = keys_ref[window, pl.ds(128 + kv * 64, 64)]
            grad_key = jnp.zeros((SPAN, 64), F32)
            grad_value = jnp.zeros((SPAN, 64), F32)
            for head in (2 * kv, 2 * kv + 1):
                query = own_ref[pl.ds(start, BLOCK), pl.ds(head * 64, 64)] * jnp.asarray(0.125, BF)
                grad = grad_ref[pl.ds(start, BLOCK), pl.ds(head * 64, 64)]
                log = log_ref[pl.ds(head, 1), pl.ds(start, BLOCK)]
                probs = jnp.exp(dot_cols(key, query) + bias - log)
                grad_probs = dot_cols(value, grad)
                shared = jnp.sum(probs * grad_probs, axis=0, keepdims=True)
                grad_scores = (probs * (grad_probs - shared)).astype(BF)
                grad_key += dot(grad_scores, query)
                grad_value += dot(probs.astype(BF), grad)
                parts.append(dot(keys[kv * 64 : kv * 64 + 64], grad_scores) * 0.125)
            kv_ref[window, pl.ds(kv * 64, 64)] += grad_key
            kv_ref[window, pl.ds(128 + kv * 64, 64)] += grad_value
        query_ref[pl.ds(start, BLOCK), :] = jnp.concatenate(parts, 0).T


HALF = 32
GATE, UP, DOWN = range(3)


def fetch_weights(core_ref, own_ref, other_ref, weights_ref, sems, order):
    core = core_ref[0]

    def copies(k):
        return [
            pltpu.make_async_copy(
                ref.at[:, pl.ds(HALF * k, HALF), :], weights_ref.at[k, :, part], sems.at[k, side]
            )
            for side, (ref, part) in enumerate(((own_ref, core), (other_ref, 1 - core)))
        ]

    for k in order:
        for copy in copies(k):
            copy.start()

    def matrix(k):
        for copy in copies(k):
            copy.wait()
        return lambda: weights_ref[k].reshape(-1, weights_ref.shape[-1])

    return matrix


def gates_back(grad_inner, gate, up):
    sigma = 1.0 / (1.0 + jnp.exp(-gate))
    silu = gate * sigma
    grad_gate = grad_inner * up * (sigma * (1.0 + gate * (1.0 - sigma)))
    return grad_gate.astype(BF), (grad_inner * silu).astype(BF), (silu * up).astype(BF)


def silu(gate):
    return gate * (1.0 / (1.0 + jnp.exp(-gate)))


class Moved:
    def __init__(self, source, target, sem):
        self.copy = pltpu.make_async_copy(source, target, sem)

    def start(self):
        self.copy.start()
        return self

    def wait(self):
        self.copy.wait()


def feed_forward_kernel(
    core_ref, in_ref, own_ref, other_ref, acts_ref, out_ref, held_ref, weights_ref, sems, out_sems
):
    matrix = fetch_weights(core_ref, own_ref, other_ref, weights_ref, sems, (GATE, UP, DOWN))
    held_ref[0] = dot(in_ref[...], matrix(GATE)())
    first = Moved(held_ref.at[0], acts_ref.at[0], out_sems.at[0]).start()
    held_ref[1] = dot(in_ref[...], matrix(UP)())
    second = Moved(held_ref.at[1], acts_ref.at[1], out_sems.at[1]).start()
    inner = (silu(held_ref[0]) * held_ref[1]).astype(BF)
    out_ref[...] = dot_cols(inner, matrix(DOWN)()).astype(BF)
    first.wait()
    second.wait()


def send_parts(parts_ref, held_ref, sems):
    return [Moved(held_ref.at[k], parts_ref.at[k], sems.at[k]).start() for k in range(3)]


def feed_backward_kernel(
    core_ref, grad_ref, own_ref, other_ref, acts_ref, parts_ref, out_ref,
    acts_held_ref, held_ref, weights_ref, sems, in_sems, out_sems,
):
    matrix = fetch_weights(core_ref, own_ref, other_ref, weights_ref, sems, (DOWN,))
    acts = [Moved(acts_ref.at[k], acts_held_ref.at[k], in_sems.at[k]).start() for k in range(2)]
    more = fetch_weights(core_ref, own_ref, other_ref, weights_ref, sems, (GATE, UP))
    grad_inner = dot(grad_ref[...], matrix(DOWN)())
    acts[0].wait()
    acts[1].wait()
    grad_gate, grad_up, inner = gates_back(grad_inner, acts_held_ref[0], acts_held_ref[1])
    held_ref[0] = grad_gate
    held_ref[1] = grad_up
    held_ref[2] = inner
    sent = send_parts(parts_ref, held_ref, out_sems)
    out = dot_cols(held_ref[0], more(GATE)())
    out_ref[...] = (out + dot_cols(held_ref[1], more(UP)())).astype(BF)
    for copy in sent:
        copy.wait()


def feed_both_kernel(
    core_ref, in_ref, grad_ref, own_ref, other_ref, parts_ref, out_ref,
    held_ref, weights_ref, sems, out_sems,
):
    matrix = fetch_weights(core_ref, own_ref, other_ref, weights_ref, sems, (DOWN, GATE, UP))
    down = matrix(DOWN)
    grad_inner = dot(grad_ref[...], down())
    gate_w = matrix(GATE)
    gate = dot(in_ref[...], gate_w())
    up_w = matrix(UP)
    up = dot(in_ref[...], up_w())
    grad_gate, grad_up, inner = gates_back(grad_inner, gate, up)
    held_ref[0] = grad_gate
    held_ref[1] = grad_up
    held_ref[2] = inner
    sent = send_parts(parts_ref, held_ref, out_sems)
    out = dot_cols(held_ref[0], gate_w())
    out_ref[...] = (out + dot_cols(held_ref[1], up_w())).astype(BF)
    for copy in sent:
        copy.wait()


def feed_weights_kernel(in_ref, grad_ref, part_ref, *refs):
    more_ref = refs[0] if len(refs) == 5 else None
    out_ref, done_ref, in_t_ref, grad_t_ref = refs[-4:]
    step = pl.program_id(0)
    done_ref[...] = jnp.zeros_like(done_ref)

    @pl.when(step == 0)
    def _():
        in_t_ref[...] = in_ref[...].astype(F32).T.astype(BF)
        grad_t_ref[...] = grad_ref[...].astype(F32).T.astype(BF)

    @pl.when(step < 2)
    def _():
        out_ref[...] = dot(in_t_ref[...], part_ref[0]).astype(BF).reshape(out_ref.shape)

    @pl.when(step == 2)
    def _():
        out_ref[...] = dot(grad_t_ref[...], part_ref[0]).astype(BF).reshape(out_ref.shape)

    if more_ref is not None:

        @pl.when(step == 3)
        def _():
            out_ref[...] = jnp.zeros_like(out_ref)
            wide = more_ref.shape[1]
            blocks = out_ref.shape[0]
            for part in range(2):
                rows = more_ref[pl.ds(part * blocks * HALF, blocks * HALF), :]
                out_ref[:, pl.ds(part * HALF, HALF), pl.ds(0, wide)] = rows.reshape(blocks, HALF, wide)


SMEM_SPEC = pl.BlockSpec(memory_space=pltpu.SMEM)
HBM_SPEC = pl.BlockSpec(memory_space=pltpu.HBM)
ANY_SPEC = pl.BlockSpec(memory_space=pl.ANY)
VMEM_SPEC = pl.BlockSpec(memory_space=pltpu.VMEM)


def feed(kernel, in_specs, outs, scratch, hidden, width, flops, vmem, *operands, needs=()):
    kernel = not_before(kernel, len(operands), len(needs))
    moved = sum(x.size * x.dtype.itemsize for x in (*operands, *outs))
    return pl.pallas_call(
        kernel,
        in_specs=in_specs + [ANY_SPEC] * len(needs),
        out_specs=(HBM_SPEC, *[VMEM_SPEC] * (len(outs) - 1)),
        out_shape=tuple(outs),
        scratch_shapes=[
            *scratch,
            pltpu.VMEM((3, width // (2 * HALF), 2, HALF, hidden), BF),
            pltpu.SemaphoreType.DMA((3, 2)),
            *[pltpu.SemaphoreType.DMA((3,))] * len(scratch),
        ],
        compiler_params=pltpu.CompilerParams(vmem_limit_bytes=vmem * 2**20),
        cost_estimate=pl.CostEstimate(flops=flops, bytes_accessed=moved, transcendentals=0),
    )(*operands, *needs)


def feed_forward(core, ffn_in, own, other):
    rows, width = ffn_in.shape
    hidden = own.shape[-1]
    return feed(
        feed_forward_kernel,
        [SMEM_SPEC, VMEM_SPEC, HBM_SPEC, HBM_SPEC],
        [jax.ShapeDtypeStruct((2, rows, hidden), F32), jax.ShapeDtypeStruct(ffn_in.shape, BF)],
        [pltpu.VMEM((2, rows, hidden), F32)],
        hidden, width, 6 * rows * width * hidden, FEED_VMEM,
        core, ffn_in, own, other,
    )


def feed_backward(core, grad_low, own, other, acts, needs=()):
    rows, width = grad_low.shape
    hidden = own.shape[-1]
    return feed(
        feed_backward_kernel,
        [SMEM_SPEC, VMEM_SPEC, HBM_SPEC, HBM_SPEC, HBM_SPEC],
        [jax.ShapeDtypeStruct((3, rows, hidden), BF), jax.ShapeDtypeStruct(grad_low.shape, BF)],
        [pltpu.VMEM((2, rows, hidden), F32), pltpu.VMEM((3, rows, hidden), BF)],
        hidden, width, 6 * rows * width * hidden, FEED_VMEM,
        core, grad_low, own, other, acts, needs=needs,
    )


def feed_both(core, ffn_in, grad_low, own, other):
    rows, width = grad_low.shape
    hidden = own.shape[-1]
    out = jax.ShapeDtypeStruct(grad_low.shape, BF)
    return feed(
        feed_both_kernel,
        [SMEM_SPEC, VMEM_SPEC, VMEM_SPEC, HBM_SPEC, HBM_SPEC],
        [jax.ShapeDtypeStruct((3, rows, hidden), BF), out],
        [pltpu.VMEM((3, rows, hidden), BF)],
        hidden, width, 10 * rows * width * hidden, FEED_VMEM,
        core, ffn_in, grad_low, own, other,
    )


FEED_VMEM = 58


def feed_weights(ffn_in, grad_low, parts, more=(), needs=()):
    rows, width = ffn_in.shape
    hidden = parts.shape[-1]
    blocks, steps = width // (2 * HALF), 3 + len(more)
    return pl.pallas_call(
        not_before(feed_weights_kernel, steps, len(needs)),
        grid=(steps,),
        in_specs=[
            VMEM_SPEC,
            VMEM_SPEC,
            pl.BlockSpec((1, rows, hidden), lambda k: (jnp.minimum(k, 2), 0, 0)),
            *[VMEM_SPEC] * len(more),
            *[ANY_SPEC] * len(needs),
        ],
        out_specs=(
            pl.BlockSpec((blocks, 2 * HALF, hidden), lambda k: (0, k, 0)),
            pl.BlockSpec((8, 128), lambda k: (0, 0)),
        ),
        out_shape=(
            shape_of(blocks, 2 * HALF * steps, hidden),
            shape_of(8, 128, kind=F32),
        ),
        scratch_shapes=[pltpu.VMEM((width, rows), BF), pltpu.VMEM((width, rows), BF)],
        compiler_params=pltpu.CompilerParams(
            dimension_semantics=("arbitrary",), vmem_limit_bytes=FEED_VMEM * 2**20
        ),
        cost_estimate=pl.CostEstimate(flops=2**20, bytes_accessed=2**20, transcendentals=0),
    )(ffn_in, grad_low, parts, *more, *needs)


def fetch_conv(core_ref, own_ref, other_ref, weights_ref, sems):
    core = core_ref[0]
    rows = pl.ds(0, HALF)
    return [
        Moved(ref.at[:, rows, :], weights_ref.at[part], sems.at[side]).start()
        for side, (ref, part) in enumerate(((own_ref, core), (other_ref, 1 - core)))
    ]


def conv_total(product_ref, near_ref, taps_ref, rows):
    total = jnp.zeros((rows, product_ref.shape[1]), F32)
    here = near_ref[pl.ds(HALO, rows), :]
    for back in range(3):
        same = here == near_ref[pl.ds(HALO - back, rows), :]
        moved = jnp.where(same, product_ref[pl.ds(HALO - back, rows), :], 0.0)
        total = total + taps_ref[pl.ds(2 - back, 1), :] * moved
    return total


def conv_forward_kernel(
    core_ref, own_ref, other_ref, window_ref, gain_ref, near_ref, taps_ref,
    projected_ref, normed_ref, convolved_ref, out_ref, weights_ref, product_ref, sems,
):
    rows, channels = convolved_ref.shape
    copies = fetch_conv(core_ref, own_ref, other_ref, weights_ref, sems)
    value = window_ref[...].astype(F32)
    scale = lax.rsqrt(jnp.mean(value * value, axis=1, keepdims=True) + EPS)
    normed = (value * scale * gain_ref[pl.ds(0, 1), :]).astype(BF)
    normed_ref[...] = normed[HALO : HALO + rows]
    for copy in copies:
        copy.wait()
    weights = weights_ref[...].reshape(-1, weights_ref.shape[-1])
    projected_ref[...] = dot(normed, weights[:, : 3 * channels])
    product_ref[...] = (
        projected_ref[:, pl.ds(0, channels)] * projected_ref[:, pl.ds(2 * channels, channels)]
    )
    out_gate = projected_ref[pl.ds(HALO, rows), pl.ds(channels, channels)]
    convolved_ref[...] = (out_gate * conv_total(product_ref, near_ref, taps_ref, rows)).astype(BF)
    out_ref[...] = dot_cols(convolved_ref[...], weights[:, 3 * channels :]).astype(BF)


def conv_backward_kernel(
    core_ref, own_ref, other_ref, window_ref, near_ref, taps_ref, projected_ref, hidden_ref, next_ref,
    grad_ref, out_ref, sums_ref, gain_ref, weights_ref, product_ref, total_ref, sems,
):
    rows, channels = hidden_ref.shape[0], taps_ref.shape[1]
    copies = fetch_conv(core_ref, own_ref, other_ref, weights_ref, sems)
    product_ref[...] = (
        projected_ref[:, pl.ds(0, channels)] * projected_ref[:, pl.ds(2 * channels, channels)]
    )
    for copy in copies:
        copy.wait()
    weights = weights_ref[...].reshape(-1, weights_ref.shape[-1])
    conv_out_t = weights[:, 3 * channels :]
    gates = pl.ds(channels, channels)
    grad_convolved = dot(hidden_ref[...], conv_out_t)
    total_ref[pl.ds(0, rows), :] = grad_convolved * projected_ref[pl.ds(HALO, rows), gates]
    total_ref[pl.ds(rows, HALO), :] = (
        dot(next_ref[...], conv_out_t) * projected_ref[pl.ds(HALO + rows, HALO), gates]
    )
    grad_gate = grad_convolved * conv_total(product_ref, near_ref, taps_ref, rows)
    grad_ref[:, gates] = grad_gate.astype(BF)
    here = near_ref[pl.ds(HALO, rows), :]
    own_total = total_ref[pl.ds(0, rows), :]
    grad_product = jnp.zeros((rows, channels), F32)
    sums_ref[...] = jnp.zeros_like(sums_ref)
    for back in range(3):
        same = here == near_ref[pl.ds(HALO + back, rows), :]
        moved = jnp.where(same, total_ref[pl.ds(back, rows), :], 0.0)
        grad_product = grad_product + taps_ref[pl.ds(2 - back, 1), :] * moved
        same = here == near_ref[pl.ds(HALO - back, rows), :]
        moved = jnp.where(same, own_total * product_ref[pl.ds(HALO - back, rows), :], 0.0)
        sums_ref[pl.ds(2 - back, 1), :] = jnp.sum(moved, axis=0, keepdims=True)
    signal = projected_ref[pl.ds(HALO, rows), pl.ds(2 * channels, channels)]
    in_gate = projected_ref[pl.ds(HALO, rows), pl.ds(0, channels)]
    grad_ref[:, pl.ds(0, channels)] = (grad_product * signal).astype(BF)
    grad_ref[:, pl.ds(2 * channels, channels)] = (grad_product * in_gate).astype(BF)
    out = dot_cols(grad_ref[...], weights[:, : 3 * channels])
    out_ref[...] = out.astype(BF)
    value = window_ref[pl.ds(HALO, rows), :].astype(F32)
    scale = lax.rsqrt(jnp.mean(value * value, axis=1, keepdims=True) + EPS)
    gain_ref[...] = jnp.zeros_like(gain_ref)
    gain_ref[pl.ds(0, 1), :] = jnp.sum(out * value * scale, axis=0, keepdims=True)


def conv_weights_kernel(
    core_ref, normed_ref, hidden_ref, grad_ref, convolved_ref, keep_ref, send_ref, in_t_ref, out_t_ref
):
    core = core_ref[0]
    half, wide = keep_ref.shape[0], grad_ref.shape[1]
    in_t_ref[...] = normed_ref[...].astype(F32).T.astype(BF)
    out_t_ref[...] = hidden_ref[...].astype(F32).T.astype(BF)
    for part, ref in ((1 - core, send_ref), (core, keep_ref)):
        at = pl.ds(pl.multiple_of(part * half, half), half)
        ref[:, pl.ds(0, wide)] = dot(in_t_ref[at, :], grad_ref[...]).astype(BF)
        ref[:, pl.ds(wide, convolved_ref.shape[1])] = dot(
            out_t_ref[at, :], convolved_ref[...]
        ).astype(BF)


def local(kernel, in_specs, outs, scratch, flops, vmem, *operands, needs=()):
    kernel = not_before(kernel, len(operands), len(needs))
    moved = sum(x.size * x.dtype.itemsize for x in (*operands, *outs))
    return pl.pallas_call(
        kernel,
        in_specs=in_specs + [ANY_SPEC] * len(needs),
        out_specs=tuple(VMEM_SPEC for _ in outs),
        out_shape=tuple(outs),
        scratch_shapes=scratch,
        compiler_params=pltpu.CompilerParams(vmem_limit_bytes=vmem * 2**20),
        cost_estimate=pl.CostEstimate(flops=flops, bytes_accessed=moved, transcendentals=0),
    )(*operands, *needs)


def conv_scratch(width, channels, rows, sums):
    return [
        pltpu.VMEM((2, width // (2 * HALF), HALF, width), BF),
        pltpu.VMEM((rows + 2 * HALO, channels), F32),
        *[pltpu.VMEM((rows + HALO, channels), F32)] * sums,
        pltpu.SemaphoreType.DMA((2,)),
    ]


def shape_of(*shape, kind=BF):
    return jax.ShapeDtypeStruct(shape, kind)


def conv_forward(core, own, other, window, gain, near, taps):
    rows, width, channels = window.shape[0] - 2 * HALO, window.shape[1], taps.shape[1]
    return local(
        conv_forward_kernel,
        [SMEM_SPEC, HBM_SPEC, HBM_SPEC] + [VMEM_SPEC] * 4,
        [
            shape_of(rows + 2 * HALO, 3 * channels, kind=F32),
            shape_of(rows, width),
            shape_of(rows, channels),
            shape_of(rows, width),
        ],
        conv_scratch(width, channels, rows, 0),
        8 * rows * width * channels, 28,
        core, own, other, window, gain, near, taps,
    )


def conv_backward(core, own, other, window, near, taps, projected, hidden, following, needs):
    rows, width, channels = hidden.shape[0], hidden.shape[1], taps.shape[1]
    return local(
        conv_backward_kernel,
        [SMEM_SPEC, HBM_SPEC, HBM_SPEC] + [VMEM_SPEC] * 6,
        [
            shape_of(rows, 3 * channels),
            shape_of(rows, width),
            shape_of(8, channels, kind=F32),
            shape_of(8, width, kind=F32),
        ],
        conv_scratch(width, channels, rows, 1),
        8 * rows * width * channels, 32,
        core, own, other, window, near, taps, projected, hidden, following, needs=needs,
    )


def conv_weights(core, normed, hidden, grad, convolved, needs):
    rows, width = hidden.shape
    out = shape_of(width // 2, width)
    return local(
        conv_weights_kernel,
        [SMEM_SPEC] + [VMEM_SPEC] * 4,
        [out, out],
        [pltpu.VMEM((width, rows), BF)] * 2,
        2**20, 24,
        core, normed, hidden, grad, convolved, needs=needs,
    )


def sum_of(parts_ref, rows):
    total = parts_ref[0, pl.ds(0, rows), :].astype(F32)
    for k in range(1, 4):
        total = total + parts_ref[k, pl.ds(0, rows), :].astype(F32)
    return total


def spread(out_ref, value):
    for k in range(4):
        out_ref[k] = value


def back_kernel(parts_ref, base_ref, value_ref, gain_ref, grad_ref, out_ref, sums_ref):
    rows = base_ref.shape[0]
    grad = sum_of(parts_ref, rows)
    value = value_ref[...].astype(F32)
    scale = lax.rsqrt(jnp.mean(value * value, axis=1, keepdims=True) + EPS)
    weighted = grad * gain_ref[pl.ds(0, 1), :]
    inner = jnp.mean(weighted * value, axis=1, keepdims=True)
    back = scale * weighted - value * (scale * scale * scale) * inner
    grad_ref[...] = base_ref[...].astype(F32) + back
    spread(out_ref, grad_ref[...].astype(BF))
    sums_ref[...] = jnp.zeros_like(sums_ref)
    if parts_ref.shape[1] == rows:
        sums_ref[pl.ds(0, 1), :] = jnp.sum(grad * value * scale, axis=0, keepdims=True)
    else:
        for k in range(4):
            sums_ref[...] += (
                parts_ref[k, pl.ds(rows, 8), :].astype(F32)
                + parts_ref[k, pl.ds(rows + 8, 8), :].astype(F32)
            )


def back(parts, base, value, gain, needs=()):
    rows, width = base.shape
    return local(
        back_kernel, [VMEM_SPEC] * 4,
        [
            shape_of(rows, width, kind=F32),
            shape_of(4, rows, width),
            shape_of(8, width, kind=F32),
        ],
        [], 2**20, 16, parts, base, value, gain, needs=needs,
    )


def arrange_kernel(place_ref, own_ref, first_ref, third_ref, second_ref, mine_ref, theirs_ref):
    lane = place_ref[0]
    rows, width = own_ref.shape[0], mine_ref.shape[1]
    for by, ref in ((0, own_ref), (1, first_ref), (3, third_ref), (2, second_ref)):
        at = lax.rem(lane + 4 - by, 4) * rows
        at = pl.ds(pl.multiple_of(at, rows), rows)
        mine_ref[at, :] = ref[:, pl.ds(0, width)]
        theirs_ref[at, :] = ref[:, pl.ds(width, width)]


def arrange(place, parts, needs):
    rows, width = parts[0].shape[0], parts[0].shape[1] // 2
    out = shape_of(4 * rows, width)
    return local(
        arrange_kernel, [SMEM_SPEC] + [VMEM_SPEC] * 4, [out, out],
        [], 2**20, 24, place, *parts, needs=needs,
    )


def second_kernel(
    core_ref, own_ref, other_ref, parts_ref, out_ref, done_ref, held_ref, weights_ref, sems, part_sem
):
    inner = Moved(parts_ref.at[2], held_ref, part_sem.at[0]).start()
    matrix = fetch_weights(core_ref, own_ref, other_ref, weights_ref, sems, (DOWN,))
    inner.wait()
    out_ref[...] = dot_cols(held_ref[...], matrix(DOWN)()).astype(BF)
    done_ref[...] = jnp.zeros_like(done_ref)


def feed_second(core, own, other, parts, needs):
    rows, hidden = parts.shape[1:]
    width = 2 * HALF * own.shape[0]
    return local(
        second_kernel, [SMEM_SPEC] + [HBM_SPEC] * 3,
        [shape_of(rows, width), shape_of(8, 128, kind=F32)],
        [
            pltpu.VMEM((rows, hidden), BF),
            pltpu.VMEM((3, own.shape[0], 2, HALF, hidden), BF),
            pltpu.SemaphoreType.DMA((3, 2)),
            pltpu.SemaphoreType.DMA((1,)),
        ],
        2**20, 56, core, own, other, parts, needs=needs,
    )


def last_sums_kernel(parts_ref, in_ref, out_ref, small_ref):
    rows, wide = in_ref.shape
    total = parts_ref[0].astype(F32)
    for k in range(1, parts_ref.shape[0]):
        total = total + parts_ref[k].astype(F32)
    in_ref[...] = total[:rows, :wide]
    out_ref[...] = total[:rows, wide:]
    small_ref[...] = total[rows : rows + 8] + total[rows + 8 :]


def last_sums(parts, wide, needs):
    rows, width = parts.shape[1] - 16, parts.shape[2]
    return local(
        last_sums_kernel, [VMEM_SPEC],
        [
            shape_of(rows, wide, kind=F32),
            shape_of(rows, width - wide, kind=F32),
            shape_of(8, width, kind=F32),
        ],
        [], 2**20, 16, parts, needs=needs,
    )


def per_device(
    tokens,
    cotangent,
    segment_ids,
    mixer_gain,
    ffn_gain,
    gate_master,
    up_master,
    down_master,
    conv_in,
    conv_kernel,
    conv_out,
    query_master,
    key_master,
    value_master,
    query_gain,
    key_gain,
    output_master,
):
    core = lax.axis_index("pipe")
    lane = lax.axis_index("tensor")
    at_dp = lax.axis_index("dp_0") * 4 + lax.axis_index("dp_1")
    seq_len, width = tokens.shape
    rows = seq_len // 2
    shard = rows // 4
    channels = conv_kernel.shape[1]
    head_dim = query_gain.shape[0]
    hidden_width = gate_master.shape[2]
    dp_rows = gate_master.shape[1]
    mix_rows = conv_in.shape[0]
    attn_cols = 3 * channels
    segments = segment_ids[0]

    core_at = core.astype(jnp.int32).reshape(1)
    dense_shard = jnp.stack([gate_master[0], up_master[0], down_master[0].T]).astype(BF)
    dense_shard = dense_shard.reshape(3, 2, HALF, hidden_width)
    keep = lax.dynamic_index_in_dim(dense_shard, core, 1, False).reshape(3 * HALF, hidden_width)
    send = lax.dynamic_index_in_dim(dense_shard, 1 - core, 1, False).reshape(3 * HALF, hidden_width)
    got = other_core(send)
    attn_shard = jnp.concatenate([query_master, key_master, value_master, output_master.T], axis=1)
    attn_shard = jnp.pad(attn_shard.astype(BF), ((0, 0), (0, hidden_width - attn_cols)))
    own0 = jnp.concatenate([jnp.where(core == 0, keep, got), attn_shard], axis=0)
    own0 = lax.all_gather(own0, DP, axis=0, tiled=False)
    own1 = lax.all_gather(jnp.where(core == 0, got, keep), DP, axis=0, tiled=False)

    conv_shard = jnp.concatenate(
        [conv_in.reshape(mix_rows, 3 * channels), conv_out.T], axis=1
    ).astype(BF)
    gains = jnp.concatenate([mixer_gain, ffn_gain], 1).astype(BF)
    conv_shard = jnp.concatenate(
        [conv_shard, jnp.pad(gains, ((0, 7), (0, width - 2 * dp_rows)))], axis=0
    )
    conv_half = exchange(jnp.broadcast_to(conv_shard[None], (16, *conv_shard.shape)), DP)
    conv_other = other_core(conv_half)

    def gains_of(half):
        return half[:, mix_rows, : 2 * dp_rows].reshape(16, 2, dp_rows).swapaxes(0, 1).reshape(2, width)

    gains = in_core_order(core, gains_of(conv_half), gains_of(conv_other)).astype(F32)
    gain_mix, gain_ffn = (gains[0], gains[2]), (gains[1], gains[3])

    start = core * rows
    shard_start = start + lane * shard

    def shard_of(value):
        return lax.dynamic_slice_in_dim(value, shard_start, shard, 0).astype(F32)

    own_segments = lax.dynamic_slice_in_dim(segments, start, rows, 0)
    near = jnp.concatenate(
        [jnp.full((HALO,), -1, jnp.int32), segments, jnp.full((HALO,), -2, jnp.int32)]
    )
    near = lax.dynamic_slice_in_dim(near, start, rows + 2 * HALO, 0)

    near = jnp.broadcast_to(near[:, None], (rows + 2 * HALO, channels))
    taps_in = jnp.pad(conv_kernel, ((0, 5), (0, 0)))

    padded = jnp.pad(tokens, ((HALO, HALO), (0, 0)))
    window = lax.dynamic_slice_in_dim(padded, start, rows + 2 * HALO, 0)
    gain_rows = jnp.broadcast_to(gain_mix[0][None], (8, width))
    projected, normed0, convolved, partial = conv_forward(
        core_at, conv_half, conv_other, window, gain_rows, near, taps_in
    )
    hidden0 = shard_of(tokens) + scatter_sum(partial, "tensor")
    ffn_in0, scale_ffn0 = rms_forward(hidden0, gain_ffn[0])
    ffn_in0 = ffn_in0.astype(BF)
    own0 = after(own0, hidden0)
    other0 = other_core(own0)
    ffn_in0 = gather(ffn_in0, "tensor")
    acts0, partial = feed_forward(core_at, ffn_in0, own0, other0)
    attn_whole = in_core_order(
        core,
        own0[:, 3 * HALF :, :attn_cols].reshape(width // 2, attn_cols),
        other0[:, 3 * HALF :, :attn_cols].reshape(width // 2, attn_cols),
    )
    qkv_w, output_t = attn_whole[:, : 2 * channels], attn_whole[:, 2 * channels :]
    passed_shard = (hidden0 + scatter_sum(partial, "tensor")).astype(BF)
    passed = gather(passed_shard, "tensor")

    cosine, sine = rotation(positions_of(segments), head_dim)
    cosine = lax.dynamic_slice_in_dim(cosine, start, rows, 0)
    sine = lax.dynamic_slice_in_dim(sine, start, rows, 0)
    head_gains = jnp.stack([jnp.tile(query_gain, 2), jnp.tile(key_gain, 2)])
    head_gains = jnp.pad(head_gains, ((0, 6), (0, 0)))
    before = jnp.where(core == 0, -1, segments[:rows])
    key_column = jnp.broadcast_to(
        jnp.concatenate([before, own_segments])[:, None], (2 * rows, 128)
    )
    query_row = jnp.broadcast_to(own_segments[None, :], (8, rows))

    normed1, scale_mix1 = rms_forward(passed.astype(F32), gain_mix[1])
    normed1 = normed1.astype(BF)
    raw = dot(normed1, qkv_w)
    (low,) = whole(
        rope_forward_kernel,
        [jax.ShapeDtypeStruct((rows, 512), BF)],
        raw,
        cosine,
        sine,
        head_gains,
        vmem=16,
    )
    before_kv = lax.ppermute(low[:, 256:], "pipe", [(0, 1)])
    attended, logs = whole(
        attend_forward_kernel,
        [jax.ShapeDtypeStruct((rows, 256), BF), jax.ShapeDtypeStruct((8, rows), F32)],
        low,
        before_kv,
        key_column,
        query_row,
        scratch=[pltpu.VMEM((2 * rows, 256), BF)],
        flops=4 * 4 * rows * SPAN * 64,
        vmem=32,
    )
    partial = dot_cols(attended, output_t).astype(BF)
    hidden1 = passed_shard.astype(F32) + scatter_sum(partial, "tensor")
    ffn_in1, scale_ffn1 = rms_forward(hidden1, gain_ffn[1])
    ffn_in1 = ffn_in1.astype(BF)
    own1 = after(own1, hidden1)
    other1 = other_core(own1)
    ffn_in1 = gather(ffn_in1, "tensor")
    grad_low = lax.dynamic_slice_in_dim(cotangent, start, rows, 0)
    parts1, partial = feed_both(core_at, ffn_in1, grad_low, own1, other1)
    def gain_sum(value, scale, grad):
        return jnp.sum(grad * value * scale, axis=0)

    sum1, done = feed_weights(ffn_in1, grad_low, parts1)
    second, done = feed_second(core_at, own1, other1, parts1, (done,))
    gain_rows = jnp.broadcast_to(gain_ffn[1][None], (8, width))
    grad_hidden, copies, ffn_gain1 = back(
        blocks_of(partial), shard_of(cotangent), hidden1, gain_rows, (done,)
    )
    ffn_gain1 = ffn_gain1[0]
    sum1 = after(sum1.reshape(-1, hidden_width), grad_hidden)
    sum1 = lax.psum_scatter(sum1, DP, scatter_dimension=0, tiled=True)
    hidden_low = gathered(copies)
    grad_output_t = dot_rows(hidden_low, attended).astype(BF)
    grad_attended = dot(hidden_low, output_t).astype(BF)
    grad_query, grad_kv = whole(
        attend_backward_kernel,
        [jax.ShapeDtypeStruct((rows, 256), F32), jax.ShapeDtypeStruct((2 * rows, 256), F32)],
        low,
        before_kv,
        key_column,
        query_row,
        logs,
        grad_attended,
        scratch=[pltpu.VMEM((2 * rows, 256), BF)],
        flops=10 * 4 * rows * SPAN * 64,
        vmem=40,
    )
    more_kv = lax.ppermute(grad_kv[:rows], "pipe", [(1, 0)])
    grad_qkv, head_sums = whole(
        rope_backward_kernel,
        [jax.ShapeDtypeStruct((rows, 512), BF), jax.ShapeDtypeStruct((8, 128), F32)],
        raw,
        grad_query,
        grad_kv[rows:],
        more_kv,
        cosine,
        sine,
        head_gains,
        vmem=20,
    )
    partial = dot_cols(grad_qkv, qkv_w)
    grad_attn = jnp.concatenate([dot_rows(normed1, grad_qkv).astype(BF), grad_output_t], axis=1)
    gain_rows = jnp.broadcast_to(gain_mix[1][None], (8, width))
    grad_hidden, copies, mix_gain1 = back(
        blocks_of(partial.astype(BF)), grad_hidden, passed_shard, gain_rows, (grad_attn,)
    )
    mix_gain1 = mix_gain1[0]
    grad_shard = copies[0]
    grad_low = gathered(copies)
    grad_passed = grad_low

    parts0, partial = feed_backward(
        core_at, grad_low, own0, other0, acts0
    )
    early = other_core(jnp.where(core == 0, grad_passed, passed))

    sum0, done = feed_weights(ffn_in0, grad_low, parts0, (grad_attn,), (sum1,))
    gain_rows = jnp.broadcast_to(gain_ffn[0][None], (8, width))
    grad_hidden, copies, ffn_gain0 = back(
        blocks_of(partial), grad_shard, hidden0, gain_rows, (done,)
    )
    ffn_gain0 = ffn_gain0[0]
    hidden_low = gathered(copies)

    sum0 = after(sum0.reshape(-1, hidden_width), grad_hidden)
    sum0 = lax.psum_scatter(sum0, DP, scatter_dimension=0, tiled=True)
    dense0 = sum0[: 3 * dp_rows]
    theirs = other_core(jnp.where(core == 0, sum1, dense0)).astype(F32)
    dense = jnp.where(core == 0, dense0, sum1).astype(F32) + theirs
    grad_gate, grad_up, grad_down = (dense[k * dp_rows : (k + 1) * dp_rows] for k in range(3))
    attn_both = sum0[3 * dp_rows :, :attn_cols]
    grad_attn = half_of(attn_both, core).astype(F32) + other_core(half_of(attn_both, 1 - core))

    following = lax.ppermute(hidden_low[:HALO], "pipe", [(1, 0)])
    grad_projected, partial, taps, mix_gain0 = conv_backward(
        core_at, conv_half, conv_other, window, near, taps_in, projected, hidden_low, following,
        needs=(),
    )
    taps, mix_gain0 = taps[:3], mix_gain0[0]

    taps_wide = lax.dynamic_update_slice_in_dim(
        jnp.zeros((3, width), F32), taps, lane * channels, 1
    )
    heads = (head_sums[:2, :64] + head_sums[:2, 64:]).reshape(1, 128)
    small = jnp.concatenate(
        [
            jnp.stack([mix_gain0, ffn_gain0, mix_gain1, ffn_gain1]),
            taps_wide,
            jnp.pad(heads, ((0, 0), (0, width - 128))),
        ],
        0,
    )

    def two_terms(value):
        high = value.astype(BF)
        return jnp.concatenate([high, (value - high.astype(F32)).astype(BF)], 0)

    def one_term(value):
        return value[:8] + value[8:]

    def sum_beside(blocks, small, axis):
        terms = jnp.broadcast_to(two_terms(small)[None], (blocks.shape[0], 16, width))
        parts = exchange(jnp.concatenate([blocks.astype(BF), terms], 1), axis)
        summed = jnp.sum(parts.astype(F32), axis=0)
        return summed[:-16], one_term(summed[-16:])

    terms = jnp.broadcast_to(two_terms(small)[None], (4, 16, width))
    parts = [x.reshape(4, shard, width) for x in (partial, second)]
    parts = exchange(jnp.concatenate([*parts, terms], 1), "tensor")
    parts = jnp.sum(parts.astype(F32), axis=0)
    grad_normed = parts[:shard]
    second = (hidden1 + parts[shard : 2 * shard]).astype(BF)
    small = one_term(parts[2 * shard :])
    tokens_shard = shard_of(tokens)
    scale_shard = rms_forward(tokens_shard, gain_mix[0])[1]
    grad_tokens = grad_hidden + rms_backward(tokens_shard, scale_shard, gain_mix[0], grad_normed)
    grad_tokens = grad_tokens.astype(BF)
    late = [
        jnp.where(core == 0, grad_tokens, second),
        other_core(jnp.where(core == 0, second, grad_tokens)),
    ]
    late = jnp.concatenate(late, axis=1)
    small = small + one_term(other_core(two_terms(small)).astype(F32))

    keep, send = conv_weights(
        core_at, normed0, hidden_low, grad_projected, convolved, ()
    )
    blocks = keep.astype(F32) + other_core(send)
    terms = jnp.broadcast_to(two_terms(small)[None], (16, 16, width))
    blocks = jnp.concatenate([blocks.astype(BF).reshape(16, mix_rows, width), terms], 1)
    grad_in, grad_out, small = last_sums(
        exchange(blocks, DP), 3 * channels, ()
    )

    parts = [late, *(turned(late, "tensor", by) for by in (1, 3, 2))]
    mine, theirs = arrange(lane.astype(jnp.int32).reshape(1), parts, (small,))
    section_output = jnp.where(
        core == 0, jnp.concatenate([passed, early], 0), jnp.concatenate([theirs, mine], 0)
    )
    input_grad = jnp.where(
        core == 0, jnp.concatenate([mine, theirs], 0), jnp.concatenate([early, grad_passed], 0)
    ).astype(F32)

    def own_gain(pair):
        return lax.dynamic_slice(pair, (core, at_dp * dp_rows), (1, dp_rows))

    return (
        section_output[None],
        input_grad[None],
        own_gain(small[0:4:2]),
        own_gain(small[1:4:2]),
        grad_gate[None],
        grad_up[None],
        grad_down.T[None],
        grad_in.reshape(mix_rows, 3, channels),
        small[4:7],
        grad_out.T,
        grad_attn[:, :channels],
        grad_attn[:, channels : channels + 128],
        grad_attn[:, channels + 128 : 2 * channels],
        small[7, :64],
        small[7, 64:128],
        grad_attn[:, 2 * channels :].T,
    )


def solution(mesh):
    finer = Mesh(
        mesh.devices.reshape(mesh.shape["pipe"], mesh.shape["tensor"], 4, 4),
        ("pipe", "tensor", "dp_0", "dp_1"),
    )
    return jax.shard_map(
        per_device,
        mesh=finer,
        in_specs=(
            P(DP, None),
            P(DP, None),
            P(DP, None),
            P("pipe", DP),
            P("pipe", DP),
            P("pipe", DP, "tensor"),
            P("pipe", DP, "tensor"),
            P("pipe", "tensor", DP),
            P(PIPE_DP, None, "tensor"),
            P(None, "tensor"),
            P("tensor", PIPE_DP),
            P(PIPE_DP, "tensor"),
            P(PIPE_DP, "tensor"),
            P(PIPE_DP, "tensor"),
            P(),
            P(),
            P("tensor", PIPE_DP),
        ),
        out_specs=(
            P("pipe", DP, None),
            P("pipe", DP, None),
            P("pipe", DP),
            P("pipe", DP),
            P("pipe", DP, "tensor"),
            P("pipe", DP, "tensor"),
            P("pipe", "tensor", DP),
            P(PIPE_DP, None, "tensor"),
            P(),
            P("tensor", PIPE_DP),
            P(PIPE_DP, "tensor"),
            P(PIPE_DP, "tensor"),
            P(PIPE_DP, "tensor"),
            P(),
            P(),
            P("tensor", PIPE_DP),
        ),
        check_vma=False,
    )
```
